256 devices in a mesh: lon: 32 (over z, y_hi, core), lat: 8 (over y_lo, x).
Axes of the slice: x: 4, y: 4 (y_hi: 2, y_lo: 2; y = y_hi * 2 + y_lo), z: 8, core: 2. Of those that a mesh axis runs over, the one named last changes fastest.
Arguments:
- hidden_in: bfloat16 [128, 2048, 384], P('lat', 'lon'), may hold values from -6 to 6
- cotangent: bfloat16 [128, 2048, 384], P('lat', 'lon'), may hold values from -6 to 6
- weight_fine: bfloat16 [3, 3, 384, 384], replicated, may hold values from -0.109375 to 0.109375
- weight_mid: bfloat16 [3, 3, 384, 384], replicated, may hold values from -0.109375 to 0.109375
- weight_coarse: bfloat16 [3, 3, 384, 384], replicated, may hold values from -0.109375 to 0.109375
Outputs:
- output: bfloat16 [128, 2048, 384], P('lat', 'lon')
- grad_in: bfloat16 [128, 2048, 384], P('lat', 'lon')
The draws below stay inside these ranges and needn't reach their ends.
All inputs are finite; a program needn't handle non-finite values.
Results may differ from the reference program's by a relative error of at most 0.012.
Values may be sent and summed in bfloat16 or wider, within the bound.
A program may use at most 64 MiB of HBM per device.

```python
import math
import jax
import jax.numpy as jnp
from jax import lax

H = 384
NLAT = 128
NLON = 2048


def level_of(rng, extent, shards, least, top_value):
    gain, own = 1.0, jax.random.fold_in(rng, 6)
    for axis_at, blocks in shards:
        heights = jnp.exp(jax.random.uniform(jax.random.fold_in(own, axis_at), (blocks,), jnp.float32, least / len(shards), top_value / len(shards)))
        gain = gain * jnp.repeat(heights, extent[axis_at] // blocks).reshape([-1 if axis == axis_at else 1 for axis in range(len(extent))])
    return gain


def scatter_about(rng, extent, scale, reach, shards=(), kind=jnp.bfloat16):
    level = level_of(rng, extent, shards, -0.22, 0.18) if shards else 1.0
    array = jax.random.normal(rng, extent, jnp.float32) * scale * level
    return jnp.minimum(jnp.maximum(array, -reach), reach).astype(kind)


def setup_inputs(seed: int = 0) -> dict:
    keys = jax.random.split(jax.random.key(seed), 6)
    return {
        "hidden_in": scatter_about(keys[0], (NLAT, NLON, H), 1.0, 6.0, ((0, 8), (1, 32))),
        "cotangent": scatter_about(keys[1], (NLAT, NLON, H), 1.0, 6.0, ((0, 8), (1, 32))),
        "weight_fine": scatter_about(keys[2], (3, 3, H, H), (9 * H) ** -0.5, 0.109375),
        "weight_mid": scatter_about(keys[3], (3, 3, H, H), (9 * H) ** -0.5, 0.109375),
        "weight_coarse": scatter_about(keys[4], (3, 3, H, H), (9 * H) ** -0.5, 0.109375),
    }


def extend_global(field):
    half_loop = field.shape[1] // 2
    north = jnp.roll(field[0], -half_loop, axis=0)
    south = jnp.roll(field[-1], -half_loop, axis=0)
    with_rows = jnp.concatenate([north[None], field, south[None]], axis=0)
    return jnp.concatenate([with_rows[:, -1:], with_rows, with_rows[:, :1]], axis=1)

def convolve(field, weight):
    rows_here = field.shape[0]
    cols_here = field.shape[1]
    extended = extend_global(field)
    total = jnp.zeros((rows_here, cols_here, weight.shape[3]), jnp.float32)
    for row_tap in range(3):
        for col_tap in range(3):
            window = extended[row_tap:row_tap + rows_here, col_tap:col_tap + cols_here]
            total = total + jnp.einsum('rch,hk->rck', window, weight[row_tap, col_tap])
    return total

def convolve_adjoint(grad, weight):
    weight_wide = weight.astype(jnp.float32)
    start = jnp.zeros(grad.shape, jnp.float32)
    _, pull = jax.vjp(lambda v: convolve(v, weight_wide), start)
    return pull(grad.astype(jnp.float32))[0]

def gelu_slope(pre):
    return 0.5 * (1.0 + lax.erf(pre * (1.0 / math.sqrt(2.0)))) + pre * jnp.exp(-0.5 * pre * pre) / math.sqrt(2.0 * math.pi)

def pool_sum(field):
    rows_here, cols_here, channels = field.shape
    return field.astype(jnp.float32).reshape(rows_here // 2, 2, cols_here // 2, 2, channels).sum(axis=(1, 3))

def upsample(field):
    return jnp.repeat(jnp.repeat(field, 2, axis=0), 2, axis=1)

def level_forward(field, weight):
    pre = convolve(field.astype(jnp.float32), weight.astype(jnp.float32))
    return (pre, jax.nn.gelu(pre, approximate=False).astype(jnp.bfloat16))

def reference(hidden_in, cotangent, weight_fine, weight_mid, weight_coarse):
    pre_fine, act_fine = level_forward(hidden_in, weight_fine)
    pool_fine = (0.25 * pool_sum(act_fine)).astype(jnp.bfloat16)
    pre_mid, act_mid = level_forward(pool_fine, weight_mid)
    pool_mid = (0.25 * pool_sum(act_mid)).astype(jnp.bfloat16)
    pre_coarse, act_coarse = level_forward(pool_mid, weight_coarse)
    inner = act_mid.astype(jnp.float32) + upsample(act_coarse.astype(jnp.float32))
    output = (act_fine.astype(jnp.float32) + upsample(inner)).astype(jnp.bfloat16)
    grad_top = cotangent.astype(jnp.float32)
    grad_mid_act = pool_sum(grad_top)
    grad_coarse_act = pool_sum(grad_mid_act)
    grad_coarse = (grad_coarse_act * gelu_slope(pre_coarse)).astype(jnp.bfloat16)
    back_mid = convolve_adjoint(grad_coarse, weight_coarse)
    grad_mid = ((grad_mid_act + 0.25 * upsample(back_mid)) * gelu_slope(pre_mid)).astype(jnp.bfloat16)
    back_fine = convolve_adjoint(grad_mid, weight_mid)
    grad_fine = ((grad_top + 0.25 * upsample(back_fine)) * gelu_slope(pre_fine)).astype(jnp.bfloat16)
    grad_in = convolve_adjoint(grad_fine, weight_fine).astype(jnp.bfloat16)
    return (output, grad_in)
```

```python
import functools

import jax
import jax.numpy as jnp
from jax import lax
from jax.experimental import pallas as pl
from jax.experimental.pallas import tpu as pltpu
from jax.sharding import PartitionSpec as P

MESH = pl.DeviceIdType.MESH
F32 = jnp.float32
BF16 = jnp.bfloat16
C = 384
LANES = 3


def get(ref, start, n, stride=1):
    ds = pl.ds(start, n) if stride == 1 else pl.ds(start, n, stride=stride)
    return jnp.concatenate([ref[l, ds, :] for l in range(LANES)], axis=-1)


def put(ref, start, val, stride=1):
    n = val.shape[0]
    ds = pl.ds(start, n) if stride == 1 else pl.ds(start, n, stride=stride)
    for l in range(LANES):
        ref[l, ds, :] = val[:, l * 128 : (l + 1) * 128]


class Rows:
    def __init__(self, ref, pitch):
        self.ref, self.pitch = ref, pitch


def at_row(grid, r, start):
    if isinstance(r, int):
        return r * grid.pitch + start
    if start % 8 == 0 and grid.pitch % 8 == 0:
        return pl.multiple_of(r * grid.pitch + start, 8)
    return r * grid.pitch + start


def row_get(grid, r, start, n, stride=1):
    return get(grid.ref, at_row(grid, r, start), n, stride)


def row_put(grid, r, start, val, stride=1):
    put(grid.ref, at_row(grid, r, start), val, stride)


def col_get(grid, c, r0, n):
    return get(grid.ref, r0 * grid.pitch + c, n, grid.pitch)


def col_put(grid, c, r0, val):
    put(grid.ref, r0 * grid.pitch + c, val, grid.pitch)


def gelu_pair(z):
    e = jnp.exp(-0.5 * z * z)
    t = 1.0 / (1.0 + (0.3275911 * 0.7071067811865476) * jnp.abs(z))
    q = t * (
        0.127414796
        + t * (-0.142248368 + t * (0.7107068705 + t * (-0.7265760135 + t * 0.5307027145)))
    )
    h = q * e
    cdf = jnp.where(z >= 0, 1.0 - h, h)
    return z * cdf, cdf + z * (e * 0.3989422804014327)


def rounded(x):
    return x.astype(BF16).astype(F32)


def conv_dot(parts, weight):
    lhs = jnp.concatenate([parts(a, b) for a in range(3) for b in range(3)], axis=-1)
    return jnp.dot(lhs, weight[...].reshape(9 * C, C), preferred_element_type=F32)


def conv_dot_t(parts, weight):
    lhs = jnp.concatenate([parts(a, b) for a in range(3) for b in range(3)], axis=-1)
    rhs = jnp.concatenate([weight[a, b] for a in range(3) for b in range(3)], axis=-1)
    return lax.dot_general(lhs, rhs, (((1,), (1,)), ((), ())), preferred_element_type=F32)


def kernel(
    nlat, nlon,
    hid_hbm, cot_hbm, wf_hbm, wm_hbm, wc_hbm, out_hbm, grad_hbm,
    hid, cot, wf, wm, wc, out_v, grad_v,
    s_ext, e_ext, l_edge, pre, pre_e, act, slp, act_e, slp_e,
    sx, ctp, cte, gma, gmae, gcax,
    pf, sm0, sm1, pre_m, am, slm, sle, slb, pml, sc, cb, ac, gs, gb, bm,
    mg, ms0, ms1, mc, ml, bfm, bfe, g_ext, fs0, fs3, ge, ns, tile, ts,
    c_buf, k_buf, r_slot, c_slot, k_slot,
    lr_buf, lc_buf, lr_slot, lc_slot,
    pc_buf, pr_slot, sr_slot, pc_slot,
    lsem, ssem, rsem,
):
    s_ext = Rows(s_ext, 80)
    act = Rows(act, 64)
    slp = Rows(slp, 64)
    act_e = Rows(act_e, 40)
    slp_e = Rows(slp_e, 32)
    sx = Rows(sx, 64)
    cte = Rows(cte, 32)
    gma = Rows(gma, 32)
    gmae = Rows(gmae, 16)
    gcax = Rows(gcax, 32)
    sm0 = Rows(sm0, 32)
    sm1 = Rows(sm1, 32)
    slm = Rows(slm, 32)
    sle = Rows(sle, 16)
    sc = Rows(sc, 48)
    gs = Rows(gs, 48)
    bm = Rows(bm, 32)
    ms0 = Rows(ms0, 32)
    ms1 = Rows(ms1, 32)
    mc = Rows(mc, 24)
    bfe = Rows(bfe, 16)
    fs0 = Rows(fs0, 32)
    fs3 = Rows(fs3, 32)
    ge = Rows(ge, 32)
    ns = Rows(ns, 64)
    lat = lax.axis_index("lat")
    lon = lax.axis_index("lon")
    north = lat == 0
    south = lat == nlat - 1
    sgn_n = jnp.where(north, -1, 1)
    sgn_s = jnp.where(south, -1, 1)

    def device(dlat, dlon):
        to_lat, to_lon = lat, lon + dlon + nlon
        if dlat:
            pole = north if dlat < 0 else south
            to_lat = jnp.where(pole, lat, lat + dlat)
            to_lon = to_lon + jnp.where(pole, nlon // 2, 0)
        return {"lat": to_lat, "lon": lax.rem(to_lon, nlon)}

    there = [device(*d) for d in ((-1, 0), (1, 0), (0, -1), (0, 1), (-1, -1), (-1, 1), (1, -1), (1, 1))]
    slot = [
        jnp.where(north, 0, 1), jnp.where(south, 1, 0), 3, 2,
        jnp.where(north, 5, 7), jnp.where(north, 4, 6),
        jnp.where(south, 7, 5), jnp.where(south, 6, 4),
    ]

    def remote(kind, d, src, dst, where):
        return pltpu.make_async_remote_copy(
            src_ref=src, dst_ref=dst, send_sem=ssem.at[kind, d], recv_sem=rsem.at[kind, where],
            device_id=there[d], device_id_type=MESH,
        )

    def load(i, src, dst):
        copy = pltpu.make_async_copy(src, dst, lsem.at[i])
        copy.start()
        return copy

    barrier = pltpu.get_barrier_semaphore()
    for t in there:
        pl.semaphore_signal(barrier, inc=1, device_id=t, device_id_type=MESH)

    hid_in = load(0, hid_hbm, hid)
    wf_in = load(1, wf_hbm, wf)
    cot_in = load(2, cot_hbm, cot)
    wm_in = load(3, wm_hbm, wm)
    wc_in = load(4, wc_hbm, wc)
    hid_in.wait()

    @pl.loop(0, 16)
    def _(r):
        row_put(s_ext, r + 3, 8, hid[r].astype(F32))

    for side, first in ((0, 0), (1, 61)):
        for c in range(3):
            c_buf[side, pl.ds(c * 16, 16)] = col_get(s_ext, 8 + first + c, 3, 16).astype(BF16)
    for k, (row, first) in enumerate(((0, 0), (0, 61), (12, 0), (12, 61))):
        for c in range(3):
            put(tile, c * 4, col_get(s_ext, 8 + first + c, 3 + row, 8)[:4])
        k_buf[k] = get(tile, 0, 16).astype(BF16)

    pl.semaphore_wait(barrier, 8)

    sends = []

    def send(kind, d, src, slots, base):
        copy = remote(kind, d, src, slots.at[slot[d] - base], slot[d])
        copy.start()
        sends.append(copy)

    def recv(kind, where, src, dst):
        remote(kind, where, src, dst, where).wait_recv()

    send(0, 0, hid.at[pl.ds(0, 3)], r_slot, 0)
    send(0, 1, hid.at[pl.ds(13, 3)], r_slot, 0)
    for d in (4, 5, 6, 7):
        send(0, d, k_buf.at[d - 4], k_slot, 4)
    for d in (2, 3):
        send(0, d, c_buf.at[d - 2], c_slot, 2)

    @pl.loop(0, 16)
    def _(r):
        for ph in range(6):
            e_ext[r + 3, ph] = row_get(s_ext, r + 3, 7 + ph, 16, 4).astype(BF16)

    wf_in.wait()
    pre[pl.ds(3, 14)] = conv_dot(
        lambda a, b: e_ext[3 + a : 17 + a, b : b + 4].reshape(14 * 64, C), wf
    ).reshape(14, 64, C)

    def fine_gelu(i):
        a, s = gelu_pair(pre[i])
        row_put(act, i, 0, rounded(a))
        row_put(slp, i, 0, s)

    @pl.loop(3, 17)
    def _(i):
        fine_gelu(i)

    cot_in.wait()

    @pl.loop(0, 16)
    def _(r):
        row_put(sx, r, 0, cot[r].astype(F32))
        for p in range(4):
            ctp[r + 1, pl.ds(p * 16, 16)] = row_get(sx, r, p, 16, 4).astype(BF16)

    @pl.loop(0, 8)
    def _(m):
        for p in range(2):
            total = 0.0
            for dr in range(2):
                for dp in range(2):
                    total = total + ctp[2 * m + dr + 1, pl.ds((2 * p + dp) * 16, 16)].astype(F32)
            row_put(gma, m + 2, p * 16, total)

    for q in range(4):
        total = 0.0
        for dr in range(2):
            for p in range(2):
                total = total + row_get(gma, 2 * q + dr + 2, p * 16, 16)
        row_put(gcax, q + 2, 8, total)

    for side, (row, mid, coarse) in enumerate(((0, 0, 0), (15, 6, 2))):
        lr_buf[side, pl.ds(0, 64)] = ctp[row + 1]
        for k in range(2):
            lr_buf[side, pl.ds(64 + 32 * k, 32)] = row_get(gma, mid + k + 2, 0, 32).astype(BF16)
            lr_buf[side, pl.ds(128 + 16 * k, 16)] = row_get(gcax, coarse + k + 2, 8, 16).astype(BF16)
    for side, (col, mids, coarse) in enumerate(((0, (0, 16), 0), (63, (15, 31), 14))):
        put(tile, 0, col_get(sx, col, 0, 16))
        for c in range(2):
            put(tile, 16 + 8 * c, col_get(gma, mids[c], 2, 8))
            put(tile, 32 + 4 * c, col_get(gcax, 8 + coarse + c, 2, 8)[:4])
        lc_buf[side] = get(tile, 0, 48).astype(BF16)
    for d in (0, 1):
        send(1, d, lr_buf.at[d], lr_slot, 0)
    for d in range(2, 8):
        send(1, d, lc_buf.at[d % 2], lc_slot, 2)

    for k in range(2):
        recv(0, k, hid.at[pl.ds(0, 3)], r_slot.at[k])
    for k in range(4):
        recv(0, 4 + k, k_buf.at[k], k_slot.at[k])
    for k in range(2):
        recv(0, 2 + k, c_buf.at[k], c_slot.at[k])

    for j in range(3):
        row_put(s_ext, 2 - j, 8, r_slot[0, jnp.where(north, j, 2 - j)].astype(F32))
        row_put(s_ext, 19 + j, 8, r_slot[1, jnp.where(south, 2 - j, j)].astype(F32))
    for side, first in ((0, -3), (1, 64)):
        for c in range(3):
            col_put(s_ext, 8 + first + c, 3, c_slot[side, pl.ds(c * 16, 16)].astype(F32))
    for k in range(4):
        put(tile, 0, k_slot[k].astype(F32))
        first = 64 if k % 2 else -3
        for c in range(3):
            for j in range(3):
                if k < 2:
                    at, row = jnp.where(north, j, 3 - j), 2 - j
                else:
                    at, row = jnp.where(south, 3 - j, j), 19 + j
                row_put(s_ext, row, 8 + first + c, get(tile, c * 4 + at, 1))

    @pl.loop(0, 6)
    def _(i):
        r = i + jnp.where(i >= 3, 16, 0)
        for ph in range(6):
            e_ext[r, ph] = row_get(s_ext, r, 7 + ph, 16, 4).astype(BF16)

    for r in (3, 4, 17, 18):
        for ph in (0, 5):
            e_ext[r, ph] = row_get(s_ext, r, 7 + ph, 16, 4).astype(BF16)

    edge_rows = lax.broadcasted_iota(jnp.int32, (32, 1), 0)
    flip = (north & (edge_rows < 2)) | (south & ((edge_rows == 18) | (edge_rows == 19)))

    @pl.loop(0, 10)
    def _(i):
        side = i // 5
        col = 8 - 3 + i + side * 60
        low, mid, high = (get(s_ext.ref, a * 80 + col, 32, 80) for a in range(3))
        l_edge[0, i] = jnp.where(flip, high, low).astype(BF16)
        l_edge[1, i] = mid.astype(BF16)
        l_edge[2, i] = jnp.where(flip, low, high).astype(BF16)

    def ring(a, b):
        rows = [1 + sgn_n * (a - 1), 2 + sgn_n * (a - 1), 2 + a, 17 + a, 19 + sgn_s * (a - 1), 20 + sgn_s * (a - 1)]
        parts = [e_ext[r, b : b + 4].reshape(64, C) for r in rows]
        parts += [l_edge[a, s * 5 + b : s * 5 + b + 3].reshape(96, C) for s in range(2)]
        return jnp.concatenate(parts, axis=0)

    res = conv_dot(ring, wf)
    for k, i in enumerate((0, 1, 2, 17, 18, 19)):
        pre[i] = res[k * 64 : (k + 1) * 64]
    pre_e[...] = res[384:].reshape(6, 32, C)

    @pl.loop(0, 6)
    def _(i):
        fine_gelu(i + jnp.where(i >= 3, 14, 0))
        a, s = gelu_pair(pre_e[i])
        row_put(act_e, i, 0, rounded(a))
        row_put(slp_e, i, 0, s)

    for dst, src in ((act, act_e), (slp, slp_e)):
        col_put(dst, 0, 0, row_get(src, 2, 0, 24))
        col_put(dst, 63, 0, row_get(src, 3, 0, 24))

    @pl.loop(0, 10)
    def _(m):
        for p, shifted in ((0, sm0), (1, sm1)):
            total = 0.0
            for dr in range(2):
                for dp in range(2):
                    total = total + row_get(act, 2 * m + dr, (2 * p + dp) * 16, 16)
            total = 0.25 * total
            pf[m, 1 + p] = total.astype(BF16)
            row_put(shifted, m, 8, total)

    for first, shifted, at in ((0, sm1, 7), (4, sm0, 24)):
        total = 0.0
        for c in range(2):
            for dr in range(2):
                total = total + row_get(act_e, first + c, dr, 16, 2)
        col_put(shifted, at, 0, 0.25 * total)

    @pl.loop(0, 10)
    def _(m):
        pf[m, 0] = row_get(sm1, m, 7, 16).astype(BF16)
        pf[m, 3] = row_get(sm0, m, 9, 16).astype(BF16)

    wm_in.wait()
    pre_m[...] = conv_dot(
        lambda a, b: pf[a : a + 8, b : b + 2].reshape(256, C), wm
    ).reshape(8, 32, C)

    @pl.loop(0, 8)
    def _(m):
        a, s = gelu_pair(pre_m[m])
        am[m] = rounded(a)
        row_put(slm, m + 2, 0, s)
        slb[m] = s.astype(BF16)

    for q in range(4):
        total = 0.0
        for dr in range(2):
            for p in range(2):
                total = total + am[2 * q + dr, pl.ds(p * 16, 16)]
        total = 0.25 * total
        pml[q] = total.astype(BF16)
        row_put(sc, q + 3, 16, total)
    for side, (first, mids) in enumerate(((0, (0, 16)), (13, (15, 31)))):
        for c in range(3):
            put(tile, c * 4, col_get(sc, 16 + first + c, 3, 8)[:4])
        for c in range(2):
            put(tile, 16 + 8 * c, col_get(slm, mids[c], 2, 8))
        pc_buf[side] = get(tile, 0, 32).astype(BF16)

    for d in (0, 1):
        send(2, d, pml.at[pl.ds(d, 3)], pr_slot, 0)
    for d in (4, 5, 6, 7, 2, 3):
        send(2, d, pc_buf.at[d % 2], pc_slot, 2)
    for d in (0, 1):
        send(3, d, slb.at[pl.ds(6 * d, 2)], sr_slot, 0)

    for k in range(2):
        recv(1, k, lr_buf.at[k], lr_slot.at[k])
    for k in range(6):
        recv(1, 2 + k, lc_buf.at[0], lc_slot.at[k])
    for k in range(6):
        put(ts, k * 48, lc_slot[k].astype(F32))
    ctp[0] = lr_slot[0, pl.ds(0, 64)]
    ctp[17] = lr_slot[1, pl.ds(0, 64)]

    def pick(k, at):
        return get(ts, k * 48 + at, 1)

    def edge_columns(dst, base):
        for side in range(2):
            for c in range(2):
                to = side * 2 + c
                row_put(dst, to, 2, get(ts, side * 48 + base + 8 * c, 8))
                for j in range(2):
                    at = base + 8 * c + jnp.where(north, j, 7 - j)
                    row_put(dst, to, 1 - j, pick(2 + side, at))
                    at = base + 8 * c + jnp.where(south, 7 - j, j)
                    row_put(dst, to, 10 + j, pick(4 + side, at))

    for j in range(2):
        at_n, at_s = jnp.where(north, j, 1 - j), jnp.where(south, 1 - j, j)
        row_put(gma, 1 - j, 0, lr_slot[0, pl.ds(pl.multiple_of(64 + 32 * at_n, 32), 32)].astype(F32))
        row_put(gma, 10 + j, 0, lr_slot[1, pl.ds(pl.multiple_of(64 + 32 * at_s, 32), 32)].astype(F32))
        row_put(gcax, 1 - j, 8, lr_slot[0, pl.ds(pl.multiple_of(128 + 16 * at_n, 16), 16)].astype(F32))
        row_put(gcax, 6 + j, 8, lr_slot[1, pl.ds(pl.multiple_of(128 + 16 * at_s, 16), 16)].astype(F32))
    for side in range(2):
        row_put(cte, side, 2, get(ts, side * 48, 16))
        row_put(cte, side, 1, pick(2 + side, jnp.where(north, 0, 15)))
        row_put(cte, side, 18, pick(4 + side, jnp.where(south, 15, 0)))
        for c in range(2):
            col = 8 + (16 if side else -2) + c
            for q in range(4):
                row_put(gcax, q + 2, col, pick(side, 32 + 4 * c + q))
            for j in range(2):
                row_put(gcax, 1 - j, col, pick(2 + side, 32 + 4 * c + jnp.where(north, j, 3 - j)))
                row_put(gcax, 6 + j, col, pick(4 + side, 32 + 4 * c + jnp.where(south, 3 - j, j)))
    edge_columns(gmae, 16)

    wc_in.wait()
    for k in range(2):
        recv(2, k, pml.at[pl.ds(0, 3)], pr_slot.at[k])
    for k in range(6):
        recv(2, 2 + k, pc_buf.at[0], pc_slot.at[k])
    for k in range(6):
        put(ts, k * 48, pc_slot[k].astype(F32))
    for j in range(3):
        row_put(sc, 2 - j, 16, pr_slot[0, jnp.where(north, j, 2 - j)].astype(F32))
        row_put(sc, 7 + j, 16, pr_slot[1, jnp.where(south, 2 - j, j)].astype(F32))
    for side in range(2):
        for c in range(3):
            col = 16 + (16 if side else -3) + c
            for q in range(4):
                row_put(sc, q + 3, col, pick(side, 4 * c + q))
            for j in range(3):
                row_put(sc, 2 - j, col, pick(2 + side, 4 * c + jnp.where(north, j, 3 - j)))
                row_put(sc, 7 + j, col, pick(4 + side, 4 * c + jnp.where(south, 3 - j, j)))

    @pl.loop(0, 10)
    def _(r):
        for b in range(3):
            cb[b, r] = row_get(sc, r, 7 + b, 32).astype(BF16)

    def coarse(a, b):
        rows = [1 + sgn_n * (a - 1), 2 + sgn_n * (a - 1)]
        tail = [7 + sgn_s * (a - 1), 8 + sgn_s * (a - 1)]
        parts = [cb[b, r] for r in rows] + [cb[b, 2 + a : 6 + a].reshape(128, C)]
        return jnp.concatenate(parts + [cb[b, r] for r in tail], axis=0)

    res = conv_dot(coarse, wc)
    for i in range(8):
        a, s = gelu_pair(res[i * 32 : (i + 1) * 32])
        if 2 <= i < 6:
            ac[i - 2] = rounded(a[8:24])
        row_put(gs, i, 8, row_get(gcax, i, 0, 32) * s)

    @pl.loop(0, 8)
    def _(r):
        for d in range(3):
            gb[d, r] = row_get(gs, r, 7 + d, 32).astype(BF16)

    for d in range(3):
        for k, (x, y) in enumerate(((0, 2), (1, 3), (4, 6), (5, 7))):
            gb[d, 8 + k] = (gb[d, x].astype(F32) + gb[d, y].astype(F32)).astype(BF16)
        gb[d, 12] = jnp.zeros((32, C), BF16)

    def coarse_t(a, b):
        d = 2 - b
        if a == 1:
            return gb[d, 1:7].reshape(192, C)
        if a == 0:
            rows = [jnp.where(north, 8, 2), jnp.where(north, 9, 3), 4, 5, jnp.where(south, 12, 6), jnp.where(south, 12, 7)]
        else:
            rows = [jnp.where(north, 12, 0), jnp.where(north, 12, 1), 2, 3, jnp.where(south, 10, 4), jnp.where(south, 11, 5)]
        return jnp.concatenate([gb[d, r] for r in rows], axis=0)

    res = conv_dot_t(coarse_t, wc)
    for i in range(6):
        row_put(bm, i, 0, 0.25 * res[i * 32 : (i + 1) * 32])

    for k in range(2):
        recv(3, k, slb.at[pl.ds(0, 2)], sr_slot.at[k])
    for j in range(2):
        row_put(slm, 1 - j, 0, sr_slot[0, jnp.where(north, j, 1 - j)].astype(F32))
        row_put(slm, 10 + j, 0, sr_slot[1, jnp.where(south, 1 - j, j)].astype(F32))
    edge_columns(sle, 16)

    @pl.loop(0, 12)
    def _(k):
        below = row_get(bm, k // 2, 8, 16)
        for p, shifted in ((0, ms0), (1, ms1)):
            g = (row_get(gma, k, p * 16, 16) + below) * row_get(slm, k, p * 16, 16)
            mg[k, 1 + p] = g.astype(BF16)
            row_put(shifted, k, 8, g)

    for side in range(2):
        below = col_get(bm, 24 if side else 7, 0, 8)
        put(tile, 0, below, 2)
        put(tile, 1, below, 2)
        below = get(tile, 0, 16)
        for c in range(2):
            g = (row_get(gmae, side * 2 + c, 0, 16) + below) * row_get(sle, side * 2 + c, 0, 16)
            row_put(mc, side * 3 + (c + 1 if side else c), 0, g)
            if side == 0 and c == 1:
                col_put(ms1, 7, 0, g)
            if side == 1 and c == 0:
                col_put(ms0, 24, 0, g)
    row_put(mc, 2, 0, col_get(ms0, 8, 0, 16))
    row_put(mc, 3, 0, col_get(ms1, 23, 0, 16))

    @pl.loop(0, 12)
    def _(k):
        mg[k, 0] = row_get(ms1, k, 7, 16).astype(BF16)
        mg[k, 3] = row_get(ms0, k, 9, 16).astype(BF16)

    for k, (x, y) in enumerate(((0, 2), (1, 3), (8, 10), (9, 11))):
        mg[12 + k] = (mg[x].astype(F32) + mg[y].astype(F32)).astype(BF16)
    mg[16] = jnp.zeros((4, 16, C), BF16)

    half_rows = lax.broadcasted_iota(jnp.int32, (16, 1), 0)
    at_north = north & (half_rows < 2)
    at_south = south & ((half_rows == 8) | (half_rows == 9))
    for i in range(6):
        low, mid, high = (rounded(row_get(mc, i, e, 16)) for e in range(3))
        both = low + high
        ml[0, i] = jnp.where(at_north, both, jnp.where(at_south, 0.0, high)).astype(BF16)
        ml[1, i] = mid.astype(BF16)
        ml[2, i] = jnp.where(at_south, both, jnp.where(at_north, 0.0, low)).astype(BF16)

    def mid_t(a, b):
        ph = slice(2 - b, 4 - b)
        if a == 1:
            parts = [mg[1:11, ph].reshape(320, C)]
        else:
            if a == 0:
                top = [jnp.where(north, 12, 2), jnp.where(north, 13, 3)]
                body, tail = 4, [jnp.where(south, 16, 10), jnp.where(south, 16, 11)]
            else:
                top = [jnp.where(north, 16, 0), jnp.where(north, 16, 1)]
                body, tail = 2, [jnp.where(south, 14, 8), jnp.where(south, 15, 9)]
            parts = [mg[r, ph].reshape(32, C) for r in top]
            parts += [mg[body : body + 6, ph].reshape(192, C)]
            parts += [mg[r, ph].reshape(32, C) for r in tail]
        return jnp.concatenate(parts + [ml[a, 2 - b], ml[a, 5 - b]], axis=0)

    res = 0.25 * conv_dot_t(mid_t, wm)
    bfm[...] = res[:320].reshape(10, 32, C)
    for side in range(2):
        row_put(bfe, side, 0, res[320 + 16 * side : 336 + 16 * side])

    @pl.loop(0, 18)
    def _(k):
        for p in range(4):
            g = (
                ctp[k, pl.ds(p * 16, 16)].astype(F32) + bfm[(k + 1) // 2, pl.ds((p // 2) * 16, 16)]
            ) * row_get(slp, k + 1, p * 16, 16)
            g_ext[k, 1 + p] = g.astype(BF16)
            if p == 0:
                row_put(fs0, k, 8, g)
            if p == 3:
                row_put(fs3, k, 8, g)

    for side, (shifted, at) in enumerate(((fs3, 7), (fs0, 24))):
        below = row_get(bfe, side, 0, 16)
        put(tile, 0, below, 2)
        put(tile, 1, below, 2)
        g = (row_get(cte, side, 0, 32) + get(tile, 0, 32)) * row_get(slp_e, 1 + 3 * side, 0, 32)
        row_put(ge, side, 0, g)
        col_put(shifted, at, 0, row_get(ge, side, 1, 24))

    @pl.loop(0, 18)
    def _(k):
        g_ext[k, 0] = row_get(fs3, k, 7, 16).astype(BF16)
        g_ext[k, 5] = row_get(fs0, k, 9, 16).astype(BF16)

    for k, (x, y) in enumerate(((0, 2), (15, 17))):
        g_ext[18 + k] = (g_ext[x].astype(F32) + g_ext[y].astype(F32)).astype(BF16)
    g_ext[20] = jnp.zeros((6, 16, C), BF16)

    def fine_t(a, b):
        ph = slice(2 - b, 6 - b)
        if a == 1:
            return g_ext[1:17, ph].reshape(1024, C)
        if a == 0:
            top, body, tail = jnp.where(north, 18, 2), 3, jnp.where(south, 20, 17)
        else:
            top, body, tail = jnp.where(north, 20, 0), 1, jnp.where(south, 19, 15)
        parts = [g_ext[top, ph].reshape(64, C), g_ext[body : body + 14, ph].reshape(896, C)]
        return jnp.concatenate(parts + [g_ext[tail, ph].reshape(64, C)], axis=0)

    pre[pl.ds(0, 16)] = conv_dot_t(fine_t, wf).reshape(16, 64, C)

    @pl.loop(0, 16)
    def _(r):
        for p in range(4):
            v = row_get(act, r + 2, p * 16, 16) + (am[r // 2, pl.ds((p // 2) * 16, 16)] + ac[r // 4])
            row_put(ns, r, p, v, 4)
            row_put(sx, r, p, pre[r, pl.ds(p * 16, 16)], 4)
        out_v[r] = row_get(ns, r, 0, 64).astype(BF16)
        grad_v[r] = row_get(sx, r, 0, 64).astype(BF16)

    a = load(5, out_v, out_hbm)
    b = load(6, grad_v, grad_hbm)
    for copy in sends:
        copy.wait_send()
    a.wait()
    b.wait()


def body(nlat, nlon, hidden_in, cotangent, weight_fine, weight_mid, weight_coarse):
    hbm = pl.BlockSpec(memory_space=pl.ANY)
    field = (16, 64, C)
    weight = (3, 3, C, C)

    def v(*shape, dtype=BF16):
        return pltpu.VMEM(shape, dtype)

    def f(*shape):
        return pltpu.VMEM(shape, F32)

    scratch = dict(
        hid=v(*field), cot=v(*field), wf=v(*weight), wm=v(*weight), wc=v(*weight), out_v=v(*field), grad_v=v(*field),
        s_ext=f(3, 36 * 80, 128), e_ext=v(22, 6, 16, C), l_edge=v(3, 10, 32, C), pre=f(24, 64, C), pre_e=f(6, 32, C),
        act=f(3, 24 * 64, 128), slp=f(3, 24 * 64, 128), act_e=f(3, 6 * 40, 128), slp_e=f(3, 6 * 32, 128),
        sx=f(3, 16 * 64, 128), ctp=v(18, 64, C), cte=f(3, 2 * 32, 128), gma=f(3, 16 * 32, 128), gmae=f(3, 4 * 16, 128),
        gcax=f(3, 16 * 32, 128),
        pf=v(10, 4, 16, C), sm0=f(3, 16 * 32, 128), sm1=f(3, 16 * 32, 128), pre_m=f(8, 32, C), am=f(8, 32, C),
        slm=f(3, 16 * 32, 128), sle=f(3, 4 * 16, 128), slb=v(8, 32, C), pml=v(4, 16, C), sc=f(3, 12 * 48, 128),
        cb=v(3, 10, 32, C), ac=f(4, 16, C), gs=f(3, 8 * 48, 128), gb=v(3, 13, 32, C), bm=f(3, 8 * 32, 128),
        mg=v(17, 4, 16, C), ms0=f(3, 16 * 32, 128), ms1=f(3, 16 * 32, 128), mc=f(3, 6 * 24, 128), ml=v(3, 6, 16, C),
        bfm=f(10, 32, C), bfe=f(3, 2 * 16, 128), g_ext=v(21, 6, 16, C), fs0=f(3, 24 * 32, 128), fs3=f(3, 24 * 32, 128),
        ge=f(3, 2 * 32, 128), ns=f(3, 16 * 64, 128), tile=f(3, 48, 128), ts=f(3, 288, 128),
        c_buf=v(2, 48, C), k_buf=v(4, 16, C), r_slot=v(2, 3, 64, C), c_slot=v(2, 48, C), k_slot=v(4, 16, C),
        lr_buf=v(2, 160, C), lc_buf=v(2, 48, C), lr_slot=v(2, 160, C), lc_slot=v(6, 48, C),
        pc_buf=v(2, 32, C), pr_slot=v(2, 3, 16, C), sr_slot=v(2, 2, 32, C), pc_slot=v(6, 32, C),
        lsem=pltpu.SemaphoreType.DMA((8,)), ssem=pltpu.SemaphoreType.DMA((4, 8)), rsem=pltpu.SemaphoreType.DMA((4, 8)),
    )
    shape = jax.ShapeDtypeStruct(field, BF16)
    return pl.pallas_call(
        functools.partial(kernel, nlat, nlon),
        out_shape=(shape, shape),
        in_specs=[hbm] * 5,
        out_specs=(hbm, hbm),
        scratch_shapes=list(scratch.values()),
        compiler_params=pltpu.CompilerParams(
            collective_id=0, has_side_effects=True, vmem_limit_bytes=60 * 2**20
        ),
    )(hidden_in, cotangent, weight_fine, weight_mid, weight_coarse)


def solution(mesh):
    field = P("lat", "lon", None)
    return jax.shard_map(
        functools.partial(body, mesh.shape["lat"], mesh.shape["lon"]),
        mesh=mesh,
        in_specs=(field, field, P(), P(), P()),
        out_specs=(field, field),
        check_vma=False,
    )
```

```python
import functools

import jax
import jax.numpy as jnp
from jax import lax
from jax.experimental import pallas as pl
from jax.experimental.pallas import tpu as pltpu
from jax.sharding import PartitionSpec as P

MESH = pl.DeviceIdType.MESH
F32 = jnp.float32
BF16 = jnp.bfloat16
C = 384
LANES = 3


def get(ref, start, n, stride=1):
    ds = pl.ds(start, n) if stride == 1 else pl.ds(start, n, stride=stride)
    return jnp.concatenate([ref[l, ds, :] for l in range(LANES)], axis=-1)


def put(ref, start, val, stride=1):
    n = val.shape[0]
    ds = pl.ds(start, n) if stride == 1 else pl.ds(start, n, stride=stride)
    for l in range(LANES):
        ref[l, ds, :] = val[:, l * 128 : (l + 1) * 128]


class Rows:
    def __init__(self, ref, pitch):
        self.ref, self.pitch = ref, pitch


def at_row(grid, r, start):
    if isinstance(r, int):
        return r * grid.pitch + start
    if start % 8 == 0 and grid.pitch % 8 == 0:
        return pl.multiple_of(r * grid.pitch + start, 8)
    return r * grid.pitch + start


def row_get(grid, r, start, n, stride=1):
    return get(grid.ref, at_row(grid, r, start), n, stride)


def row_put(grid, r, start, val, stride=1):
    put(grid.ref, at_row(grid, r, start), val, stride)


def col_get(grid, c, r0, n):
    return get(grid.ref, r0 * grid.pitch + c, n, grid.pitch)


def col_put(grid, c, r0, val):
    put(grid.ref, r0 * grid.pitch + c, val, grid.pitch)


def gelu_pair(z):
    e = jnp.exp(-0.5 * z * z)
    t = 1.0 / (1.0 + (0.3275911 * 0.7071067811865476) * jnp.abs(z))
    q = t * (
        0.127414796
        + t * (-0.142248368 + t * (0.7107068705 + t * (-0.7265760135 + t * 0.5307027145)))
    )
    h = q * e
    cdf = jnp.where(z >= 0, 1.0 - h, h)
    return z * cdf, cdf + z * (e * 0.3989422804014327)


def rounded(x):
    return x.astype(BF16).astype(F32)


def conv_dot(parts, weight):
    lhs = jnp.concatenate([parts(a, b) for a in range(3) for b in range(3)], axis=-1)
    return jnp.dot(lhs, weight[...].reshape(9 * C, C), preferred_element_type=F32)


def conv_dot_t(parts, weight):
    lhs = jnp.concatenate([parts(a, b) for a in range(3) for b in range(3)], axis=-1)
    rhs = jnp.concatenate([weight[a, b] for a in range(3) for b in range(3)], axis=-1)
    return lax.dot_general(lhs, rhs, (((1,), (1,)), ((), ())), preferred_element_type=F32)


def kernel(
    nlat, nlon,
    hid_hbm, cot_hbm, wf_hbm, wm_hbm, wc_hbm, out_v, g_ext, wf,
    hid, cot, wm, wc,
    s_ext, e_ext, l_edge, l_late, pre, pre_e, act, slp, act_e, slp_e,
    sx, ctp, cte, gma, gmae, gcax,
    pf, sm0, sm1, pre_m, am, slm, sle, slb, pml, sc, cb, ac, gs, gb, bm,
    mg, ms0, ms1, mc, ml, bfm, bfe, fs0, fs3, ge, ns, tile, ts, tk,
    c_buf, k_buf, r_slot, c_slot, k_slot,
    lr_buf, lc_buf, lk_buf, lr_slot, lc_slot, lk_slot,
    pc_buf, pk_buf, pr_slot, sr_slot, ct_slot, pc_slot, pk_slot,
    lsem, ssem, rsem,
):
    s_ext = Rows(s_ext, 80)
    act = Rows(act, 64)
    slp = Rows(slp, 64)
    act_e = Rows(act_e, 40)
    slp_e = Rows(slp_e, 32)
    sx = Rows(sx, 64)
    cte = Rows(cte, 32)
    gma = Rows(gma, 32)
    gmae = Rows(gmae, 16)
    gcax = Rows(gcax, 32)
    sm0 = Rows(sm0, 32)
    sm1 = Rows(sm1, 32)
    slm = Rows(slm, 32)
    sle = Rows(sle, 16)
    sc = Rows(sc, 48)
    gs = Rows(gs, 48)
    bm = Rows(bm, 32)
    ms0 = Rows(ms0, 32)
    ms1 = Rows(ms1, 32)
    mc = Rows(mc, 24)
    bfe = Rows(bfe, 16)
    fs0 = Rows(fs0, 32)
    fs3 = Rows(fs3, 32)
    ge = Rows(ge, 32)
    ns = Rows(ns, 64)
    lat = lax.axis_index("lat")
    lon = lax.axis_index("lon")
    north = lat == 0
    south = lat == nlat - 1
    sgn_n = jnp.where(north, -1, 1)
    sgn_s = jnp.where(south, -1, 1)

    def device(dlat, dlon):
        to_lat, to_lon = lat, lon + dlon + nlon
        if dlat:
            pole = north if dlat < 0 else south
            to_lat = jnp.where(pole, lat, lat + dlat)
            to_lon = to_lon + jnp.where(pole, nlon // 2, 0)
        return {"lat": to_lat, "lon": lax.rem(to_lon, nlon)}

    there = [device(*d) for d in ((-1, 0), (1, 0), (0, -1), (0, 1), (-1, -1), (-1, 1), (1, -1), (1, 1))]
    slot = [
        jnp.where(north, 0, 1), jnp.where(south, 1, 0), 3, 2,
        jnp.where(north, 5, 7), jnp.where(north, 4, 6),
        jnp.where(south, 7, 5), jnp.where(south, 6, 4),
    ]

    def remote(kind, d, src, dst, where):
        return pltpu.make_async_remote_copy(
            src_ref=src, dst_ref=dst, send_sem=ssem.at[kind, d], recv_sem=rsem.at[kind, where],
            device_id=there[d], device_id_type=MESH,
        )

    def load(i, src, dst):
        copy = pltpu.make_async_copy(src, dst, lsem.at[i])
        copy.start()
        return copy

    barrier = pltpu.get_barrier_semaphore()
    for t in there:
        pl.semaphore_signal(barrier, inc=1, device_id=t, device_id_type=MESH)

    hid_in = load(0, hid_hbm, hid)
    wf_in = load(1, wf_hbm, wf)
    sends = []

    def send(kind, d, src, slots, base):
        copy = remote(kind, d, src, slots.at[slot[d] - base], slot[d])
        copy.start()
        sends.append(copy)

    def recv(kind, where, src, dst):
        remote(kind, 0, src, dst, where).wait_recv()

    pl.semaphore_wait(barrier, 8)
    send(0, 0, hid_hbm.at[pl.ds(0, 3)], r_slot, 0)
    send(0, 1, hid_hbm.at[pl.ds(13, 3)], r_slot, 0)
    hid_in.wait()

    @pl.loop(0, 16, unroll=4)
    def _(r):
        row_put(s_ext, r + 3, 8, hid[r].astype(F32))

    for side, first in ((0, 0), (1, 61)):
        for c in range(3):
            c_buf[side, pl.ds(c * 16, 16)] = col_get(s_ext, 8 + first + c, 3, 16).astype(BF16)
    for k, (row, first) in enumerate(((0, 0), (0, 61), (12, 0), (12, 61))):
        for c in range(3):
            put(tile, c * 4, col_get(s_ext, 8 + first + c, 3 + row, 8)[:4])
        k_buf[k] = get(tile, 0, 16).astype(BF16)

    for d in (4, 5, 6, 7):
        send(0, d, k_buf.at[d - 4], k_slot, 4)
    for d in (2, 3):
        send(0, d, c_buf.at[d - 2], c_slot, 2)

    @pl.loop(0, 16, unroll=4)
    def _(r):
        for ph in range(6):
            e_ext[r + 3, ph] = row_get(s_ext, r + 3, 7 + ph, 16, 4).astype(BF16)

    wf_in.wait()
    cot_in = load(2, cot_hbm, cot)
    wm_in = load(3, wm_hbm, wm)
    wc_in = load(4, wc_hbm, wc)
    pre[pl.ds(3, 14)] = conv_dot(
        lambda a, b: e_ext[3 + a : 17 + a, b : b + 4].reshape(14 * 64, C), wf
    ).reshape(14, 64, C)

    def fine_gelu(i):
        a, s = gelu_pair(pre[i])
        row_put(act, i, 0, rounded(a))
        row_put(slp, i, 0, s)

    @pl.loop(3, 17, unroll=2)
    def _(i):
        fine_gelu(i)

    cot_in.wait()

    @pl.loop(0, 16, unroll=4)
    def _(r):
        row_put(sx, r, 0, cot[r].astype(F32))
        for p in range(4):
            ctp[r + 1, pl.ds(p * 16, 16)] = row_get(sx, r, p, 16, 4).astype(BF16)

    @pl.loop(0, 8, unroll=4)
    def _(m):
        for p in range(2):
            total = 0.0
            for dr in range(2):
                for dp in range(2):
                    total = total + ctp[2 * m + dr + 1, pl.ds((2 * p + dp) * 16, 16)].astype(F32)
            row_put(gma, m + 2, p * 16, total)

    for q in range(4):
        total = 0.0
        for dr in range(2):
            for p in range(2):
                total = total + row_get(gma, 2 * q + dr + 2, p * 16, 16)
        row_put(gcax, q + 2, 8, total)

    for side, (mid, coarse) in enumerate(((0, 0), (6, 2))):
        for k in range(2):
            lr_buf[side, pl.ds(32 * k, 32)] = row_get(gma, mid + k + 2, 0, 32).astype(BF16)
            lr_buf[side, pl.ds(64 + 16 * k, 16)] = row_get(gcax, coarse + k + 2, 8, 16).astype(BF16)
    for side, (col, mids, coarse) in enumerate(((0, (0, 16), 0), (63, (15, 31), 14))):
        put(tile, 0, col_get(sx, col, 0, 16))
        for c in range(2):
            put(tile, 16 + 8 * c, col_get(gma, mids[c], 2, 8))
            put(tile, 32 + 4 * c, col_get(gcax, 8 + coarse + c, 2, 8)[:4])
        lc_buf[side] = get(tile, 0, 48).astype(BF16)
        for k, (row, mid, low) in enumerate(((0, 2, 2), (15, 8, 4))):
            for c in range(2):
                put(tile, 2 * c, col_get(gma, mids[c], mid, 8)[:2])
                put(tile, 4 + 2 * c, col_get(gcax, 8 + coarse + c, low, 8)[:2])
            put(tile, 8, get(sx.ref, row * 64 + col, 1))
            lk_buf[2 * k + side] = get(tile, 0, 16).astype(BF16)

    side_e, side_l = jnp.where(north, 1, 0), jnp.where(north, 0, 1)
    sgn_l = jnp.where(north | south, -1, 1)

    def receive(side):
        recv(0, side, hid.at[pl.ds(0, 3)], r_slot.at[side])
        for k in range(2):
            recv(0, 4 + 2 * side + k, k_buf.at[k], k_slot.at[2 * side + k])

    def place(side, first, step, row_order, corner_order):
        for j in range(3):
            row_put(s_ext, first + step * j, 8, r_slot[side, row_order(j)].astype(F32))
        for k in range(2):
            put(tile, 0, k_slot[2 * side + k].astype(F32))
            for c in range(3):
                for j in range(3):
                    at = (first + step * j) * 80 + 8 + (64 if k else -3) + c
                    put(s_ext.ref, at, get(tile, c * 4 + corner_order(j), 1))

    def phases(r, which):
        for ph in which:
            e_ext[r, ph] = row_get(s_ext, r, 7 + ph, 16, 4).astype(BF16)

    def pool_row(m):
        for p, shifted in ((0, sm0), (1, sm1)):
            total = 0.0
            for dr in range(2):
                for dp in range(2):
                    total = total + row_get(act, 2 * m + dr, (2 * p + dp) * 16, 16)
            total = 0.25 * total
            pf[m, 1 + p] = total.astype(BF16)
            row_put(shifted, m, 8, total)

    def pool_edges():
        for first, shifted, at in ((0, sm1, 7), (4, sm0, 24)):
            total = 0.0
            for c in range(2):
                for dr in range(2):
                    total = total + row_get(act_e, first + c, dr, 16, 2)
            col_put(shifted, at, 0, 0.25 * total)

    def pool_shift(m):
        pf[m, 0] = row_get(sm1, m, 7, 16).astype(BF16)
        pf[m, 3] = row_get(sm0, m, 9, 16).astype(BF16)

    def mid_gelu(m):
        a, s = gelu_pair(pre_m[m])
        am[m] = rounded(a)
        row_put(slm, m + 2, 0, s)
        slb[m] = s.astype(BF16)

    receive(side_e)
    for k in range(2):
        recv(0, 2 + k, c_buf.at[k], c_slot.at[k])
    for side, first in ((0, -3), (1, 64)):
        for c in range(3):
            col_put(s_ext, 8 + first + c, 3, c_slot[side, pl.ds(c * 16, 16)].astype(F32))
    place(
        side_e, jnp.where(north, 19, 2), jnp.where(north, 1, -1),
        lambda j: jnp.where(north, j, 2 - j), lambda j: jnp.where(north, j, 3 - j),
    )
    for i in range(3):
        phases(jnp.where(north, 19, 0) + i, range(6))
    for r in (3, 4, 17, 18):
        phases(r, (0, 5))

    @pl.loop(0, 10, unroll=5)
    def _(i):
        col = 8 - 3 + i + (i // 5) * 60
        for a in range(3):
            l_edge[a, i] = get(s_ext.ref, a * 80 + col, 32, 80).astype(BF16)

    def ring(a, b):
        parts = [e_ext[jnp.where(north, 20 - q, 1 + q) + a - 1, b : b + 4].reshape(64, C) for q in range(3)]
        parts += [l_edge[a, s * 5 + b : s * 5 + b + 3].reshape(96, C) for s in range(2)]
        return jnp.concatenate(parts, axis=0)

    res = conv_dot(ring, wf)
    for q in range(3):
        pre[jnp.where(north, 19 - q, q)] = res[q * 64 : (q + 1) * 64]
    pre_e[...] = res[192:].reshape(6, 32, C)

    @pl.loop(0, 6, unroll=2)
    def _(i):
        a, s = gelu_pair(pre_e[i])
        row_put(act_e, i, 0, rounded(a))
        row_put(slp_e, i, 0, s)

    for dst, src in ((act, act_e), (slp, slp_e)):
        col_put(dst, 0, 0, row_get(src, 2, 0, 24))
        col_put(dst, 63, 0, row_get(src, 3, 0, 24))

    @pl.loop(0, 3, unroll=3)
    def _(q):
        fine_gelu(jnp.where(north, 17, 0) + q)

    wm_in.wait()

    @pl.loop(0, 8, unroll=4)
    def _(i):
        pool_row(jnp.where(north, 2, 0) + i)

    pool_edges()

    @pl.loop(0, 8, unroll=8)
    def _(i):
        pool_shift(jnp.where(north, 2, 0) + i)

    early = jnp.where(north, 2, 0)
    pre_m[pl.ds(early, 6)] = conv_dot(
        lambda a, b: pf[pl.ds(early + a, 6), b : b + 2].reshape(192, C), wm
    ).reshape(6, 32, C)

    @pl.loop(0, 6, unroll=2)
    def _(i):
        mid_gelu(early + i)

    receive(side_l)
    for d in (0, 1):
        send(1, d, lr_buf.at[d], lr_slot, 0)
    for d in (2, 3):
        send(1, d, lc_buf.at[d - 2], lc_slot, 2)
    for d in (4, 5, 6, 7):
        send(1, d, lk_buf.at[d - 4], lk_slot, 4)

    place(
        side_l, jnp.where(north, 2, 19), jnp.where(north, -1, 1),
        lambda j: jnp.where(south, 2 - j, j), lambda j: jnp.where(south, 3 - j, j),
    )
    for i in range(3):
        phases(jnp.where(north, 0, 19) + i, range(6))
    edge_first = jnp.where(north, 0, 17)
    edge_rows = lax.broadcasted_iota(jnp.int32, (16, 1), 0)
    flip = (north & (edge_rows < 2)) | (south & ((edge_rows == 1) | (edge_rows == 2)))

    @pl.loop(0, 10, unroll=5)
    def _(i):
        col = 8 - 3 + i + (i // 5) * 60
        low, mid, high = (get(s_ext.ref, (edge_first + a) * 80 + col, 16, 80) for a in range(3))
        l_late[0, i] = jnp.where(flip, high, low).astype(BF16)
        l_late[1, i] = mid.astype(BF16)
        l_late[2, i] = jnp.where(flip, low, high).astype(BF16)

    def ring_late(a, b):
        rows = [jnp.where(north, 1 + q, 20 - q) + (1 if q == 2 else sgn_l) * (a - 1) for q in range(3)]
        parts = [e_ext[r, b : b + 4].reshape(64, C) for r in rows]
        parts += [l_late[a, s * 5 + b : s * 5 + b + 3].reshape(48, C) for s in range(2)]
        return jnp.concatenate(parts, axis=0)

    res = conv_dot(ring_late, wf)
    for q in range(3):
        pre[jnp.where(north, q, 19 - q)] = res[q * 64 : (q + 1) * 64]
    for i in range(6):
        a, s = gelu_pair(res[192 + 16 * i : 208 + 16 * i])
        a = rounded(a)
        for k in range(3):
            put(act_e.ref, i * act_e.pitch + edge_first + k, a[k : k + 1])
            put(slp_e.ref, i * slp_e.pitch + edge_first + k, s[k : k + 1])

    @pl.loop(0, 3, unroll=3)
    def _(q):
        fine_gelu(jnp.where(north, 0, 17) + q)

    for i in range(2):
        pool_row(jnp.where(north, 0, 8) + i)
    pool_edges()
    for i in range(2):
        pool_shift(jnp.where(north, 0, 8) + i)
    late = jnp.where(north, 0, 6)
    pre_m[pl.ds(late, 2)] = conv_dot(
        lambda a, b: pf[pl.ds(late + a, 2), b : b + 2].reshape(64, C), wm
    ).reshape(2, 32, C)
    for i in range(2):
        mid_gelu(late + i)

    for q in range(4):
        total = 0.0
        for dr in range(2):
            for p in range(2):
                total = total + am[2 * q + dr, pl.ds(p * 16, 16)]
        total = 0.25 * total
        pml[q] = total.astype(BF16)
        row_put(sc, q + 3, 16, total)
    for side, (first, mids) in enumerate(((0, (0, 16)), (13, (15, 31)))):
        for c in range(3):
            put(tile, c * 4, col_get(sc, 16 + first + c, 3, 8)[:4])
        for c in range(2):
            put(tile, 16 + 8 * c, col_get(slm, mids[c], 2, 8))
        pc_buf[side] = get(tile, 0, 32).astype(BF16)
        for k, row in enumerate((2, 8)):
            for c in range(2):
                put(tile, 12 + 2 * c, col_get(slm, mids[c], row, 8)[:2])
            pk_buf[2 * k + side] = get(tile, 0, 16).astype(BF16)

    for d in (0, 1):
        send(2, d, pml.at[pl.ds(d, 3)], pr_slot, 0)
    for d in (4, 5, 6, 7):
        send(2, d, pk_buf.at[d - 4], pk_slot, 4)
    for d in (2, 3):
        send(2, d, pc_buf.at[d - 2], pc_slot, 2)
    for d in (0, 1):
        send(3, d, slb.at[pl.ds(6 * d, 2)], sr_slot, 0)
    for d in (0, 1):
        send(4, d, ctp.at[1 + 15 * d], ct_slot, 0)

    @pl.loop(0, 16, unroll=4)
    def _(r):
        for p in range(4):
            v = row_get(act, r + 2, p * 16, 16) + am[r // 2, pl.ds((p // 2) * 16, 16)]
            row_put(ns, r, p, v, 4)

    for k in range(2):
        recv(1, k, lr_buf.at[k], lr_slot.at[k])
    for k in range(2):
        recv(1, 2 + k, lc_buf.at[0], lc_slot.at[k])
        put(ts, k * 48, lc_slot[k].astype(F32))
    for k in range(4):
        recv(1, 4 + k, lk_buf.at[0], lk_slot.at[k])
        put(tk, k * 16, lk_slot[k].astype(F32))

    def pick(k, at):
        return get(ts, k * 48 + at, 1)

    def corner(k, at):
        return get(tk, k * 16 + at, 1)

    def edge_columns(dst, base, corner_base):
        for side in range(2):
            for c in range(2):
                to = side * 2 + c
                row_put(dst, to, 2, get(ts, side * 48 + base + 8 * c, 8))
                for j in range(2):
                    at = corner_base + 2 * c
                    row_put(dst, to, 1 - j, corner(side, at + jnp.where(north, j, 1 - j)))
                    row_put(dst, to, 10 + j, corner(2 + side, at + jnp.where(south, 1 - j, j)))

    for j in range(2):
        at_n, at_s = jnp.where(north, j, 1 - j), jnp.where(south, 1 - j, j)
        row_put(gma, 1 - j, 0, lr_slot[0, pl.ds(pl.multiple_of(32 * at_n, 32), 32)].astype(F32))
        row_put(gma, 10 + j, 0, lr_slot[1, pl.ds(pl.multiple_of(32 * at_s, 32), 32)].astype(F32))
        row_put(gcax, 1 - j, 8, lr_slot[0, pl.ds(pl.multiple_of(64 + 16 * at_n, 16), 16)].astype(F32))
        row_put(gcax, 6 + j, 8, lr_slot[1, pl.ds(pl.multiple_of(64 + 16 * at_s, 16), 16)].astype(F32))
    for side in range(2):
        row_put(cte, side, 2, get(ts, side * 48, 16))
        row_put(cte, side, 1, corner(side, 8))
        row_put(cte, side, 18, corner(2 + side, 8))
        for c in range(2):
            col = 8 + (16 if side else -2) + c
            for q in range(4):
                row_put(gcax, q + 2, col, pick(side, 32 + 4 * c + q))
            for j in range(2):
                row_put(gcax, 1 - j, col, corner(side, 4 + 2 * c + jnp.where(north, j, 1 - j)))
                row_put(gcax, 6 + j, col, corner(2 + side, 4 + 2 * c + jnp.where(south, 1 - j, j)))
    edge_columns(gmae, 16, 0)

    wc_in.wait()
    for k in range(2):
        recv(2, k, pml.at[pl.ds(0, 3)], pr_slot.at[k])
    for k in range(2):
        recv(2, 2 + k, pc_buf.at[0], pc_slot.at[k])
        put(ts, k * 48, pc_slot[k].astype(F32))
    for k in range(4):
        recv(2, 4 + k, pk_buf.at[0], pk_slot.at[k])
        put(tk, k * 16, pk_slot[k].astype(F32))
    for j in range(3):
        row_put(sc, 2 - j, 16, pr_slot[0, jnp.where(north, j, 2 - j)].astype(F32))
        row_put(sc, 7 + j, 16, pr_slot[1, jnp.where(south, 2 - j, j)].astype(F32))
    for side in range(2):
        for c in range(3):
            col = 16 + (16 if side else -3) + c
            for q in range(4):
                row_put(sc, q + 3, col, pick(side, 4 * c + q))
            for j in range(3):
                row_put(sc, 2 - j, col, corner(side, 4 * c + jnp.where(north, j, 3 - j)))
                row_put(sc, 7 + j, col, corner(2 + side, 4 * c + jnp.where(south, 3 - j, j)))

    @pl.loop(0, 10, unroll=True)
    def _(r):
        for b in range(3):
            cb[b, r] = row_get(sc, r, 7 + b, 32).astype(BF16)

    def coarse(a, b):
        rows = [1 + sgn_n * (a - 1), 2 + sgn_n * (a - 1)]
        tail = [7 + sgn_s * (a - 1), 8 + sgn_s * (a - 1)]
        parts = [cb[b, r] for r in rows] + [cb[b, 2 + a : 6 + a].reshape(128, C)]
        return jnp.concatenate(parts + [cb[b, r] for r in tail], axis=0)

    res = conv_dot(coarse, wc)
    for i in range(8):
        a, s = gelu_pair(res[i * 32 : (i + 1) * 32])
        if 2 <= i < 6:
            ac[i - 2] = rounded(a[8:24])
        row_put(gs, i, 8, row_get(gcax, i, 0, 32) * s)

    @pl.loop(0, 8, unroll=True)
    def _(r):
        for d in range(3):
            gb[d, r] = row_get(gs, r, 7 + d, 32).astype(BF16)

    for d in range(3):
        for k, (x, y) in enumerate(((0, 2), (1, 3), (4, 6), (5, 7))):
            gb[d, 8 + k] = (gb[d, x].astype(F32) + gb[d, y].astype(F32)).astype(BF16)
        gb[d, 12] = jnp.zeros((32, C), BF16)

    def coarse_t(a, b):
        d = 2 - b
        if a == 1:
            return gb[d, 1:7].reshape(192, C)
        if a == 0:
            rows = [jnp.where(north, 8, 2), jnp.where(north, 9, 3), 4, 5, jnp.where(south, 12, 6), jnp.where(south, 12, 7)]
        else:
            rows = [jnp.where(north, 12, 0), jnp.where(north, 12, 1), 2, 3, jnp.where(south, 10, 4), jnp.where(south, 11, 5)]
        return jnp.concatenate([gb[d, r] for r in rows], axis=0)

    res = conv_dot_t(coarse_t, wc)
    for i in range(6):
        row_put(bm, i, 0, 0.25 * res[i * 32 : (i + 1) * 32])

    for q in range(4):
        for p in range(4):
            row_put(sx, q, p, ac[q], 4)
    for r in range(16):
        out_v[r] = (row_get(ns, r, 0, 64) + row_get(sx, r // 4, 0, 64)).astype(BF16)

    for k in range(2):
        recv(3, k, slb.at[pl.ds(0, 2)], sr_slot.at[k])
    for j in range(2):
        row_put(slm, 1 - j, 0, sr_slot[0, jnp.where(north, j, 1 - j)].astype(F32))
        row_put(slm, 10 + j, 0, sr_slot[1, jnp.where(south, 1 - j, j)].astype(F32))
    edge_columns(sle, 16, 12)

    @pl.loop(0, 12, unroll=True)
    def _(k):
        below = row_get(bm, k // 2, 8, 16)
        for p, shifted in ((0, ms0), (1, ms1)):
            g = (row_get(gma, k, p * 16, 16) + below) * row_get(slm, k, p * 16, 16)
            mg[k, 1 + p] = g.astype(BF16)
            row_put(shifted, k, 8, g)

    for side in range(2):
        below = col_get(bm, 24 if side else 7, 0, 8)
        put(tile, 0, below, 2)
        put(tile, 1, below, 2)
        below = get(tile, 0, 16)
        for c in range(2):
            g = (row_get(gmae, side * 2 + c, 0, 16) + below) * row_get(sle, side * 2 + c, 0, 16)
            row_put(mc, side * 3 + (c + 1 if side else c), 0, g)
            if side == 0 and c == 1:
                col_put(ms1, 7, 0, g)
            if side == 1 and c == 0:
                col_put(ms0, 24, 0, g)
    row_put(mc, 2, 0, col_get(ms0, 8, 0, 16))
    row_put(mc, 3, 0, col_get(ms1, 23, 0, 16))

    @pl.loop(0, 12, unroll=True)
    def _(k):
        mg[k, 0] = row_get(ms1, k, 7, 16).astype(BF16)
        mg[k, 3] = row_get(ms0, k, 9, 16).astype(BF16)

    for k, (x, y) in enumerate(((0, 2), (1, 3), (8, 10), (9, 11))):
        mg[12 + k] = (mg[x].astype(F32) + mg[y].astype(F32)).astype(BF16)
    mg[16] = jnp.zeros((4, 16, C), BF16)

    half_rows = lax.broadcasted_iota(jnp.int32, (16, 1), 0)
    at_north = north & (half_rows < 2)
    at_south = south & ((half_rows == 8) | (half_rows == 9))
    for i in range(6):
        low, mid, high = (rounded(row_get(mc, i, e, 16)) for e in range(3))
        both = low + high
        ml[0, i] = jnp.where(at_north, both, jnp.where(at_south, 0.0, high)).astype(BF16)
        ml[1, i] = mid.astype(BF16)
        ml[2, i] = jnp.where(at_south, both, jnp.where(at_north, 0.0, low)).astype(BF16)

    def mid_t(a, b):
        ph = slice(2 - b, 4 - b)
        if a == 1:
            parts = [mg[1:11, ph].reshape(320, C)]
        else:
            if a == 0:
                top = [jnp.where(north, 12, 2), jnp.where(north, 13, 3)]
                body, tail = 4, [jnp.where(south, 16, 10), jnp.where(south, 16, 11)]
            else:
                top = [jnp.where(north, 16, 0), jnp.where(north, 16, 1)]
                body, tail = 2, [jnp.where(south, 14, 8), jnp.where(south, 15, 9)]
            parts = [mg[r, ph].reshape(32, C) for r in top]
            parts += [mg[body : body + 6, ph].reshape(192, C)]
            parts += [mg[r, ph].reshape(32, C) for r in tail]
        return jnp.concatenate(parts + [ml[a, 2 - b], ml[a, 5 - b]], axis=0)

    res = 0.25 * conv_dot_t(mid_t, wm)
    bfm[...] = res[:320].reshape(10, 32, C)
    for side in range(2):
        row_put(bfe, side, 0, res[320 + 16 * side : 336 + 16 * side])

    for k in range(2):
        recv(4, k, ctp.at[1], ct_slot.at[k])
        ctp[17 * k] = ct_slot[k]

    @pl.loop(0, 18, unroll=6)
    def _(k):
        for p in range(4):
            g = (
                ctp[k, pl.ds(p * 16, 16)].astype(F32) + bfm[(k + 1) // 2, pl.ds((p // 2) * 16, 16)]
            ) * row_get(slp, k + 1, p * 16, 16)
            g_ext[k, 1 + p] = g.astype(BF16)
            if p == 0:
                row_put(fs0, k, 8, g)
            if p == 3:
                row_put(fs3, k, 8, g)

    for side, (shifted, at) in enumerate(((fs3, 7), (fs0, 24))):
        below = row_get(bfe, side, 0, 16)
        put(tile, 0, below, 2)
        put(tile, 1, below, 2)
        g = (row_get(cte, side, 0, 32) + get(tile, 0, 32)) * row_get(slp_e, 1 + 3 * side, 0, 32)
        row_put(ge, side, 0, g)
        col_put(shifted, at, 0, row_get(ge, side, 1, 24))

    @pl.loop(0, 18, unroll=True)
    def _(k):
        g_ext[k, 0] = row_get(fs3, k, 7, 16).astype(BF16)
        g_ext[k, 5] = row_get(fs0, k, 9, 16).astype(BF16)

    for k, (x, y) in enumerate(((0, 2), (15, 17))):
        g_ext[18 + k] = (g_ext[x].astype(F32) + g_ext[y].astype(F32)).astype(BF16)
    g_ext[20] = jnp.zeros((6, 16, C), BF16)

    for copy in sends:
        copy.wait_send()


def last_kernel(nlat, out_v, g_ext, wf, out_hbm, grad_hbm, grad_v, sx, sem):
    lat = lax.axis_index("lat")
    north = lat == 0
    south = lat == nlat - 1
    sx = Rows(sx, 64)
    copies = [pltpu.make_async_copy(out_v, out_hbm, sem.at[0])]
    copies[0].start()
    for h in range(2):

        def fine_t(a, b):
            ph = slice(2 - b, 6 - b)
            if a == 1:
                return g_ext[8 * h + 1 : 8 * h + 9, ph].reshape(512, C)
            first = 8 * h + 2 - a
            if h == 0:
                row = jnp.where(north, 20 if a else 18, first)
                parts = [g_ext[row, ph].reshape(64, C), g_ext[first + 1 : first + 8, ph].reshape(448, C)]
            else:
                row = jnp.where(south, 19 if a else 20, first + 7)
                parts = [g_ext[first : first + 7, ph].reshape(448, C), g_ext[row, ph].reshape(64, C)]
            return jnp.concatenate(parts, axis=0)

        res = conv_dot_t(fine_t, wf)
        for r in range(8):
            for p in range(4):
                row_put(sx, 8 * h + r, p, res[r * 64 + p * 16 : r * 64 + p * 16 + 16], 4)
            grad_v[8 * h + r] = row_get(sx, 8 * h + r, 0, 64).astype(BF16)
        half = pl.ds(8 * h, 8)
        copies.append(pltpu.make_async_copy(grad_v.at[half], grad_hbm.at[half], sem.at[1 + h]))
        copies[-1].start()
    for copy in copies:
        copy.wait()


def body(nlat, nlon, hidden_in, cotangent, weight_fine, weight_mid, weight_coarse):
    hbm = pl.BlockSpec(memory_space=pltpu.HBM)
    field = (16, 64, C)
    weight = (3, 3, C, C)

    def v(*shape, dtype=BF16):
        return pltpu.VMEM(shape, dtype)

    def f(*shape):
        return pltpu.VMEM(shape, F32)

    scratch = dict(
        hid=v(*field), cot=v(*field), wm=v(*weight), wc=v(*weight),
        s_ext=f(3, 36 * 80, 128), e_ext=v(22, 6, 16, C), l_edge=v(3, 10, 32, C), l_late=v(3, 10, 16, C), pre=f(24, 64, C), pre_e=f(6, 32, C),
        act=f(3, 24 * 64, 128), slp=f(3, 24 * 64, 128), act_e=f(3, 6 * 40, 128), slp_e=f(3, 6 * 32, 128),
        sx=f(3, 16 * 64, 128), ctp=v(18, 64, C), cte=f(3, 2 * 32, 128), gma=f(3, 16 * 32, 128), gmae=f(3, 4 * 16, 128),
        gcax=f(3, 16 * 32, 128),
        pf=v(10, 4, 16, C), sm0=f(3, 16 * 32, 128), sm1=f(3, 16 * 32, 128), pre_m=f(8, 32, C), am=f(8, 32, C),
        slm=f(3, 16 * 32, 128), sle=f(3, 4 * 16, 128), slb=v(8, 32, C), pml=v(4, 16, C), sc=f(3, 12 * 48, 128),
        cb=v(3, 10, 32, C), ac=f(4, 16, C), gs=f(3, 8 * 48, 128), gb=v(3, 13, 32, C), bm=f(3, 8 * 32, 128),
        mg=v(17, 4, 16, C), ms0=f(3, 16 * 32, 128), ms1=f(3, 16 * 32, 128), mc=f(3, 6 * 24, 128), ml=v(3, 6, 16, C),
        bfm=f(10, 32, C), bfe=f(3, 2 * 16, 128), fs0=f(3, 24 * 32, 128), fs3=f(3, 24 * 32, 128),
        ge=f(3, 2 * 32, 128), ns=f(3, 16 * 64, 128), tile=f(3, 48, 128), ts=f(3, 96, 128), tk=f(3, 64, 128),
        c_buf=v(2, 48, C), k_buf=v(4, 16, C), r_slot=v(2, 3, 64, C), c_slot=v(2, 48, C), k_slot=v(4, 16, C),
        lr_buf=v(2, 96, C), lc_buf=v(2, 48, C), lk_buf=v(4, 16, C),
        lr_slot=v(2, 96, C), lc_slot=v(2, 48, C), lk_slot=v(4, 16, C),
        pc_buf=v(2, 32, C), pk_buf=v(4, 16, C),
        pr_slot=v(2, 3, 16, C), sr_slot=v(2, 2, 32, C), ct_slot=v(2, 64, C), pc_slot=v(2, 32, C), pk_slot=v(4, 16, C),
        lsem=pltpu.SemaphoreType.DMA((8,)), ssem=pltpu.SemaphoreType.DMA((5, 8)), rsem=pltpu.SemaphoreType.DMA((5, 8)),
    )
    vmem = pl.BlockSpec(memory_space=pltpu.VMEM)
    results = pl.pallas_call(
        functools.partial(kernel, nlat, nlon),
        out_shape=(v(*field), v(21, 6, 16, C), v(*weight)),
        in_specs=[hbm] * 5,
        out_specs=(vmem, vmem, vmem),
        scratch_shapes=list(scratch.values()),
        compiler_params=pltpu.CompilerParams(
            collective_id=0, has_side_effects=True, vmem_limit_bytes=52 * 2**20
        ),
    )(hidden_in, cotangent, weight_fine, weight_mid, weight_coarse)
    shape = jax.ShapeDtypeStruct(field, BF16)
    return pl.pallas_call(
        functools.partial(last_kernel, nlat),
        out_shape=(shape, shape),
        in_specs=[vmem] * 3,
        out_specs=(hbm, hbm),
        scratch_shapes=[v(*field), f(3, 16 * 64, 128), pltpu.SemaphoreType.DMA((3,))],
        compiler_params=pltpu.CompilerParams(vmem_limit_bytes=40 * 2**20),
    )(*results)


def solution(mesh):
    field = P("lat", "lon", None)
    return jax.shard_map(
        functools.partial(body, mesh.shape["lat"], mesh.shape["lon"]),
        mesh=mesh,
        in_specs=(field, field, P(), P(), P()),
        out_specs=(field, field),
        check_vma=False,
    )
```

```python
import functools

import jax
import jax.numpy as jnp
from jax import lax
from jax.experimental import pallas as pl
from jax.experimental.pallas import tpu as pltpu
from jax.sharding import PartitionSpec as P

MESH = pl.DeviceIdType.MESH
F32 = jnp.float32
BF16 = jnp.bfloat16
C = 384
LANES = 3


def get(ref, start, n, stride=1):
    ds = pl.ds(start, n) if stride == 1 else pl.ds(start, n, stride=stride)
    return jnp.concatenate([ref[l, ds, :] for l in range(LANES)], axis=-1)


def put(ref, start, val, stride=1):
    n = val.shape[0]
    ds = pl.ds(start, n) if stride == 1 else pl.ds(start, n, stride=stride)
    for l in range(LANES):
        ref[l, ds, :] = val[:, l * 128 : (l + 1) * 128]


class Rows:
    def __init__(self, ref, pitch):
        self.ref, self.pitch = ref, pitch


def at_row(grid, r, start):
    if isinstance(r, int):
        return r * grid.pitch + start
    if start % 8 == 0 and grid.pitch % 8 == 0:
        return pl.multiple_of(r * grid.pitch + start, 8)
    return r * grid.pitch + start


def row_get(grid, r, start, n, stride=1):
    return get(grid.ref, at_row(grid, r, start), n, stride)


def row_put(grid, r, start, val, stride=1):
    put(grid.ref, at_row(grid, r, start), val, stride)


def col_get(grid, c, r0, n):
    return get(grid.ref, r0 * grid.pitch + c, n, grid.pitch)


def col_put(grid, c, r0, val):
    put(grid.ref, r0 * grid.pitch + c, val, grid.pitch)


def gelu_pair(z):
    e = jnp.exp(-0.5 * z * z)
    t = 1.0 / (1.0 + (0.3275911 * 0.7071067811865476) * jnp.abs(z))
    q = t * (
        0.127414796
        + t * (-0.142248368 + t * (0.7107068705 + t * (-0.7265760135 + t * 0.5307027145)))
    )
    h = q * e
    cdf = jnp.where(z >= 0, 1.0 - h, h)
    return z * cdf, cdf + z * (e * 0.3989422804014327)


def rounded(x):
    return x.astype(BF16).astype(F32)


def conv_dot(parts, weight):
    lhs = jnp.concatenate([parts(a, b) for a in range(3) for b in range(3)], axis=-1)
    return jnp.dot(lhs, weight[...].reshape(9 * C, C), preferred_element_type=F32)


def conv_dot_t(parts, weight):
    lhs = jnp.concatenate([parts(a, b) for a in range(3) for b in range(3)], axis=-1)
    rhs = jnp.concatenate([weight[a, b] for a in range(3) for b in range(3)], axis=-1)
    return lax.dot_general(lhs, rhs, (((1,), (1,)), ((), ())), preferred_element_type=F32)


def kernel(
    nlat, nlon,
    hid_hbm, cot_hbm, wf_hbm, wm_hbm, wc_hbm, ns, ac, g_ext, wf,
    hid, cot, wm, wc,
    s_ext, e_ext, l_edge, l_late, pre, pre_e, act, slp, act_e, slp_e,
    sx, ctp, cte, gma, gmae, gcax,
    pf, sm0, sm1, pre_m, am, slm, sle, slb, pml, sc, cb, gs, gb, bm,
    mg, ms0, ms1, mc, ml, bfm, bfe, fs0, fs3, ge, tile, ts, tk,
    c_buf, k_buf, r_slot, c_slot, k_slot, kp_buf, kp_slot,
    lr_buf, lc_buf, lk_buf, lr_slot, lc_slot, lk_slot,
    pc_buf, pk_buf, p2_buf, p2_slot, sl_buf, sl_slot, pr_slot, sr_slot, ct_slot, pc_slot, pk_slot,
    lsem, ssem, rsem,
):
    s_ext = Rows(s_ext, 80)
    act = Rows(act, 64)
    slp = Rows(slp, 64)
    act_e = Rows(act_e, 40)
    slp_e = Rows(slp_e, 32)
    sx = Rows(sx, 64)
    cte = Rows(cte, 32)
    gma = Rows(gma, 32)
    gmae = Rows(gmae, 16)
    gcax = Rows(gcax, 32)
    sm0 = Rows(sm0, 32)
    sm1 = Rows(sm1, 32)
    slm = Rows(slm, 32)
    sle = Rows(sle, 16)
    sc = Rows(sc, 48)
    gs = Rows(gs, 48)
    bm = Rows(bm, 32)
    ms0 = Rows(ms0, 32)
    ms1 = Rows(ms1, 32)
    mc = Rows(mc, 24)
    bfe = Rows(bfe, 16)
    fs0 = Rows(fs0, 32)
    fs3 = Rows(fs3, 32)
    ge = Rows(ge, 32)
    ns = Rows(ns, 64)
    lat = lax.axis_index("lat")
    lon = lax.axis_index("lon")
    north = lat == 0
    south = lat == nlat - 1
    sgn_n = jnp.where(north, -1, 1)
    sgn_s = jnp.where(south, -1, 1)

    def device(dlat, dlon):
        to_lat, to_lon = lat, lon + dlon + nlon
        if dlat:
            pole = north if dlat < 0 else south
            to_lat = jnp.where(pole, lat, lat + dlat)
            to_lon = to_lon + jnp.where(pole, nlon // 2, 0)
        return {"lat": to_lat, "lon": lax.rem(to_lon, nlon)}

    there = [device(*d) for d in ((-1, 0), (1, 0), (0, -1), (0, 1), (-1, -1), (-1, 1), (1, -1), (1, 1))]
    slot = [
        jnp.where(north, 0, 1), jnp.where(south, 1, 0), 3, 2,
        jnp.where(north, 5, 7), jnp.where(north, 4, 6),
        jnp.where(south, 7, 5), jnp.where(south, 6, 4),
    ]

    def remote(kind, d, src, dst, where, target):
        return pltpu.make_async_remote_copy(
            src_ref=src, dst_ref=dst, send_sem=ssem.at[kind, d], recv_sem=rsem.at[kind, where],
            device_id=target, device_id_type=MESH,
        )

    def load(i, src, dst):
        copy = pltpu.make_async_copy(src, dst, lsem.at[i])
        copy.start()
        return copy

    barrier = pltpu.get_barrier_semaphore()
    for t in there:
        pl.semaphore_signal(barrier, inc=1, device_id=t, device_id_type=MESH)

    hid_in = load(0, hid_hbm, hid)
    wf_in = load(1, wf_hbm, wf)
    sends = []

    def send(kind, d, src, slots, base):
        copy = remote(kind, d, src, slots.at[slot[d] - base], slot[d], there[d])
        copy.start()
        sends.append(copy)

    def recv(kind, where, src, dst):
        remote(kind, 0, src, dst, where, there[0]).wait_recv()

    pl.semaphore_wait(barrier, 8)
    pole = north | south
    far = {k: jnp.where(north, there[0][k], there[1][k]) for k in ("lat", "lon")}
    near = {k: jnp.where(north, there[1][k], there[0][k]) for k in ("lat", "lon")}
    far_slot, near_slot = jnp.where(north, slot[0], slot[1]), jnp.where(north, slot[1], slot[0])

    def far_rows(n):
        src = hid_hbm.at[pl.ds(jnp.where(north, 0, 16 - n), n)]
        return remote(0, 0, src, r_slot.at[far_slot, pl.ds(0, n)], far_slot, far)

    @pl.when(pole)
    def _():
        far_rows(1).start()

    @pl.when(jnp.logical_not(pole))
    def _():
        far_rows(3).start()

    copy = remote(0, 1, hid_hbm.at[pl.ds(jnp.where(north, 13, 0), 3)], r_slot.at[near_slot], near_slot, near)
    copy.start()
    sends.append(copy)
    hid_in.wait()

    @pl.loop(0, 16, unroll=4)
    def _(r):
        row_put(s_ext, r + 3, 8, hid[r].astype(F32))

    for side, first in ((0, 0), (1, 61)):
        for c in range(3):
            c_buf[side, pl.ds(c * 16, 16)] = col_get(s_ext, 8 + first + c, 3, 16).astype(BF16)
    for k, (row, first) in enumerate(((0, 0), (0, 61), (12, 0), (12, 61))):
        for c in range(3):
            put(tile, c * 4, col_get(s_ext, 8 + first + c, 3 + row, 8)[:4])
        k_buf[k] = get(tile, 0, 16).astype(BF16)

    for side, first in ((0, 0), (1, 61)):
        at = (3 + jnp.where(north, 0, 15)) * 80 + 8 + first
        for c in range(3):
            for l in range(LANES):
                tile[0, pl.ds(3 * c + l, 1), :] = s_ext.ref[l, pl.ds(at + c, 1), :]
        kp_buf[side] = tile[0, pl.ds(0, 16), :].astype(BF16)

    def corner_copy(side, at_far, small):
        top = north if at_far else jnp.logical_not(north)
        target = {k: jnp.where(top, there[4 + side][k], there[6 + side][k]) for k in ("lat", "lon")}
        to = jnp.where(top, slot[4 + side], slot[6 + side])
        if small:
            return remote(0, 4 + side, kp_buf.at[side], kp_slot.at[to - 4], to, target)
        src = k_buf.at[side + jnp.where(top, 0, 2)]
        return remote(0, (4 if at_far else 6) + side, src, k_slot.at[to - 4], to, target)

    @pl.when(pole)
    def _():
        for side in range(2):
            corner_copy(side, True, True).start()

    @pl.when(jnp.logical_not(pole))
    def _():
        for side in range(2):
            corner_copy(side, True, False).start()

    for side in range(2):
        sends.append(corner_copy(side, False, False))
        sends[-1].start()
    for d in (2, 3):
        send(0, d, c_buf.at[d - 2], c_slot, 2)

    @pl.loop(0, 16, unroll=4)
    def _(r):
        for ph in range(6):
            e_ext[r + 3, ph] = row_get(s_ext, r + 3, 7 + ph, 16, 4).astype(BF16)

    wf_in.wait()
    cot_in = load(2, cot_hbm, cot)
    wm_in = load(3, wm_hbm, wm)
    wc_in = load(4, wc_hbm, wc)
    pre[pl.ds(3, 14)] = conv_dot(
        lambda a, b: e_ext[3 + a : 17 + a, b : b + 4].reshape(14 * 64, C), wf
    ).reshape(14, 64, C)

    def fine_gelu(i):
        a, s = gelu_pair(pre[i])
        row_put(act, i, 0, rounded(a))
        row_put(slp, i, 0, s)

    side_e, side_l = jnp.where(north, 1, 0), jnp.where(north, 0, 1)
    sgn_l = jnp.where(north | south, -1, 1)

    def receive(side):
        recv(0, side, hid.at[pl.ds(0, 3)], r_slot.at[side])
        for k in range(2):
            recv(0, 4 + 2 * side + k, k_buf.at[k], k_slot.at[2 * side + k])

    def place(side, first, step, row_order, corner_order):
        for j in range(3):
            row_put(s_ext, first + step * j, 8, r_slot[side, row_order(j)].astype(F32))
        for k in range(2):
            put(tile, 0, k_slot[2 * side + k].astype(F32))
            for c in range(3):
                for j in range(3):
                    at = (first + step * j) * 80 + 8 + (64 if k else -3) + c
                    put(s_ext.ref, at, get(tile, c * 4 + corner_order(j), 1))

    def phases(r, which):
        for ph in which:
            e_ext[r, ph] = row_get(s_ext, r, 7 + ph, 16, 4).astype(BF16)

    def pool_row(m):
        for p, shifted in ((0, sm0), (1, sm1)):
            total = 0.0
            for dr in range(2):
                for dp in range(2):
                    total = total + row_get(act, 2 * m + dr, (2 * p + dp) * 16, 16)
            total = 0.25 * total
            pf[m, 1 + p] = total.astype(BF16)
            row_put(shifted, m, 8, total)

    def pool_edges():
        for first, shifted, at in ((0, sm1, 7), (4, sm0, 24)):
            total = 0.0
            for c in range(2):
                for dr in range(2):
                    total = total + row_get(act_e, first + c, dr, 16, 2)
            col_put(shifted, at, 0, 0.25 * total)

    def pool_shift(m):
        pf[m, 0] = row_get(sm1, m, 7, 16).astype(BF16)
        pf[m, 3] = row_get(sm0, m, 9, 16).astype(BF16)

    def mid_gelu(m):
        a, s = gelu_pair(pre_m[m])
        am[m] = rounded(a)
        row_put(slm, m + 2, 0, s)
        slb[m] = s.astype(BF16)

    for k in range(2):
        recv(0, 2 + k, c_buf.at[k], c_slot.at[k])
    for side, first in ((0, -3), (1, 64)):
        for c in range(3):
            col_put(s_ext, 8 + first + c, 3, c_slot[side, pl.ds(c * 16, 16)].astype(F32))
    for r in (3, 4, 17, 18):
        phases(r, (0, 5))

    @pl.loop(3, 17, unroll=2)
    def _(i):
        fine_gelu(i)

    pole_row = jnp.where(north, 2, 17)
    beyond_row = jnp.where(north, 1, 18)

    @pl.when(pole)
    def _():
        recv(0, side_l, hid.at[pl.ds(0, 1)], r_slot.at[side_l, pl.ds(0, 1)])
        halo = jnp.where(north, 2, 19)
        row_put(s_ext, halo, 8, r_slot[side_l, 0].astype(F32))
        for k in range(2):
            recv(0, 4 + 2 * side_l + k, kp_buf.at[k], kp_slot.at[2 * side_l + k])
            tile[0, pl.ds(0, 16), :] = kp_slot[2 * side_l + k].astype(F32)
            for c in range(3):
                at = halo * 80 + 8 + (64 if k else -3) + c
                for l in range(LANES):
                    s_ext.ref[l, pl.ds(at, 1), :] = tile[0, pl.ds(3 * c + l, 1), :]
        phases(halo, range(6))
        two = jnp.where(north, 2, 16)

        @pl.loop(0, 10, unroll=5)
        def _(i):
            col = 8 - 3 + i + (i // 5) * 60
            for a in range(3):
                l_late[a, i] = get(s_ext.ref, (two + a) * 80 + col, 16, 80).astype(BF16)

        def ring_pole(a, b):
            parts = [e_ext[pole_row + a, b : b + 4].reshape(64, C)]
            parts += [l_late[a, s * 5 + b : s * 5 + b + 3].reshape(48, C) for s in range(2)]
            return jnp.concatenate(parts, axis=0)

        res = conv_dot(ring_pole, wf)
        pre[pole_row] = res[:64]
        fine_gelu(pole_row)
        for i in range(6):
            a, s = gelu_pair(res[64 + 16 * i : 80 + 16 * i])
            a = rounded(a)
            for k in range(2):
                put(act_e.ref, i * act_e.pitch + two + k, a[k : k + 1])
                put(slp_e.ref, i * slp_e.pitch + two + k, s[k : k + 1])
                if i in (2, 3):
                    put(act.ref, (two + k) * act.pitch + (63 if i == 3 else 0), a[k : k + 1])
        m = jnp.where(north, 1, 8)
        pool_row(m)
        pool_edges()
        pool_shift(m)
        put(tile, 0, row_get(sm0, m, 8, 16))
        put(tile, 16, row_get(sm1, m, 8, 16))
        put(tile, 32, row_get(sm1, m, 7, 1))
        put(tile, 33, row_get(sm0, m, 24, 1))
        for side in range(2):
            put(tile, 34 + side, get(slp_e.ref, (1 + 3 * side) * slp_e.pitch + pole_row, 1))
        p2_buf[...] = get(tile, 0, 48).astype(BF16)
        remote(5, 0, p2_buf, p2_slot, 0, far).start()

    cot_in.wait()

    @pl.loop(0, 16, unroll=4)
    def _(r):
        row_put(sx, r, 0, cot[r].astype(F32))
        for p in range(4):
            ctp[r + 1, pl.ds(p * 16, 16)] = row_get(sx, r, p, 16, 4).astype(BF16)

    @pl.loop(0, 8, unroll=4)
    def _(m):
        for p in range(2):
            total = 0.0
            for dr in range(2):
                for dp in range(2):
                    total = total + ctp[2 * m + dr + 1, pl.ds((2 * p + dp) * 16, 16)].astype(F32)
            row_put(gma, m + 2, p * 16, total)

    for q in range(4):
        total = 0.0
        for dr in range(2):
            for p in range(2):
                total = total + row_get(gma, 2 * q + dr + 2, p * 16, 16)
        row_put(gcax, q + 2, 8, total)

    for side, (mid, coarse) in enumerate(((0, 0), (6, 2))):
        for k in range(2):
            lr_buf[side, pl.ds(32 * k, 32)] = row_get(gma, mid + k + 2, 0, 32).astype(BF16)
            lr_buf[side, pl.ds(64 + 16 * k, 16)] = row_get(gcax, coarse + k + 2, 8, 16).astype(BF16)
    for side, (col, mids, coarse) in enumerate(((0, (0, 16), 0), (63, (15, 31), 14))):
        put(tile, 0, col_get(sx, col, 0, 16))
        for c in range(2):
            put(tile, 16 + 8 * c, col_get(gma, mids[c], 2, 8))
            put(tile, 32 + 4 * c, col_get(gcax, 8 + coarse + c, 2, 8)[:4])
        lc_buf[side] = get(tile, 0, 48).astype(BF16)
        for k, (row, mid, low) in enumerate(((0, 2, 2), (15, 8, 4))):
            for c in range(2):
                put(tile, 2 * c, col_get(gma, mids[c], mid, 8)[:2])
                put(tile, 4 + 2 * c, col_get(gcax, 8 + coarse + c, low, 8)[:2])
            put(tile, 8, get(sx.ref, row * 64 + col, 1))
            lk_buf[2 * k + side] = get(tile, 0, 16).astype(BF16)

    for d in (0, 1):
        send(1, d, lr_buf.at[d], lr_slot, 0)
    for d in (2, 3):
        send(1, d, lc_buf.at[d - 2], lc_slot, 2)
    for d in (4, 5, 6, 7):
        send(1, d, lk_buf.at[d - 4], lk_slot, 4)


    receive(side_e)
    place(
        side_e, jnp.where(north, 19, 2), jnp.where(north, 1, -1),
        lambda j: jnp.where(north, j, 2 - j), lambda j: jnp.where(north, j, 3 - j),
    )
    for i in range(3):
        phases(jnp.where(north, 19, 0) + i, range(6))

    @pl.loop(0, 10, unroll=5)
    def _(i):
        col = 8 - 3 + i + (i // 5) * 60
        for a in range(3):
            l_edge[a, i] = get(s_ext.ref, a * 80 + col, 32, 80).astype(BF16)

    def ring(a, b):
        parts = [e_ext[jnp.where(north, 20 - q, 1 + q) + a - 1, b : b + 4].reshape(64, C) for q in range(3)]
        parts += [l_edge[a, s * 5 + b : s * 5 + b + 3].reshape(96, C) for s in range(2)]
        return jnp.concatenate(parts, axis=0)

    res = conv_dot(ring, wf)
    for q in range(3):
        pre[jnp.where(north, 19 - q, q)] = res[q * 64 : (q + 1) * 64]
    pre_e[...] = res[192:].reshape(6, 32, C)

    @pl.loop(0, 6, unroll=2)
    def _(i):
        a, s = gelu_pair(pre_e[i])
        row_put(act_e, i, 0, rounded(a))
        row_put(slp_e, i, 0, s)

    for dst, src in ((act, act_e), (slp, slp_e)):
        col_put(dst, 0, 0, row_get(src, 2, 0, 24))
        col_put(dst, 63, 0, row_get(src, 3, 0, 24))

    @pl.loop(0, 3, unroll=3)
    def _(q):
        fine_gelu(jnp.where(north, 17, 0) + q)

    wm_in.wait()

    @pl.loop(0, 8, unroll=4)
    def _(i):
        pool_row(jnp.where(north, 2, 0) + i)

    pool_edges()

    @pl.loop(0, 8, unroll=8)
    def _(i):
        pool_shift(jnp.where(north, 2, 0) + i)

    early = jnp.where(north, 2, 0)
    pre_m[pl.ds(early, 6)] = conv_dot(
        lambda a, b: pf[pl.ds(early + a, 6), b : b + 2].reshape(192, C), wm
    ).reshape(6, 32, C)

    @pl.loop(0, 6, unroll=2)
    def _(i):
        mid_gelu(early + i)

    @pl.when(jnp.logical_not(pole))
    def _():
        receive(side_l)
        place(
            side_l, jnp.where(north, 2, 19), jnp.where(north, -1, 1),
            lambda j: jnp.where(south, 2 - j, j), lambda j: jnp.where(south, 3 - j, j),
        )
        for i in range(3):
            phases(jnp.where(north, 0, 19) + i, range(6))
        edge_first = jnp.where(north, 0, 17)
        edge_rows = lax.broadcasted_iota(jnp.int32, (16, 1), 0)
        flip = (north & (edge_rows < 2)) | (south & ((edge_rows == 1) | (edge_rows == 2)))

        @pl.loop(0, 10, unroll=5)
        def _(i):
            col = 8 - 3 + i + (i // 5) * 60
            low, mid, high = (get(s_ext.ref, (edge_first + a) * 80 + col, 16, 80) for a in range(3))
            l_late[0, i] = jnp.where(flip, high, low).astype(BF16)
            l_late[1, i] = mid.astype(BF16)
            l_late[2, i] = jnp.where(flip, low, high).astype(BF16)

        def ring_late(a, b):
            rows = [jnp.where(north, 1 + q, 20 - q) + (1 if q == 2 else sgn_l) * (a - 1) for q in range(3)]
            parts = [e_ext[r, b : b + 4].reshape(64, C) for r in rows]
            parts += [l_late[a, s * 5 + b : s * 5 + b + 3].reshape(48, C) for s in range(2)]
            return jnp.concatenate(parts, axis=0)

        res = conv_dot(ring_late, wf)
        for q in range(3):
            pre[jnp.where(north, q, 19 - q)] = res[q * 64 : (q + 1) * 64]
        for i in range(6):
            a, s = gelu_pair(res[192 + 16 * i : 208 + 16 * i])
            a = rounded(a)
            for k in range(3):
                put(act_e.ref, i * act_e.pitch + edge_first + k, a[k : k + 1])
                put(slp_e.ref, i * slp_e.pitch + edge_first + k, s[k : k + 1])

        @pl.loop(0, 3, unroll=3)
        def _(q):
            fine_gelu(jnp.where(north, 0, 17) + q)

        for i in range(2):
            pool_row(jnp.where(north, 0, 8) + i)
        pool_edges()
        for i in range(2):
            pool_shift(jnp.where(north, 0, 8) + i)

    @pl.when(pole)
    def _():
        recv(5, 0, p2_buf, p2_slot)
        m = jnp.where(north, 0, 9)
        put(tile, 0, p2_slot[...].astype(F32))
        for p, shifted in ((0, sm0), (1, sm1)):
            pf[m, 1 + p] = p2_slot[pl.ds(16 * p, 16)]
            row_put(shifted, m, 8, get(tile, 16 * p, 16))
        put(sm1.ref, m * sm1.pitch + 7, get(tile, 32, 1))
        put(sm0.ref, m * sm0.pitch + 24, get(tile, 33, 1))
        pool_shift(m)
        for side in range(2):
            put(slp_e.ref, (1 + 3 * side) * slp_e.pitch + beyond_row, get(tile, 34 + side, 1))

    late = jnp.where(north, 0, 6)
    pre_m[pl.ds(late, 2)] = conv_dot(
        lambda a, b: pf[pl.ds(late + a, 2), b : b + 2].reshape(64, C), wm
    ).reshape(2, 32, C)
    for i in range(2):
        mid_gelu(late + i)

    for q in range(4):
        total = 0.0
        for dr in range(2):
            for p in range(2):
                total = total + am[2 * q + dr, pl.ds(p * 16, 16)]
        total = 0.25 * total
        pml[q] = total.astype(BF16)
        row_put(sc, q + 3, 16, total)
    for side, (first, mids) in enumerate(((0, (0, 16)), (13, (15, 31)))):
        for c in range(3):
            put(tile, c * 4, col_get(sc, 16 + first + c, 3, 8)[:4])
        for c in range(2):
            put(tile, 16 + 8 * c, col_get(slm, mids[c], 2, 8))
        pc_buf[side] = get(tile, 0, 32).astype(BF16)
        for k, row in enumerate((2, 8)):
            for c in range(2):
                put(tile, 12 + 2 * c, col_get(slm, mids[c], row, 8)[:2])
            pk_buf[2 * k + side] = get(tile, 0, 16).astype(BF16)

    far_d, near_d = jnp.where(north, 0, 1), jnp.where(north, 1, 0)
    for d, first, to, target in ((0, far_d, far_slot, far), (1, near_d, near_slot, near)):
        copy = remote(2, d, pml.at[pl.ds(first, 3)], pr_slot.at[to], to, target)
        copy.start()
        sends.append(copy)
    for d in (4, 5, 6, 7):
        send(2, d, pk_buf.at[d - 4], pk_slot, 4)
    for d in (2, 3):
        send(2, d, pc_buf.at[d - 2], pc_slot, 2)
    for d in (0, 1):
        send(3, d, slb.at[pl.ds(6 * d, 2)], sr_slot, 0)
    for d in (0, 1):
        send(4, d, ctp.at[1 + 15 * d], ct_slot, 0)
    @pl.when(pole)
    def _():
        sl_buf[...] = row_get(slp, pole_row, 0, 64).astype(BF16)
        remote(6, 0, sl_buf, sl_slot, 0, far).start()


    @pl.loop(0, 16, unroll=4)
    def _(r):
        for p in range(4):
            v = row_get(act, r + 2, p * 16, 16) + am[r // 2, pl.ds((p // 2) * 16, 16)]
            row_put(ns, r, p, v, 4)

    for k in range(2):
        recv(1, k, lr_buf.at[k], lr_slot.at[k])
    for k in range(2):
        recv(1, 2 + k, lc_buf.at[0], lc_slot.at[k])
        put(ts, k * 48, lc_slot[k].astype(F32))
    for k in range(4):
        recv(1, 4 + k, lk_buf.at[0], lk_slot.at[k])
        put(tk, k * 16, lk_slot[k].astype(F32))

    def pick(k, at):
        return get(ts, k * 48 + at, 1)

    def corner(k, at):
        return get(tk, k * 16 + at, 1)

    def edge_columns(dst, base, corner_base):
        for side in range(2):
            for c in range(2):
                to = side * 2 + c
                row_put(dst, to, 2, get(ts, side * 48 + base + 8 * c, 8))
                for j in range(2):
                    at = corner_base + 2 * c
                    row_put(dst, to, 1 - j, corner(side, at + jnp.where(north, j, 1 - j)))
                    row_put(dst, to, 10 + j, corner(2 + side, at + jnp.where(south, 1 - j, j)))

    for j in range(2):
        at_n, at_s = jnp.where(north, j, 1 - j), jnp.where(south, 1 - j, j)
        row_put(gma, 1 - j, 0, lr_slot[0, pl.ds(pl.multiple_of(32 * at_n, 32), 32)].astype(F32))
        row_put(gma, 10 + j, 0, lr_slot[1, pl.ds(pl.multiple_of(32 * at_s, 32), 32)].astype(F32))
        row_put(gcax, 1 - j, 8, lr_slot[0, pl.ds(pl.multiple_of(64 + 16 * at_n, 16), 16)].astype(F32))
        row_put(gcax, 6 + j, 8, lr_slot[1, pl.ds(pl.multiple_of(64 + 16 * at_s, 16), 16)].astype(F32))
    for side in range(2):
        row_put(cte, side, 2, get(ts, side * 48, 16))
        row_put(cte, side, 1, corner(side, 8))
        row_put(cte, side, 18, corner(2 + side, 8))
        for c in range(2):
            col = 8 + (16 if side else -2) + c
            for q in range(4):
                row_put(gcax, q + 2, col, pick(side, 32 + 4 * c + q))
            for j in range(2):
                row_put(gcax, 1 - j, col, corner(side, 4 + 2 * c + jnp.where(north, j, 1 - j)))
                row_put(gcax, 6 + j, col, corner(2 + side, 4 + 2 * c + jnp.where(south, 1 - j, j)))
    edge_columns(gmae, 16, 0)

    wc_in.wait()
    for k in range(2):
        recv(2, k, pml.at[pl.ds(0, 3)], pr_slot.at[k])
    for k in range(2):
        recv(2, 2 + k, pc_buf.at[0], pc_slot.at[k])
        put(ts, k * 48, pc_slot[k].astype(F32))
    for k in range(4):
        recv(2, 4 + k, pk_buf.at[0], pk_slot.at[k])
        put(tk, k * 16, pk_slot[k].astype(F32))
    for j in range(3):
        row_put(sc, 2 - j, 16, pr_slot[0, jnp.where(north, j, 2 - j)].astype(F32))
        row_put(sc, 7 + j, 16, pr_slot[1, jnp.where(south, 2 - j, j)].astype(F32))
    for side in range(2):
        for c in range(3):
            col = 16 + (16 if side else -3) + c
            for q in range(4):
                row_put(sc, q + 3, col, pick(side, 4 * c + q))
            for j in range(3):
                row_put(sc, 2 - j, col, corner(side, 4 * c + jnp.where(north, j, 3 - j)))
                row_put(sc, 7 + j, col, corner(2 + side, 4 * c + jnp.where(south, 3 - j, j)))

    @pl.loop(0, 10, unroll=True)
    def _(r):
        for b in range(3):
            cb[b, r] = row_get(sc, r, 7 + b, 32).astype(BF16)

    def coarse(a, b):
        rows = [1 + sgn_n * (a - 1), 2 + sgn_n * (a - 1)]
        tail = [7 + sgn_s * (a - 1), 8 + sgn_s * (a - 1)]
        parts = [cb[b, r] for r in rows] + [cb[b, 2 + a : 6 + a].reshape(128, C)]
        return jnp.concatenate(parts + [cb[b, r] for r in tail], axis=0)

    res = conv_dot(coarse, wc)
    for i in range(8):
        a, s = gelu_pair(res[i * 32 : (i + 1) * 32])
        if 2 <= i < 6:
            ac[i - 2] = rounded(a[8:24])
        row_put(gs, i, 8, row_get(gcax, i, 0, 32) * s)

    @pl.loop(0, 8, unroll=True)
    def _(r):
        for d in range(3):
            gb[d, r] = row_get(gs, r, 7 + d, 32).astype(BF16)

    for d in range(3):
        for k, (x, y) in enumerate(((0, 2), (1, 3), (4, 6), (5, 7))):
            gb[d, 8 + k] = (gb[d, x].astype(F32) + gb[d, y].astype(F32)).astype(BF16)
        gb[d, 12] = jnp.zeros((32, C), BF16)

    def coarse_t(a, b):
        d = 2 - b
        if a == 1:
            return gb[d, 1:7].reshape(192, C)
        if a == 0:
            rows = [jnp.where(north, 8, 2), jnp.where(north, 9, 3), 4, 5, jnp.where(south, 12, 6), jnp.where(south, 12, 7)]
        else:
            rows = [jnp.where(north, 12, 0), jnp.where(north, 12, 1), 2, 3, jnp.where(south, 10, 4), jnp.where(south, 11, 5)]
        return jnp.concatenate([gb[d, r] for r in rows], axis=0)

    res = conv_dot_t(coarse_t, wc)
    for i in range(6):
        row_put(bm, i, 0, 0.25 * res[i * 32 : (i + 1) * 32])

    for k in range(2):
        recv(3, k, slb.at[pl.ds(0, 2)], sr_slot.at[k])
    for j in range(2):
        row_put(slm, 1 - j, 0, sr_slot[0, jnp.where(north, j, 1 - j)].astype(F32))
        row_put(slm, 10 + j, 0, sr_slot[1, jnp.where(south, 1 - j, j)].astype(F32))
    edge_columns(sle, 16, 12)

    @pl.loop(0, 12, unroll=True)
    def _(k):
        below = row_get(bm, k // 2, 8, 16)
        for p, shifted in ((0, ms0), (1, ms1)):
            g = (row_get(gma, k, p * 16, 16) + below) * row_get(slm, k, p * 16, 16)
            mg[k, 1 + p] = g.astype(BF16)
            row_put(shifted, k, 8, g)

    for side in range(2):
        below = col_get(bm, 24 if side else 7, 0, 8)
        put(tile, 0, below, 2)
        put(tile, 1, below, 2)
        below = get(tile, 0, 16)
        for c in range(2):
            g = (row_get(gmae, side * 2 + c, 0, 16) + below) * row_get(sle, side * 2 + c, 0, 16)
            row_put(mc, side * 3 + (c + 1 if side else c), 0, g)
            if side == 0 and c == 1:
                col_put(ms1, 7, 0, g)
            if side == 1 and c == 0:
                col_put(ms0, 24, 0, g)
    row_put(mc, 2, 0, col_get(ms0, 8, 0, 16))
    row_put(mc, 3, 0, col_get(ms1, 23, 0, 16))

    @pl.loop(0, 12, unroll=True)
    def _(k):
        mg[k, 0] = row_get(ms1, k, 7, 16).astype(BF16)
        mg[k, 3] = row_get(ms0, k, 9, 16).astype(BF16)

    for k, (x, y) in enumerate(((0, 2), (1, 3), (8, 10), (9, 11))):
        mg[12 + k] = (mg[x].astype(F32) + mg[y].astype(F32)).astype(BF16)
    mg[16] = jnp.zeros((4, 16, C), BF16)

    half_rows = lax.broadcasted_iota(jnp.int32, (16, 1), 0)
    at_north = north & (half_rows < 2)
    at_south = south & ((half_rows == 8) | (half_rows == 9))
    for i in range(6):
        low, mid, high = (rounded(row_get(mc, i, e, 16)) for e in range(3))
        both = low + high
        ml[0, i] = jnp.where(at_north, both, jnp.where(at_south, 0.0, high)).astype(BF16)
        ml[1, i] = mid.astype(BF16)
        ml[2, i] = jnp.where(at_south, both, jnp.where(at_north, 0.0, low)).astype(BF16)

    def mid_t(a, b):
        ph = slice(2 - b, 4 - b)
        if a == 1:
            parts = [mg[1:11, ph].reshape(320, C)]
        else:
            if a == 0:
                top = [jnp.where(north, 12, 2), jnp.where(north, 13, 3)]
                body, tail = 4, [jnp.where(south, 16, 10), jnp.where(south, 16, 11)]
            else:
                top = [jnp.where(north, 16, 0), jnp.where(north, 16, 1)]
                body, tail = 2, [jnp.where(south, 14, 8), jnp.where(south, 15, 9)]
            parts = [mg[r, ph].reshape(32, C) for r in top]
            parts += [mg[body : body + 6, ph].reshape(192, C)]
            parts += [mg[r, ph].reshape(32, C) for r in tail]
        return jnp.concatenate(parts + [ml[a, 2 - b], ml[a, 5 - b]], axis=0)

    res = 0.25 * conv_dot_t(mid_t, wm)
    bfm[...] = res[:320].reshape(10, 32, C)
    for side in range(2):
        row_put(bfe, side, 0, res[320 + 16 * side : 336 + 16 * side])

    for k in range(2):
        recv(4, k, ctp.at[1], ct_slot.at[k])
        ctp[17 * k] = ct_slot[k]

    @pl.when(pole)
    def _():
        recv(6, 0, sl_buf, sl_slot)
        row_put(slp, beyond_row, 0, sl_slot[...].astype(F32))

    @pl.loop(0, 18, unroll=6)
    def _(k):
        for p in range(4):
            g = (
                ctp[k, pl.ds(p * 16, 16)].astype(F32) + bfm[(k + 1) // 2, pl.ds((p // 2) * 16, 16)]
            ) * row_get(slp, k + 1, p * 16, 16)
            g_ext[k, 1 + p] = g.astype(BF16)
            if p == 0:
                row_put(fs0, k, 8, g)
            if p == 3:
                row_put(fs3, k, 8, g)

    for side, (shifted, at) in enumerate(((fs3, 7), (fs0, 24))):
        below = row_get(bfe, side, 0, 16)
        put(tile, 0, below, 2)
        put(tile, 1, below, 2)
        g = (row_get(cte, side, 0, 32) + get(tile, 0, 32)) * row_get(slp_e, 1 + 3 * side, 0, 32)
        row_put(ge, side, 0, g)
        col_put(shifted, at, 0, row_get(ge, side, 1, 24))

    @pl.loop(0, 18, unroll=True)
    def _(k):
        g_ext[k, 0] = row_get(fs3, k, 7, 16).astype(BF16)
        g_ext[k, 5] = row_get(fs0, k, 9, 16).astype(BF16)

    for k, (x, y) in enumerate(((0, 2), (15, 17))):
        g_ext[18 + k] = (g_ext[x].astype(F32) + g_ext[y].astype(F32)).astype(BF16)
    g_ext[20] = jnp.zeros((6, 16, C), BF16)

    for copy in sends:
        copy.wait_send()

    @pl.when(pole)
    def _():
        far_rows(1).wait_send()
        for side in range(2):
            corner_copy(side, True, True).wait_send()
        remote(5, 0, p2_buf, p2_slot, 0, far).wait_send()
        remote(6, 0, sl_buf, sl_slot, 0, far).wait_send()

    @pl.when(jnp.logical_not(pole))
    def _():
        far_rows(3).wait_send()
        for side in range(2):
            corner_copy(side, True, False).wait_send()


def last_kernel(nlat, ns, ac, g_ext, wf, out_hbm, grad_hbm, out_v, grad_v, sx, acx, sem):
    lat = lax.axis_index("lat")
    north = lat == 0
    south = lat == nlat - 1
    sx, ns, acx = Rows(sx, 64), Rows(ns, 64), Rows(acx, 64)
    copies = []
    for h in range(2):

        def fine_t(a, b):
            ph = slice(2 - b, 6 - b)
            if a == 1:
                return g_ext[8 * h + 1 : 8 * h + 9, ph].reshape(512, C)
            first = 8 * h + 2 - a
            if h == 0:
                row = jnp.where(north, 20 if a else 18, first)
                parts = [g_ext[row, ph].reshape(64, C), g_ext[first + 1 : first + 8, ph].reshape(448, C)]
            else:
                row = jnp.where(south, 19 if a else 20, first + 7)
                parts = [g_ext[first : first + 7, ph].reshape(448, C), g_ext[row, ph].reshape(64, C)]
            return jnp.concatenate(parts, axis=0)

        res = conv_dot_t(fine_t, wf)
        if h == 0:
            for q in range(4):
                for p in range(4):
                    row_put(acx, q, p, ac[q], 4)
            for r in range(16):
                out_v[r] = (row_get(ns, r, 0, 64) + row_get(acx, r // 4, 0, 64)).astype(BF16)
            copies.append(pltpu.make_async_copy(out_v, out_hbm, sem.at[2]))
            copies[-1].start()
        for r in range(8):
            for p in range(4):
                row_put(sx, 8 * h + r, p, res[r * 64 + p * 16 : r * 64 + p * 16 + 16], 4)
            grad_v[8 * h + r] = row_get(sx, 8 * h + r, 0, 64).astype(BF16)
        half = pl.ds(8 * h, 8)
        copies.append(pltpu.make_async_copy(grad_v.at[half], grad_hbm.at[half], sem.at[h]))
        copies[-1].start()
    for copy in copies:
        copy.wait()


def body(nlat, nlon, hidden_in, cotangent, weight_fine, weight_mid, weight_coarse):
    hbm = pl.BlockSpec(memory_space=pltpu.HBM)
    field = (16, 64, C)
    weight = (3, 3, C, C)

    def v(*shape, dtype=BF16):
        return pltpu.VMEM(shape, dtype)

    def f(*shape):
        return pltpu.VMEM(shape, F32)

    scratch = dict(
        hid=v(*field), cot=v(*field), wm=v(*weight), wc=v(*weight),
        s_ext=f(3, 36 * 80, 128), e_ext=v(22, 6, 16, C), l_edge=v(3, 10, 32, C), l_late=v(3, 10, 16, C), pre=f(24, 64, C), pre_e=f(6, 32, C),
        act=f(3, 24 * 64, 128), slp=f(3, 24 * 64, 128), act_e=f(3, 6 * 40, 128), slp_e=f(3, 6 * 32, 128),
        sx=f(3, 16 * 64, 128), ctp=v(18, 64, C), cte=f(3, 2 * 32, 128), gma=f(3, 16 * 32, 128), gmae=f(3, 4 * 16, 128),
        gcax=f(3, 16 * 32, 128),
        pf=v(10, 4, 16, C), sm0=f(3, 16 * 32, 128), sm1=f(3, 16 * 32, 128), pre_m=f(8, 32, C), am=f(8, 32, C),
        slm=f(3, 16 * 32, 128), sle=f(3, 4 * 16, 128), slb=v(8, 32, C), pml=v(4, 16, C), sc=f(3, 12 * 48, 128),
        cb=v(3, 10, 32, C), gs=f(3, 8 * 48, 128), gb=v(3, 13, 32, C), bm=f(3, 8 * 32, 128),
        mg=v(17, 4, 16, C), ms0=f(3, 16 * 32, 128), ms1=f(3, 16 * 32, 128), mc=f(3, 6 * 24, 128), ml=v(3, 6, 16, C),
        bfm=f(10, 32, C), bfe=f(3, 2 * 16, 128), fs0=f(3, 24 * 32, 128), fs3=f(3, 24 * 32, 128),
        ge=f(3, 2 * 32, 128), tile=f(3, 48, 128), ts=f(3, 96, 128), tk=f(3, 64, 128),
        c_buf=v(2, 48, C), k_buf=v(4, 16, C), r_slot=v(2, 3, 64, C), c_slot=v(2, 48, C), k_slot=v(4, 16, C),
        kp_buf=v(2, 16, 128), kp_slot=v(4, 16, 128),
        lr_buf=v(2, 96, C), lc_buf=v(2, 48, C), lk_buf=v(4, 16, C),
        lr_slot=v(2, 96, C), lc_slot=v(2, 48, C), lk_slot=v(4, 16, C),
        pc_buf=v(2, 32, C), pk_buf=v(4, 16, C),
        p2_buf=v(48, C), p2_slot=v(48, C), sl_buf=v(64, C), sl_slot=v(64, C),
        pr_slot=v(2, 3, 16, C), sr_slot=v(2, 2, 32, C), ct_slot=v(2, 64, C), pc_slot=v(2, 32, C), pk_slot=v(4, 16, C),
        lsem=pltpu.SemaphoreType.DMA((8,)), ssem=pltpu.SemaphoreType.DMA((7, 8)), rsem=pltpu.SemaphoreType.DMA((7, 8)),
    )
    vmem = pl.BlockSpec(memory_space=pltpu.VMEM)
    results = pl.pallas_call(
        functools.partial(kernel, nlat, nlon),
        out_shape=(f(3, 16 * 64, 128), f(4, 16, C), v(21, 6, 16, C), v(*weight)),
        in_specs=[hbm] * 5,
        out_specs=(vmem,) * 4,
        scratch_shapes=list(scratch.values()),
        compiler_params=pltpu.CompilerParams(
            collective_id=0, has_side_effects=True, vmem_limit_bytes=52 * 2**20
        ),
    )(hidden_in, cotangent, weight_fine, weight_mid, weight_coarse)
    shape = jax.ShapeDtypeStruct(field, BF16)
    return pl.pallas_call(
        functools.partial(last_kernel, nlat),
        out_shape=(shape, shape),
        in_specs=[vmem] * 4,
        out_specs=(hbm, hbm),
        scratch_shapes=[v(*field), v(*field), f(3, 16 * 64, 128), f(3, 4 * 64, 128), pltpu.SemaphoreType.DMA((3,))],
        compiler_params=pltpu.CompilerParams(vmem_limit_bytes=36 * 2**20),
    )(*results)


def solution(mesh):
    field = P("lat", "lon", None)
    return jax.shard_map(
        functools.partial(body, mesh.shape["lat"], mesh.shape["lon"]),
        mesh=mesh,
        in_specs=(field, field, P(), P(), P()),
        out_specs=(field, field),
        check_vma=False,
    )
```

```python
import functools

import jax
import jax.numpy as jnp
from jax import lax
from jax.experimental import pallas as pl
from jax.experimental.pallas import tpu as pltpu
from jax.sharding import PartitionSpec as P

MESH = pl.DeviceIdType.MESH
F32 = jnp.float32
BF16 = jnp.bfloat16
C = 384
LANES = 3


def get(ref, start, n, stride=1):
    ds = pl.ds(start, n) if stride == 1 else pl.ds(start, n, stride=stride)
    return jnp.concatenate([ref[l, ds, :] for l in range(LANES)], axis=-1)


def put(ref, start, val, stride=1):
    n = val.shape[0]
    ds = pl.ds(start, n) if stride == 1 else pl.ds(start, n, stride=stride)
    for l in range(LANES):
        ref[l, ds, :] = val[:, l * 128 : (l + 1) * 128]


class Rows:
    def __init__(self, ref, pitch):
        self.ref, self.pitch = ref, pitch


def at_row(grid, r, start):
    if isinstance(r, int):
        return r * grid.pitch + start
    if start % 8 == 0 and grid.pitch % 8 == 0:
        return pl.multiple_of(r * grid.pitch + start, 8)
    return r * grid.pitch + start


def row_get(grid, r, start, n, stride=1):
    return get(grid.ref, at_row(grid, r, start), n, stride)


def row_put(grid, r, start, val, stride=1):
    put(grid.ref, at_row(grid, r, start), val, stride)


def col_get(grid, c, r0, n):
    return get(grid.ref, r0 * grid.pitch + c, n, grid.pitch)


def col_put(grid, c, r0, val):
    put(grid.ref, r0 * grid.pitch + c, val, grid.pitch)


def gelu_pair(z):
    e = jnp.exp(-0.5 * z * z)
    t = 1.0 / (1.0 + (0.3275911 * 0.7071067811865476) * jnp.abs(z))
    q = t * (
        0.127414796
        + t * (-0.142248368 + t * (0.7107068705 + t * (-0.7265760135 + t * 0.5307027145)))
    )
    h = q * e
    cdf = jnp.where(z >= 0, 1.0 - h, h)
    return z * cdf, cdf + z * (e * 0.3989422804014327)


def rounded(x):
    return x.astype(BF16).astype(F32)


def conv_dot(parts, weight):
    lhs = jnp.concatenate([parts(a, b) for a in range(3) for b in range(3)], axis=-1)
    return jnp.dot(lhs, weight[...].reshape(9 * C, C), preferred_element_type=F32)


def conv_dot_t(parts, weight):
    lhs = jnp.concatenate([parts(a, b) for a in range(3) for b in range(3)], axis=-1)
    rhs = jnp.concatenate([weight[a, b] for a in range(3) for b in range(3)], axis=-1)
    return lax.dot_general(lhs, rhs, (((1,), (1,)), ((), ())), preferred_element_type=F32)


def kernel(
    nlat, nlon,
    hid_hbm, cot_hbm, wf_hbm, wm_hbm, wc_hbm, ns, ac, g_ext, wf,
    hid, cot, wm, wc,
    s_ext, e_ext, l_edge, l_late, pre, pre_e, act, slp, act_e, slp_e,
    sx, ctp, cte, gma, gmae, gcax,
    pf, sm0, sm1, pre_m, am, slm, sle, slb, pml, sc, cb, gs, gb, bm,
    mg, ms0, ms1, mc, ml, bfm, bfe, fs0, fs3, ge, tile, ts, tk,
    c_buf, k_buf, r_slot, c_slot, k_slot, kp_buf, kp_slot,
    lr_buf, lc_buf, lk_buf, lr_slot, lc_slot, lk_slot,
    pc_buf, pk_buf, p2_buf, p2_slot, sl_buf, sl_slot, pr_slot, sr_slot, ct_slot, pc_slot, pk_slot,
    lsem, ssem, rsem,
):
    s_ext = Rows(s_ext, 80)
    act = Rows(act, 64)
    slp = Rows(slp, 64)
    act_e = Rows(act_e, 40)
    slp_e = Rows(slp_e, 32)
    sx = Rows(sx, 64)
    cte = Rows(cte, 32)
    gma = Rows(gma, 32)
    gmae = Rows(gmae, 16)
    gcax = Rows(gcax, 32)
    sm0 = Rows(sm0, 32)
    sm1 = Rows(sm1, 32)
    slm = Rows(slm, 32)
    sle = Rows(sle, 16)
    sc = Rows(sc, 48)
    gs = Rows(gs, 48)
    bm = Rows(bm, 32)
    ms0 = Rows(ms0, 32)
    ms1 = Rows(ms1, 32)
    mc = Rows(mc, 24)
    bfe = Rows(bfe, 16)
    fs0 = Rows(fs0, 32)
    fs3 = Rows(fs3, 32)
    ge = Rows(ge, 32)
    ns = Rows(ns, 64)
    lat = lax.axis_index("lat")
    lon = lax.axis_index("lon")
    north = lat == 0
    south = lat == nlat - 1
    sgn_n = jnp.where(north, -1, 1)
    sgn_s = jnp.where(south, -1, 1)

    def device(dlat, dlon):
        to_lat, to_lon = lat, lon + dlon + nlon
        if dlat:
            pole = north if dlat < 0 else south
            to_lat = jnp.where(pole, lat, lat + dlat)
            to_lon = to_lon + jnp.where(pole, nlon // 2, 0)
        return {"lat": to_lat, "lon": lax.rem(to_lon, nlon)}

    there = [device(*d) for d in ((-1, 0), (1, 0), (0, -1), (0, 1), (-1, -1), (-1, 1), (1, -1), (1, 1))]
    slot = [
        jnp.where(north, 0, 1), jnp.where(south, 1, 0), 3, 2,
        jnp.where(north, 5, 7), jnp.where(north, 4, 6),
        jnp.where(south, 7, 5), jnp.where(south, 6, 4),
    ]

    def remote(kind, d, src, dst, where, target):
        return pltpu.make_async_remote_copy(
            src_ref=src, dst_ref=dst, send_sem=ssem.at[kind, d], recv_sem=rsem.at[kind, where],
            device_id=target, device_id_type=MESH,
        )

    def load(i, src, dst):
        copy = pltpu.make_async_copy(src, dst, lsem.at[i])
        copy.start()
        return copy

    barrier = pltpu.get_barrier_semaphore()
    for t in there:
        pl.semaphore_signal(barrier, inc=1, device_id=t, device_id_type=MESH)

    hid_in = load(0, hid_hbm, hid)
    wf_in = load(1, wf_hbm, wf)
    sends = []

    def send(kind, d, src, slots, base):
        copy = remote(kind, d, src, slots.at[slot[d] - base], slot[d], there[d])
        copy.start()
        sends.append(copy)

    def recv(kind, where, src, dst):
        remote(kind, 0, src, dst, where, there[0]).wait_recv()

    pl.semaphore_wait(barrier, 8)
    pole = north | south
    far = {k: jnp.where(north, there[0][k], there[1][k]) for k in ("lat", "lon")}
    near = {k: jnp.where(north, there[1][k], there[0][k]) for k in ("lat", "lon")}
    far_slot, near_slot = jnp.where(north, slot[0], slot[1]), jnp.where(north, slot[1], slot[0])

    def far_rows(n):
        src = hid_hbm.at[pl.ds(jnp.where(north, 0, 16 - n), n)]
        return remote(0, 0, src, r_slot.at[far_slot, pl.ds(0, n)], far_slot, far)

    @pl.when(pole)
    def _():
        far_rows(1).start()

    @pl.when(jnp.logical_not(pole))
    def _():
        far_rows(3).start()

    copy = remote(0, 1, hid_hbm.at[pl.ds(jnp.where(north, 13, 0), 3)], r_slot.at[near_slot], near_slot, near)
    copy.start()
    sends.append(copy)
    hid_in.wait()

    @pl.loop(0, 16, unroll=4)
    def _(r):
        row_put(s_ext, r + 3, 8, hid[r].astype(F32))

    for side, first in ((0, 0), (1, 61)):
        for c in range(3):
            c_buf[side, pl.ds(c * 16, 16)] = col_get(s_ext, 8 + first + c, 3, 16).astype(BF16)
    for k, (row, first) in enumerate(((0, 0), (0, 61), (12, 0), (12, 61))):
        for c in range(3):
            put(tile, c * 4, col_get(s_ext, 8 + first + c, 3 + row, 8)[:4])
        k_buf[k] = get(tile, 0, 16).astype(BF16)

    for side, first in ((0, 0), (1, 61)):
        at = (3 + jnp.where(north, 0, 15)) * 80 + 8 + first
        for c in range(3):
            for l in range(LANES):
                tile[0, pl.ds(3 * c + l, 1), :] = s_ext.ref[l, pl.ds(at + c, 1), :]
        kp_buf[side] = tile[0, pl.ds(0, 16), :].astype(BF16)

    def corner_copy(side, at_far, small):
        top = north if at_far else jnp.logical_not(north)
        target = {k: jnp.where(top, there[4 + side][k], there[6 + side][k]) for k in ("lat", "lon")}
        to = jnp.where(top, slot[4 + side], slot[6 + side])
        if small:
            return remote(0, 4 + side, kp_buf.at[side], kp_slot.at[to - 4], to, target)
        src = k_buf.at[side + jnp.where(top, 0, 2)]
        return remote(0, (4 if at_far else 6) + side, src, k_slot.at[to - 4], to, target)

    @pl.when(pole)
    def _():
        for side in range(2):
            corner_copy(side, True, True).start()

    @pl.when(jnp.logical_not(pole))
    def _():
        for side in range(2):
            corner_copy(side, True, False).start()

    for side in range(2):
        sends.append(corner_copy(side, False, False))
        sends[-1].start()
    for d in (2, 3):
        send(0, d, c_buf.at[d - 2], c_slot, 2)

    @pl.loop(0, 16, unroll=4)
    def _(r):
        for ph in range(6):
            e_ext[r + 3, ph] = row_get(s_ext, r + 3, 7 + ph, 16, 4).astype(BF16)

    wf_in.wait()
    cot_in = load(2, cot_hbm, cot)
    wm_in = load(3, wm_hbm, wm)
    wc_in = load(4, wc_hbm, wc)
    pre[pl.ds(3, 14)] = conv_dot(
        lambda a, b: e_ext[3 + a : 17 + a, b : b + 4].reshape(14 * 64, C), wf
    ).reshape(14, 64, C)

    def fine_gelu(i):
        a, s = gelu_pair(pre[i])
        row_put(act, i, 0, rounded(a))
        row_put(slp, i, 0, s)

    side_e, side_l = jnp.where(north, 1, 0), jnp.where(north, 0, 1)
    sgn_l = jnp.where(north | south, -1, 1)

    def receive(side):
        recv(0, side, hid.at[pl.ds(0, 3)], r_slot.at[side])
        for k in range(2):
            recv(0, 4 + 2 * side + k, k_buf.at[k], k_slot.at[2 * side + k])

    def place(side, first, step, row_order, corner_order):
        for j in range(3):
            row_put(s_ext, first + step * j, 8, r_slot[side, row_order(j)].astype(F32))
        for k in range(2):
            put(tile, 0, k_slot[2 * side + k].astype(F32))
            for c in range(3):
                for j in range(3):
                    at = (first + step * j) * 80 + 8 + (64 if k else -3) + c
                    put(s_ext.ref, at, get(tile, c * 4 + corner_order(j), 1))

    def phases(r, which):
        for ph in which:
            e_ext[r, ph] = row_get(s_ext, r, 7 + ph, 16, 4).astype(BF16)

    def pool_row(m):
        for p, shifted in ((0, sm0), (1, sm1)):
            total = 0.0
            for dr in range(2):
                for dp in range(2):
                    total = total + row_get(act, 2 * m + dr, (2 * p + dp) * 16, 16)
            total = 0.25 * total
            pf[m, 1 + p] = total.astype(BF16)
            row_put(shifted, m, 8, total)

    def pool_edges():
        for first, shifted, at in ((0, sm1, 7), (4, sm0, 24)):
            total = 0.0
            for c in range(2):
                for dr in range(2):
                    total = total + row_get(act_e, first + c, dr, 16, 2)
            col_put(shifted, at, 0, 0.25 * total)

    def pool_shift(m):
        pf[m, 0] = row_get(sm1, m, 7, 16).astype(BF16)
        pf[m, 3] = row_get(sm0, m, 9, 16).astype(BF16)

    def mid_gelu(m):
        a, s = gelu_pair(pre_m[m])
        am[m] = rounded(a)
        row_put(slm, m + 2, 0, s)
        slb[m] = s.astype(BF16)

    for k in range(2):
        recv(0, 2 + k, c_buf.at[k], c_slot.at[k])
    for side, first in ((0, -3), (1, 64)):
        for c in range(3):
            col_put(s_ext, 8 + first + c, 3, c_slot[side, pl.ds(c * 16, 16)].astype(F32))
    for r in (3, 4, 17, 18):
        phases(r, (0, 5))

    @pl.loop(3, 17, unroll=2)
    def _(i):
        fine_gelu(i)

    pole_row = jnp.where(north, 2, 17)
    beyond_row = jnp.where(north, 1, 18)

    @pl.when(pole)
    def _():
        recv(0, side_l, hid.at[pl.ds(0, 1)], r_slot.at[side_l, pl.ds(0, 1)])
        halo = jnp.where(north, 2, 19)
        row_put(s_ext, halo, 8, r_slot[side_l, 0].astype(F32))
        for k in range(2):
            recv(0, 4 + 2 * side_l + k, kp_buf.at[k], kp_slot.at[2 * side_l + k])
            tile[0, pl.ds(0, 16), :] = kp_slot[2 * side_l + k].astype(F32)
            for c in range(3):
                at = halo * 80 + 8 + (64 if k else -3) + c
                for l in range(LANES):
                    s_ext.ref[l, pl.ds(at, 1), :] = tile[0, pl.ds(3 * c + l, 1), :]
        phases(halo, range(6))
        two = jnp.where(north, 2, 16)

        @pl.loop(0, 10, unroll=5)
        def _(i):
            col = 8 - 3 + i + (i // 5) * 60
            for a in range(3):
                l_late[a, i] = get(s_ext.ref, (two + a) * 80 + col, 16, 80).astype(BF16)

        def ring_pole(a, b):
            parts = [e_ext[pole_row + a, b : b + 4].reshape(64, C)]
            parts += [l_late[a, s * 5 + b : s * 5 + b + 3].reshape(48, C) for s in range(2)]
            return jnp.concatenate(parts, axis=0)

        res = conv_dot(ring_pole, wf)
        pre[pole_row] = res[:64]
        fine_gelu(pole_row)
        for i in range(6):
            a, s = gelu_pair(res[64 + 16 * i : 80 + 16 * i])
            a = rounded(a)
            for k in range(2):
                put(act_e.ref, i * act_e.pitch + two + k, a[k : k + 1])
                put(slp_e.ref, i * slp_e.pitch + two + k, s[k : k + 1])
                if i in (2, 3):
                    put(act.ref, (two + k) * act.pitch + (63 if i == 3 else 0), a[k : k + 1])
        m = jnp.where(north, 1, 8)
        pool_row(m)
        pool_edges()
        pool_shift(m)
        put(tile, 0, row_get(sm0, m, 8, 16))
        put(tile, 16, row_get(sm1, m, 8, 16))
        put(tile, 32, row_get(sm1, m, 7, 1))
        put(tile, 33, row_get(sm0, m, 24, 1))
        for side in range(2):
            put(tile, 34 + side, get(slp_e.ref, (1 + 3 * side) * slp_e.pitch + pole_row, 1))
        p2_buf[...] = get(tile, 0, 48).astype(BF16)
        remote(5, 0, p2_buf, p2_slot, 0, far).start()

    cot_in.wait()

    @pl.loop(0, 16, unroll=4)
    def _(r):
        row_put(sx, r, 0, cot[r].astype(F32))
        for p in range(4):
            ctp[r + 1, pl.ds(p * 16, 16)] = row_get(sx, r, p, 16, 4).astype(BF16)

    @pl.loop(0, 8, unroll=4)
    def _(m):
        for p in range(2):
            total = 0.0
            for dr in range(2):
                for dp in range(2):
                    total = total + ctp[2 * m + dr + 1, pl.ds((2 * p + dp) * 16, 16)].astype(F32)
            row_put(gma, m + 2, p * 16, total)

    for q in range(4):
        total = 0.0
        for dr in range(2):
            for p in range(2):
                total = total + row_get(gma, 2 * q + dr + 2, p * 16, 16)
        row_put(gcax, q + 2, 8, total)

    for side, (mid, coarse) in enumerate(((0, 0), (6, 2))):
        for k in range(2):
            lr_buf[side, pl.ds(32 * k, 32)] = row_get(gma, mid + k + 2, 0, 32).astype(BF16)
            lr_buf[side, pl.ds(64 + 16 * k, 16)] = row_get(gcax, coarse + k + 2, 8, 16).astype(BF16)
    for side, (col, mids, coarse) in enumerate(((0, (0, 16), 0), (63, (15, 31), 14))):
        put(tile, 0, col_get(sx, col, 0, 16))
        for c in range(2):
            put(tile, 16 + 8 * c, col_get(gma, mids[c], 2, 8))
            put(tile, 32 + 4 * c, col_get(gcax, 8 + coarse + c, 2, 8)[:4])
        lc_buf[side] = get(tile, 0, 48).astype(BF16)
        for k, (row, mid, low) in enumerate(((0, 2, 2), (15, 8, 4))):
            for c in range(2):
                put(tile, 2 * c, col_get(gma, mids[c], mid, 8)[:2])
                put(tile, 4 + 2 * c, col_get(gcax, 8 + coarse + c, low, 8)[:2])
            put(tile, 8, get(sx.ref, row * 64 + col, 1))
            lk_buf[2 * k + side] = get(tile, 0, 16).astype(BF16)

    for d in (0, 1):
        send(1, d, lr_buf.at[d], lr_slot, 0)
    for d in (2, 3):
        send(1, d, lc_buf.at[d - 2], lc_slot, 2)
    for d in (4, 5, 6, 7):
        send(1, d, lk_buf.at[d - 4], lk_slot, 4)


    receive(side_e)
    place(
        side_e, jnp.where(north, 19, 2), jnp.where(north, 1, -1),
        lambda j: jnp.where(north, j, 2 - j), lambda j: jnp.where(north, j, 3 - j),
    )
    for i in range(3):
        phases(jnp.where(north, 19, 0) + i, range(6))

    @pl.loop(0, 10, unroll=5)
    def _(i):
        col = 8 - 3 + i + (i // 5) * 60
        for a in range(3):
            l_edge[a, i] = get(s_ext.ref, a * 80 + col, 32, 80).astype(BF16)

    def ring(a, b):
        parts = [e_ext[jnp.where(north, 20 - q, 1 + q) + a - 1, b : b + 4].reshape(64, C) for q in range(3)]
        parts += [l_edge[a, s * 5 + b : s * 5 + b + 3].reshape(96, C) for s in range(2)]
        return jnp.concatenate(parts, axis=0)

    res = conv_dot(ring, wf)
    for q in range(3):
        pre[jnp.where(north, 19 - q, q)] = res[q * 64 : (q + 1) * 64]
    pre_e[...] = res[192:].reshape(6, 32, C)

    @pl.loop(0, 6, unroll=2)
    def _(i):
        a, s = gelu_pair(pre_e[i])
        row_put(act_e, i, 0, rounded(a))
        row_put(slp_e, i, 0, s)

    for dst, src in ((act, act_e), (slp, slp_e)):
        col_put(dst, 0, 0, row_get(src, 2, 0, 24))
        col_put(dst, 63, 0, row_get(src, 3, 0, 24))

    @pl.loop(0, 3, unroll=3)
    def _(q):
        fine_gelu(jnp.where(north, 17, 0) + q)

    wm_in.wait()

    @pl.loop(0, 8, unroll=4)
    def _(i):
        pool_row(jnp.where(north, 2, 0) + i)

    pool_edges()

    @pl.loop(0, 8, unroll=8)
    def _(i):
        pool_shift(jnp.where(north, 2, 0) + i)

    early = jnp.where(north, 2, 0)
    pre_m[pl.ds(early, 6)] = conv_dot(
        lambda a, b: pf[pl.ds(early + a, 6), b : b + 2].reshape(192, C), wm
    ).reshape(6, 32, C)

    @pl.loop(0, 6, unroll=2)
    def _(i):
        mid_gelu(early + i)

    @pl.when(jnp.logical_not(pole))
    def _():
        receive(side_l)
        place(
            side_l, jnp.where(north, 2, 19), jnp.where(north, -1, 1),
            lambda j: jnp.where(south, 2 - j, j), lambda j: jnp.where(south, 3 - j, j),
        )
        for i in range(3):
            phases(jnp.where(north, 0, 19) + i, range(6))
        edge_first = jnp.where(north, 0, 17)
        edge_rows = lax.broadcasted_iota(jnp.int32, (16, 1), 0)
        flip = (north & (edge_rows < 2)) | (south & ((edge_rows == 1) | (edge_rows == 2)))

        @pl.loop(0, 10, unroll=5)
        def _(i):
            col = 8 - 3 + i + (i // 5) * 60
            low, mid, high = (get(s_ext.ref, (edge_first + a) * 80 + col, 16, 80) for a in range(3))
            l_late[0, i] = jnp.where(flip, high, low).astype(BF16)
            l_late[1, i] = mid.astype(BF16)
            l_late[2, i] = jnp.where(flip, low, high).astype(BF16)

        def ring_late(a, b):
            rows = [jnp.where(north, 1 + q, 20 - q) + (1 if q == 2 else sgn_l) * (a - 1) for q in range(3)]
            parts = [e_ext[r, b : b + 4].reshape(64, C) for r in rows]
            parts += [l_late[a, s * 5 + b : s * 5 + b + 3].reshape(48, C) for s in range(2)]
            return jnp.concatenate(parts, axis=0)

        res = conv_dot(ring_late, wf)
        for q in range(3):
            pre[jnp.where(north, q, 19 - q)] = res[q * 64 : (q + 1) * 64]
        for i in range(6):
            a, s = gelu_pair(res[192 + 16 * i : 208 + 16 * i])
            a = rounded(a)
            for k in range(3):
                put(act_e.ref, i * act_e.pitch + edge_first + k, a[k : k + 1])
                put(slp_e.ref, i * slp_e.pitch + edge_first + k, s[k : k + 1])

        @pl.loop(0, 3, unroll=3)
        def _(q):
            fine_gelu(jnp.where(north, 0, 17) + q)

        for i in range(2):
            pool_row(jnp.where(north, 0, 8) + i)
        pool_edges()
        for i in range(2):
            pool_shift(jnp.where(north, 0, 8) + i)

    @pl.when(pole)
    def _():
        recv(5, 0, p2_buf, p2_slot)
        m = jnp.where(north, 0, 9)
        put(tile, 0, p2_slot[...].astype(F32))
        for p, shifted in ((0, sm0), (1, sm1)):
            pf[m, 1 + p] = p2_slot[pl.ds(16 * p, 16)]
            row_put(shifted, m, 8, get(tile, 16 * p, 16))
        put(sm1.ref, m * sm1.pitch + 7, get(tile, 32, 1))
        put(sm0.ref, m * sm0.pitch + 24, get(tile, 33, 1))
        pool_shift(m)
        for side in range(2):
            put(slp_e.ref, (1 + 3 * side) * slp_e.pitch + beyond_row, get(tile, 34 + side, 1))

    late = jnp.where(north, 0, 6)
    pre_m[pl.ds(late, 2)] = conv_dot(
        lambda a, b: pf[pl.ds(late + a, 2), b : b + 2].reshape(64, C), wm
    ).reshape(2, 32, C)
    for i in range(2):
        mid_gelu(late + i)

    for q in range(4):
        total = 0.0
        for dr in range(2):
            for p in range(2):
                total = total + am[2 * q + dr, pl.ds(p * 16, 16)]
        total = 0.25 * total
        pml[q] = total.astype(BF16)
        row_put(sc, q + 3, 16, total)
    for side, (first, mids) in enumerate(((0, (0, 16)), (13, (15, 31)))):
        for c in range(3):
            put(tile, c * 4, col_get(sc, 16 + first + c, 3, 8)[:4])
        for c in range(2):
            put(tile, 16 + 8 * c, col_get(slm, mids[c], 2, 8))
        pc_buf[side] = get(tile, 0, 32).astype(BF16)
        for k, row in enumerate((2, 8)):
            for c in range(2):
                put(tile, 12 + 2 * c, col_get(slm, mids[c], row, 8)[:2])
            pk_buf[2 * k + side] = get(tile, 0, 16).astype(BF16)

    far_d, near_d = jnp.where(north, 0, 1), jnp.where(north, 1, 0)
    for d, first, to, target in ((0, far_d, far_slot, far), (1, near_d, near_slot, near)):
        copy = remote(2, d, pml.at[pl.ds(first, 3)], pr_slot.at[to], to, target)
        copy.start()
        sends.append(copy)
    for d in (4, 5, 6, 7):
        send(2, d, pk_buf.at[d - 4], pk_slot, 4)
    for d in (2, 3):
        send(2, d, pc_buf.at[d - 2], pc_slot, 2)
    for d in (0, 1):
        send(3, d, slb.at[pl.ds(6 * d, 2)], sr_slot, 0)
    for d in (0, 1):
        send(4, d, ctp.at[1 + 15 * d], ct_slot, 0)
    @pl.when(pole)
    def _():
        sl_buf[...] = row_get(slp, pole_row, 0, 64).astype(BF16)
        remote(6, 0, sl_buf, sl_slot, 0, far).start()


    @pl.loop(0, 16, unroll=4)
    def _(r):
        for p in range(4):
            v = row_get(act, r + 2, p * 16, 16) + am[r // 2, pl.ds((p // 2) * 16, 16)]
            row_put(ns, r, p, v, 4)

    for k in range(2):
        recv(1, k, lr_buf.at[k], lr_slot.at[k])
    for k in range(2):
        recv(1, 2 + k, lc_buf.at[0], lc_slot.at[k])
        put(ts, k * 48, lc_slot[k].astype(F32))
    for k in range(4):
        recv(1, 4 + k, lk_buf.at[0], lk_slot.at[k])
        put(tk, k * 16, lk_slot[k].astype(F32))

    def pick(k, at):
        return get(ts, k * 48 + at, 1)

    def corner(k, at):
        return get(tk, k * 16 + at, 1)

    def edge_columns(dst, base, corner_base):
        for side in range(2):
            for c in range(2):
                to = side * 2 + c
                row_put(dst, to, 2, get(ts, side * 48 + base + 8 * c, 8))
                for j in range(2):
                    at = corner_base + 2 * c
                    row_put(dst, to, 1 - j, corner(side, at + jnp.where(north, j, 1 - j)))
                    row_put(dst, to, 10 + j, corner(2 + side, at + jnp.where(south, 1 - j, j)))

    for j in range(2):
        at_n, at_s = jnp.where(north, j, 1 - j), jnp.where(south, 1 - j, j)
        row_put(gma, 1 - j, 0, lr_slot[0, pl.ds(pl.multiple_of(32 * at_n, 32), 32)].astype(F32))
        row_put(gma, 10 + j, 0, lr_slot[1, pl.ds(pl.multiple_of(32 * at_s, 32), 32)].astype(F32))
        row_put(gcax, 1 - j, 8, lr_slot[0, pl.ds(pl.multiple_of(64 + 16 * at_n, 16), 16)].astype(F32))
        row_put(gcax, 6 + j, 8, lr_slot[1, pl.ds(pl.multiple_of(64 + 16 * at_s, 16), 16)].astype(F32))
    for side in range(2):
        row_put(cte, side, 2, get(ts, side * 48, 16))
        row_put(cte, side, 1, corner(side, 8))
        row_put(cte, side, 18, corner(2 + side, 8))
        for c in range(2):
            col = 8 + (16 if side else -2) + c
            for q in range(4):
                row_put(gcax, q + 2, col, pick(side, 32 + 4 * c + q))
            for j in range(2):
                row_put(gcax, 1 - j, col, corner(side, 4 + 2 * c + jnp.where(north, j, 1 - j)))
                row_put(gcax, 6 + j, col, corner(2 + side, 4 + 2 * c + jnp.where(south, 1 - j, j)))
    edge_columns(gmae, 16, 0)

    wc_in.wait()
    for k in range(2):
        recv(2, k, pml.at[pl.ds(0, 3)], pr_slot.at[k])
    for k in range(2):
        recv(2, 2 + k, pc_buf.at[0], pc_slot.at[k])
        put(ts, k * 48, pc_slot[k].astype(F32))
    for k in range(4):
        recv(2, 4 + k, pk_buf.at[0], pk_slot.at[k])
        put(tk, k * 16, pk_slot[k].astype(F32))
    for j in range(3):
        row_put(sc, 2 - j, 16, pr_slot[0, jnp.where(north, j, 2 - j)].astype(F32))
        row_put(sc, 7 + j, 16, pr_slot[1, jnp.where(south, 2 - j, j)].astype(F32))
    for side in range(2):
        for c in range(3):
            col = 16 + (16 if side else -3) + c
            for q in range(4):
                row_put(sc, q + 3, col, pick(side, 4 * c + q))
            for j in range(3):
                row_put(sc, 2 - j, col, corner(side, 4 * c + jnp.where(north, j, 3 - j)))
                row_put(sc, 7 + j, col, corner(2 + side, 4 * c + jnp.where(south, 3 - j, j)))

    @pl.loop(0, 10, unroll=True)
    def _(r):
        for b in range(3):
            cb[b, r] = row_get(sc, r, 7 + b, 32).astype(BF16)

    def coarse(a, b):
        rows = [1 + sgn_n * (a - 1), 2 + sgn_n * (a - 1)]
        tail = [7 + sgn_s * (a - 1), 8 + sgn_s * (a - 1)]
        parts = [cb[b, r] for r in rows] + [cb[b, 2 + a : 6 + a].reshape(128, C)]
        return jnp.concatenate(parts + [cb[b, r] for r in tail], axis=0)

    res = conv_dot(coarse, wc)
    for i in range(8):
        a, s = gelu_pair(res[i * 32 : (i + 1) * 32])
        if 2 <= i < 6:
            ac[i - 2] = rounded(a[8:24])
        row_put(gs, i, 8, row_get(gcax, i, 0, 32) * s)

    @pl.loop(0, 8, unroll=True)
    def _(r):
        for d in range(3):
            gb[d, r] = row_get(gs, r, 7 + d, 32).astype(BF16)

    for d in range(3):
        for k, (x, y) in enumerate(((0, 2), (1, 3), (4, 6), (5, 7))):
            gb[d, 8 + k] = (gb[d, x].astype(F32) + gb[d, y].astype(F32)).astype(BF16)
        gb[d, 12] = jnp.zeros((32, C), BF16)

    def coarse_t(a, b):
        d = 2 - b
        if a == 1:
            return gb[d, 1:7].reshape(192, C)
        if a == 0:
            rows = [jnp.where(north, 8, 2), jnp.where(north, 9, 3), 4, 5, jnp.where(south, 12, 6), jnp.where(south, 12, 7)]
        else:
            rows = [jnp.where(north, 12, 0), jnp.where(north, 12, 1), 2, 3, jnp.where(south, 10, 4), jnp.where(south, 11, 5)]
        return jnp.concatenate([gb[d, r] for r in rows], axis=0)

    res = conv_dot_t(coarse_t, wc)
    for i in range(6):
        row_put(bm, i, 0, 0.25 * res[i * 32 : (i + 1) * 32])

    for k in range(2):
        recv(3, k, slb.at[pl.ds(0, 2)], sr_slot.at[k])
    for j in range(2):
        row_put(slm, 1 - j, 0, sr_slot[0, jnp.where(north, j, 1 - j)].astype(F32))
        row_put(slm, 10 + j, 0, sr_slot[1, jnp.where(south, 1 - j, j)].astype(F32))
    edge_columns(sle, 16, 12)

    @pl.loop(0, 12, unroll=True)
    def _(k):
        below = row_get(bm, k // 2, 8, 16)
        for p, shifted in ((0, ms0), (1, ms1)):
            g = (row_get(gma, k, p * 16, 16) + below) * row_get(slm, k, p * 16, 16)
            mg[k, 1 + p] = g.astype(BF16)
            row_put(shifted, k, 8, g)

    for side in range(2):
        below = col_get(bm, 24 if side else 7, 0, 8)
        put(tile, 0, below, 2)
        put(tile, 1, below, 2)
        below = get(tile, 0, 16)
        for c in range(2):
            g = (row_get(gmae, side * 2 + c, 0, 16) + below) * row_get(sle, side * 2 + c, 0, 16)
            row_put(mc, side * 3 + (c + 1 if side else c), 0, g)
            if side == 0 and c == 1:
                col_put(ms1, 7, 0, g)
            if side == 1 and c == 0:
                col_put(ms0, 24, 0, g)
    row_put(mc, 2, 0, col_get(ms0, 8, 0, 16))
    row_put(mc, 3, 0, col_get(ms1, 23, 0, 16))

    @pl.loop(0, 12, unroll=True)
    def _(k):
        mg[k, 0] = row_get(ms1, k, 7, 16).astype(BF16)
        mg[k, 3] = row_get(ms0, k, 9, 16).astype(BF16)

    for k, (x, y) in enumerate(((0, 2), (1, 3), (8, 10), (9, 11))):
        mg[12 + k] = (mg[x].astype(F32) + mg[y].astype(F32)).astype(BF16)
    mg[16] = jnp.zeros((4, 16, C), BF16)

    half_rows = lax.broadcasted_iota(jnp.int32, (16, 1), 0)
    at_north = north & (half_rows < 2)
    at_south = south & ((half_rows == 8) | (half_rows == 9))
    for i in range(6):
        low, mid, high = (rounded(row_get(mc, i, e, 16)) for e in range(3))
        both = low + high
        ml[0, i] = jnp.where(at_north, both, jnp.where(at_south, 0.0, high)).astype(BF16)
        ml[1, i] = mid.astype(BF16)
        ml[2, i] = jnp.where(at_south, both, jnp.where(at_north, 0.0, low)).astype(BF16)

    def mid_t(a, b):
        ph = slice(2 - b, 4 - b)
        if a == 1:
            parts = [mg[1:11, ph].reshape(320, C)]
        else:
            if a == 0:
                top = [jnp.where(north, 12, 2), jnp.where(north, 13, 3)]
                body, tail = 4, [jnp.where(south, 16, 10), jnp.where(south, 16, 11)]
            else:
                top = [jnp.where(north, 16, 0), jnp.where(north, 16, 1)]
                body, tail = 2, [jnp.where(south, 14, 8), jnp.where(south, 15, 9)]
            parts = [mg[r, ph].reshape(32, C) for r in top]
            parts += [mg[body : body + 6, ph].reshape(192, C)]
            parts += [mg[r, ph].reshape(32, C) for r in tail]
        return jnp.concatenate(parts + [ml[a, 2 - b], ml[a, 5 - b]], axis=0)

    res = 0.25 * conv_dot_t(mid_t, wm)
    bfm[...] = res[:320].reshape(10, 32, C)
    for side in range(2):
        row_put(bfe, side, 0, res[320 + 16 * side : 336 + 16 * side])

    for k in range(2):
        recv(4, k, ctp.at[1], ct_slot.at[k])
        ctp[17 * k] = ct_slot[k]

    @pl.when(pole)
    def _():
        recv(6, 0, sl_buf, sl_slot)
        row_put(slp, beyond_row, 0, sl_slot[...].astype(F32))

    @pl.loop(0, 18, unroll=6)
    def _(k):
        for p in range(4):
            g = (
                ctp[k, pl.ds(p * 16, 16)].astype(F32) + bfm[(k + 1) // 2, pl.ds((p // 2) * 16, 16)]
            ) * row_get(slp, k + 1, p * 16, 16)
            g_ext[k, 1 + p] = g.astype(BF16)
            if p == 0:
                row_put(fs0, k, 8, g)
            if p == 3:
                row_put(fs3, k, 8, g)

    for side, (shifted, at) in enumerate(((fs3, 7), (fs0, 24))):
        below = row_get(bfe, side, 0, 16)
        put(tile, 0, below, 2)
        put(tile, 1, below, 2)
        g = (row_get(cte, side, 0, 32) + get(tile, 0, 32)) * row_get(slp_e, 1 + 3 * side, 0, 32)
        row_put(ge, side, 0, g)
        col_put(shifted, at, 0, row_get(ge, side, 1, 24))

    @pl.loop(0, 18, unroll=True)
    def _(k):
        g_ext[k, 0] = row_get(fs3, k, 7, 16).astype(BF16)
        g_ext[k, 5] = row_get(fs0, k, 9, 16).astype(BF16)

    for k, (x, y) in enumerate(((0, 2), (15, 17))):
        g_ext[18 + k] = (g_ext[x].astype(F32) + g_ext[y].astype(F32)).astype(BF16)
    g_ext[20] = jnp.zeros((6, 16, C), BF16)

    for copy in sends:
        copy.wait_send()

    @pl.when(pole)
    def _():
        far_rows(1).wait_send()
        for side in range(2):
            corner_copy(side, True, True).wait_send()
        remote(5, 0, p2_buf, p2_slot, 0, far).wait_send()
        remote(6, 0, sl_buf, sl_slot, 0, far).wait_send()

    @pl.when(jnp.logical_not(pole))
    def _():
        far_rows(3).wait_send()
        for side in range(2):
            corner_copy(side, True, False).wait_send()


def last_kernel(nlat, ns, ac, g_ext, wf, out_hbm, grad_hbm, out_v, grad_v, sx, acx, sem):
    lat = lax.axis_index("lat")
    north = lat == 0
    south = lat == nlat - 1
    sx, ns, acx = Rows(sx, 64), Rows(ns, 64), Rows(acx, 64)
    copies = []
    for h in range(2):

        def fine_t(a, b):
            ph = slice(2 - b, 6 - b)
            if a == 1:
                return g_ext[8 * h + 1 : 8 * h + 9, ph].reshape(512, C)
            first = 8 * h + 2 - a
            if h == 0:
                row = jnp.where(north, 20 if a else 18, first)
                parts = [g_ext[row, ph].reshape(64, C), g_ext[first + 1 : first + 8, ph].reshape(448, C)]
            else:
                row = jnp.where(south, 19 if a else 20, first + 7)
                parts = [g_ext[first : first + 7, ph].reshape(448, C), g_ext[row, ph].reshape(64, C)]
            return jnp.concatenate(parts, axis=0)

        res = conv_dot_t(fine_t, wf)
        if h == 0:
            for q in range(4):
                for p in range(4):
                    row_put(acx, q, p, ac[q], 4)
            for r in range(16):
                out_v[r] = (row_get(ns, r, 0, 64) + row_get(acx, r // 4, 0, 64)).astype(BF16)
            copies.append(pltpu.make_async_copy(out_v, out_hbm, sem.at[2]))
            copies[-1].start()
        for r in range(8):
            for p in range(4):
                row_put(sx, 8 * h + r, p, res[r * 64 + p * 16 : r * 64 + p * 16 + 16], 4)
            grad_v[8 * h + r] = row_get(sx, 8 * h + r, 0, 64).astype(BF16)
        half = pl.ds(8 * h, 8)
        copies.append(pltpu.make_async_copy(grad_v.at[half], grad_hbm.at[half], sem.at[h]))
        copies[-1].start()
    for copy in copies:
        copy.wait()


def body(nlat, nlon, hidden_in, cotangent, weight_fine, weight_mid, weight_coarse):
    hbm = pl.BlockSpec(memory_space=pltpu.HBM)
    field = (16, 64, C)
    weight = (3, 3, C, C)

    def v(*shape, dtype=BF16):
        return pltpu.VMEM(shape, dtype)

    def f(*shape):
        return pltpu.VMEM(shape, F32)

    scratch = dict(
        hid=v(*field), cot=v(*field), wm=v(*weight), wc=v(*weight),
        s_ext=f(3, 36 * 80, 128), e_ext=v(22, 6, 16, C), l_edge=v(3, 10, 32, C), l_late=v(3, 10, 16, C), pre=f(24, 64, C), pre_e=f(6, 32, C),
        act=f(3, 25 * 64, 128), slp=f(3, 25 * 64, 128), act_e=f(3, 6 * 40, 128), slp_e=f(3, 6 * 32, 128),
        sx=f(3, 17 * 64, 128), ctp=v(18, 64, C), cte=f(3, 2 * 32, 128), gma=f(3, 17 * 32, 128), gmae=f(3, 5 * 16, 128),
        gcax=f(3, 16 * 32, 128),
        pf=v(10, 4, 16, C), sm0=f(3, 17 * 32, 128), sm1=f(3, 17 * 32, 128), pre_m=f(8, 32, C), am=f(8, 32, C),
        slm=f(3, 17 * 32, 128), sle=f(3, 5 * 16, 128), slb=v(8, 32, C), pml=v(4, 16, C), sc=f(3, 12 * 48, 128),
        cb=v(3, 10, 32, C), gs=f(3, 8 * 48, 128), gb=v(3, 13, 32, C), bm=f(3, 9 * 32, 128),
        mg=v(17, 4, 16, C), ms0=f(3, 17 * 32, 128), ms1=f(3, 17 * 32, 128), mc=f(3, 6 * 24, 128), ml=v(3, 6, 16, C),
        bfm=f(10, 32, C), bfe=f(3, 2 * 16, 128), fs0=f(3, 25 * 32, 128), fs3=f(3, 25 * 32, 128),
        ge=f(3, 2 * 32, 128), tile=f(3, 48, 128), ts=f(3, 96, 128), tk=f(3, 80, 128),
        c_buf=v(2, 48, C), k_buf=v(4, 16, C), r_slot=v(2, 3, 64, C), c_slot=v(2, 48, C), k_slot=v(4, 16, C),
        kp_buf=v(2, 16, 128), kp_slot=v(4, 16, 128),
        lr_buf=v(2, 96, C), lc_buf=v(2, 48, C), lk_buf=v(4, 16, C),
        lr_slot=v(2, 96, C), lc_slot=v(2, 48, C), lk_slot=v(4, 16, C),
        pc_buf=v(2, 32, C), pk_buf=v(4, 16, C),
        p2_buf=v(48, C), p2_slot=v(48, C), sl_buf=v(64, C), sl_slot=v(64, C),
        pr_slot=v(2, 3, 16, C), sr_slot=v(2, 2, 32, C), ct_slot=v(2, 64, C), pc_slot=v(2, 32, C), pk_slot=v(4, 16, C),
        lsem=pltpu.SemaphoreType.DMA((8,)), ssem=pltpu.SemaphoreType.DMA((7, 8)), rsem=pltpu.SemaphoreType.DMA((7, 8)),
    )
    vmem = pl.BlockSpec(memory_space=pltpu.VMEM)
    results = pl.pallas_call(
        functools.partial(kernel, nlat, nlon),
        out_shape=(f(3, 17 * 64, 128), f(4, 16, C), v(21, 6, 16, C), v(*weight)),
        in_specs=[hbm] * 5,
        out_specs=(vmem,) * 4,
        scratch_shapes=list(scratch.values()),
        compiler_params=pltpu.CompilerParams(
            collective_id=0, has_side_effects=True, vmem_limit_bytes=52 * 2**20
        ),
    )(hidden_in, cotangent, weight_fine, weight_mid, weight_coarse)
    shape = jax.ShapeDtypeStruct(field, BF16)
    return pl.pallas_call(
        functools.partial(last_kernel, nlat),
        out_shape=(shape, shape),
        in_specs=[vmem] * 4,
        out_specs=(hbm, hbm),
        scratch_shapes=[v(*field), v(*field), f(3, 17 * 64, 128), f(3, 5 * 64, 128), pltpu.SemaphoreType.DMA((3,))],
        compiler_params=pltpu.CompilerParams(vmem_limit_bytes=36 * 2**20),
    )(*results)


def solution(mesh):
    field = P("lat", "lon", None)
    return jax.shard_map(
        functools.partial(body, mesh.shape["lat"], mesh.shape["lon"]),
        mesh=mesh,
        in_specs=(field, field, P(), P(), P()),
        out_specs=(field, field),
        check_vma=False,
    )
```

```python
import functools

import jax
import jax.numpy as jnp
from jax import lax
from jax.experimental import pallas as pl
from jax.experimental.pallas import tpu as pltpu
from jax.sharding import PartitionSpec as P

MESH = pl.DeviceIdType.MESH
F32 = jnp.float32
BF16 = jnp.bfloat16
C = 384
LANES = 3


def get(ref, start, n, stride=1):
    ds = pl.ds(start, n) if stride == 1 else pl.ds(start, n, stride=stride)
    return jnp.concatenate([ref[l, ds, :] for l in range(LANES)], axis=-1)


def put(ref, start, val, stride=1):
    n = val.shape[0]
    ds = pl.ds(start, n) if stride == 1 else pl.ds(start, n, stride=stride)
    for l in range(LANES):
        ref[l, ds, :] = val[:, l * 128 : (l + 1) * 128]


class Rows:
    def __init__(self, ref, pitch):
        self.ref, self.pitch = ref, pitch


def at_row(grid, r, start):
    if isinstance(r, int):
        return r * grid.pitch + start
    if start % 8 == 0 and grid.pitch % 8 == 0:
        return pl.multiple_of(r * grid.pitch + start, 8)
    return r * grid.pitch + start


def row_get(grid, r, start, n, stride=1):
    return get(grid.ref, at_row(grid, r, start), n, stride)


def row_put(grid, r, start, val, stride=1):
    put(grid.ref, at_row(grid, r, start), val, stride)


def col_get(grid, c, r0, n):
    return get(grid.ref, r0 * grid.pitch + c, n, grid.pitch)


def col_put(grid, c, r0, val):
    put(grid.ref, r0 * grid.pitch + c, val, grid.pitch)


def gelu_pair(z):
    e = jnp.exp(-0.5 * z * z)
    t = 1.0 / (1.0 + (0.3275911 * 0.7071067811865476) * jnp.abs(z))
    q = t * (
        0.127414796
        + t * (-0.142248368 + t * (0.7107068705 + t * (-0.7265760135 + t * 0.5307027145)))
    )
    h = q * e
    cdf = jnp.where(z >= 0, 1.0 - h, h)
    return z * cdf, cdf + z * (e * 0.3989422804014327)


def rounded(x):
    return x.astype(BF16).astype(F32)


def conv_dot(parts, weight):
    lhs = jnp.concatenate([parts(a, b) for a in range(3) for b in range(3)], axis=-1)
    return jnp.dot(lhs, weight[...].reshape(9 * C, C), preferred_element_type=F32)


def conv_dot_t(parts, weight):
    lhs = jnp.concatenate([parts(a, b) for a in range(3) for b in range(3)], axis=-1)
    rhs = jnp.concatenate([weight[a, b] for a in range(3) for b in range(3)], axis=-1)
    return lax.dot_general(lhs, rhs, (((1,), (1,)), ((), ())), preferred_element_type=F32)


def kernel(
    nlat, nlon,
    hid_hbm, cot_hbm, wf_hbm, wm_hbm, wc_hbm, ns, ac, g_ext, wf,
    hid, cot, wm, wc,
    s_ext, e_ext, l_edge, l_late, pre, pre_e, act, slp, act_e, slp_e,
    sx, ctp, cte, gma, gmae, gcax,
    pf, sm0, sm1, pre_m, am, slm, sle, slb, pml, sc, cb, gs, gb, bm,
    mg, ms0, ms1, mc, ml, bfm, bfe, fs0, fs3, ge, tile, ts, tk,
    c_buf, k_buf, r_slot, c_slot, k_slot, kp_buf, kp_slot,
    lr_buf, lc_buf, lk_buf, lr_slot, lc_slot, lk_slot,
    pc_buf, pk_buf, p2_buf, p2_slot, sl_buf, sl_slot, pr_slot, sr_slot, ct_slot, pc_slot, pk_slot,
    lsem, ssem, rsem,
):
    s_ext = Rows(s_ext, 80)
    act = Rows(act, 64)
    slp = Rows(slp, 64)
    act_e = Rows(act_e, 40)
    slp_e = Rows(slp_e, 32)
    sx = Rows(sx, 64)
    cte = Rows(cte, 32)
    gma = Rows(gma, 32)
    gmae = Rows(gmae, 16)
    gcax = Rows(gcax, 32)
    sm0 = Rows(sm0, 32)
    sm1 = Rows(sm1, 32)
    slm = Rows(slm, 32)
    sle = Rows(sle, 16)
    sc = Rows(sc, 48)
    gs = Rows(gs, 48)
    bm = Rows(bm, 32)
    ms0 = Rows(ms0, 32)
    ms1 = Rows(ms1, 32)
    mc = Rows(mc, 24)
    bfe = Rows(bfe, 16)
    fs0 = Rows(fs0, 32)
    fs3 = Rows(fs3, 32)
    ge = Rows(ge, 32)
    ns = Rows(ns, 64)
    lat = lax.axis_index("lat")
    lon = lax.axis_index("lon")
    north = lat == 0
    south = lat == nlat - 1
    sgn_n = jnp.where(north, -1, 1)
    sgn_s = jnp.where(south, -1, 1)

    def device(dlat, dlon):
        to_lat, to_lon = lat, lon + dlon + nlon
        if dlat:
            pole = north if dlat < 0 else south
            to_lat = jnp.where(pole, lat, lat + dlat)
            to_lon = to_lon + jnp.where(pole, nlon // 2, 0)
        return {"lat": to_lat, "lon": lax.rem(to_lon, nlon)}

    there = [device(*d) for d in ((-1, 0), (1, 0), (0, -1), (0, 1), (-1, -1), (-1, 1), (1, -1), (1, 1))]
    slot = [
        jnp.where(north, 0, 1), jnp.where(south, 1, 0), 3, 2,
        jnp.where(north, 5, 7), jnp.where(north, 4, 6),
        jnp.where(south, 7, 5), jnp.where(south, 6, 4),
    ]

    def remote(kind, d, src, dst, where, target):
        return pltpu.make_async_remote_copy(
            src_ref=src, dst_ref=dst, send_sem=ssem.at[kind, d], recv_sem=rsem.at[kind, where],
            device_id=target, device_id_type=MESH,
        )

    def load(i, src, dst):
        copy = pltpu.make_async_copy(src, dst, lsem.at[i])
        copy.start()
        return copy

    barrier = pltpu.get_barrier_semaphore()
    for t in there:
        pl.semaphore_signal(barrier, inc=1, device_id=t, device_id_type=MESH)

    hid_in = load(0, hid_hbm, hid)
    wf_in = load(1, wf_hbm, wf)
    sends = []

    def send(kind, d, src, slots, base):
        copy = remote(kind, d, src, slots.at[slot[d] - base], slot[d], there[d])
        copy.start()
        sends.append(copy)

    def recv(kind, where, src, dst):
        remote(kind, 0, src, dst, where, there[0]).wait_recv()

    pl.semaphore_wait(barrier, 8)
    pole = north | south
    far = {k: jnp.where(north, there[0][k], there[1][k]) for k in ("lat", "lon")}
    near = {k: jnp.where(north, there[1][k], there[0][k]) for k in ("lat", "lon")}
    far_slot, near_slot = jnp.where(north, slot[0], slot[1]), jnp.where(north, slot[1], slot[0])

    def far_rows(n):
        src = hid_hbm.at[pl.ds(jnp.where(north, 0, 16 - n), n)]
        return remote(0, 0, src, r_slot.at[far_slot, pl.ds(0, n)], far_slot, far)

    @pl.when(pole)
    def _():
        far_rows(1).start()

    @pl.when(jnp.logical_not(pole))
    def _():
        far_rows(3).start()

    copy = remote(0, 1, hid_hbm.at[pl.ds(jnp.where(north, 13, 0), 3)], r_slot.at[near_slot], near_slot, near)
    copy.start()
    sends.append(copy)
    hid_in.wait()

    @pl.loop(0, 16, unroll=4)
    def _(r):
        row_put(s_ext, r + 3, 8, hid[r].astype(F32))

    for side, first in ((0, 0), (1, 61)):
        for c in range(3):
            c_buf[side, pl.ds(c * 16, 16)] = col_get(s_ext, 8 + first + c, 3, 16).astype(BF16)
    for k, (row, first) in enumerate(((0, 0), (0, 61), (12, 0), (12, 61))):
        for c in range(3):
            put(tile, c * 4, col_get(s_ext, 8 + first + c, 3 + row, 8)[:4])
        k_buf[k] = get(tile, 0, 16).astype(BF16)

    for side, first in ((0, 0), (1, 61)):
        at = (3 + jnp.where(north, 0, 15)) * 80 + 8 + first
        for c in range(3):
            for l in range(LANES):
                tile[0, pl.ds(3 * c + l, 1), :] = s_ext.ref[l, pl.ds(at + c, 1), :]
        kp_buf[side] = tile[0, pl.ds(0, 16), :].astype(BF16)

    def corner_copy(side, at_far, small):
        top = north if at_far else jnp.logical_not(north)
        target = {k: jnp.where(top, there[4 + side][k], there[6 + side][k]) for k in ("lat", "lon")}
        to = jnp.where(top, slot[4 + side], slot[6 + side])
        if small:
            return remote(0, 4 + side, kp_buf.at[side], kp_slot.at[to - 4], to, target)
        src = k_buf.at[side + jnp.where(top, 0, 2)]
        return remote(0, (4 if at_far else 6) + side, src, k_slot.at[to - 4], to, target)

    @pl.when(pole)
    def _():
        for side in range(2):
            corner_copy(side, True, True).start()

    @pl.when(jnp.logical_not(pole))
    def _():
        for side in range(2):
            corner_copy(side, True, False).start()

    for side in range(2):
        sends.append(corner_copy(side, False, False))
        sends[-1].start()
    for d in (2, 3):
        send(0, d, c_buf.at[d - 2], c_slot, 2)

    @pl.loop(0, 16, unroll=4)
    def _(r):
        for ph in range(6):
            e_ext[r + 3, ph] = row_get(s_ext, r + 3, 7 + ph, 16, 4).astype(BF16)

    wf_in.wait()
    cot_in = load(2, cot_hbm, cot)
    wm_in = load(3, wm_hbm, wm)
    wc_in = load(4, wc_hbm, wc)
    pre[pl.ds(3, 14)] = conv_dot(
        lambda a, b: e_ext[3 + a : 17 + a, b : b + 4].reshape(14 * 64, C), wf
    ).reshape(14, 64, C)

    def fine_gelu(i):
        a, s = gelu_pair(pre[i])
        row_put(act, i, 0, rounded(a))
        row_put(slp, i, 0, s)

    side_e, side_l = jnp.where(north, 1, 0), jnp.where(north, 0, 1)
    sgn_l = jnp.where(north | south, -1, 1)

    def receive(side):
        recv(0, side, hid.at[pl.ds(0, 3)], r_slot.at[side])
        for k in range(2):
            recv(0, 4 + 2 * side + k, k_buf.at[k], k_slot.at[2 * side + k])

    def place(side, first, step, row_order, corner_order):
        for j in range(3):
            row_put(s_ext, first + step * j, 8, r_slot[side, row_order(j)].astype(F32))
        for k in range(2):
            put(tile, 0, k_slot[2 * side + k].astype(F32))
            for c in range(3):
                for j in range(3):
                    at = (first + step * j) * 80 + 8 + (64 if k else -3) + c
                    put(s_ext.ref, at, get(tile, c * 4 + corner_order(j), 1))

    def phases(r, which):
        for ph in which:
            e_ext[r, ph] = row_get(s_ext, r, 7 + ph, 16, 4).astype(BF16)

    def pool_row(m):
        for p, shifted in ((0, sm0), (1, sm1)):
            total = 0.0
            for dr in range(2):
                for dp in range(2):
                    total = total + row_get(act, 2 * m + dr, (2 * p + dp) * 16, 16)
            total = 0.25 * total
            pf[m, 1 + p] = total.astype(BF16)
            row_put(shifted, m, 8, total)

    def pool_edges():
        for first, shifted, at in ((0, sm1, 7), (4, sm0, 24)):
            total = 0.0
            for c in range(2):
                for dr in range(2):
                    total = total + row_get(act_e, first + c, dr, 16, 2)
            col_put(shifted, at, 0, 0.25 * total)

    def pool_shift(m):
        pf[m, 0] = row_get(sm1, m, 7, 16).astype(BF16)
        pf[m, 3] = row_get(sm0, m, 9, 16).astype(BF16)

    def mid_gelu(m):
        a, s = gelu_pair(pre_m[m])
        am[m] = rounded(a)
        row_put(slm, m + 2, 0, s)
        slb[m] = s.astype(BF16)

    for k in range(2):
        recv(0, 2 + k, c_buf.at[k], c_slot.at[k])
    for side, first in ((0, -3), (1, 64)):
        for c in range(3):
            col_put(s_ext, 8 + first + c, 3, c_slot[side, pl.ds(c * 16, 16)].astype(F32))
    for r in (3, 4, 17, 18):
        phases(r, (0, 5))

    @pl.loop(3, 17, unroll=2)
    def _(i):
        fine_gelu(i)

    pole_row = jnp.where(north, 2, 17)
    beyond_row = jnp.where(north, 1, 18)

    @pl.when(pole)
    def _():
        recv(0, side_l, hid.at[pl.ds(0, 1)], r_slot.at[side_l, pl.ds(0, 1)])
        halo = jnp.where(north, 2, 19)
        row_put(s_ext, halo, 8, r_slot[side_l, 0].astype(F32))
        for k in range(2):
            recv(0, 4 + 2 * side_l + k, kp_buf.at[k], kp_slot.at[2 * side_l + k])
            tile[0, pl.ds(0, 16), :] = kp_slot[2 * side_l + k].astype(F32)
            for c in range(3):
                at = halo * 80 + 8 + (64 if k else -3) + c
                for l in range(LANES):
                    s_ext.ref[l, pl.ds(at, 1), :] = tile[0, pl.ds(3 * c + l, 1), :]
        phases(halo, range(6))
        two = jnp.where(north, 2, 16)

        @pl.loop(0, 10, unroll=5)
        def _(i):
            col = 8 - 3 + i + (i // 5) * 60
            for a in range(3):
                l_late[a, i] = get(s_ext.ref, (two + a) * 80 + col, 16, 80).astype(BF16)

        def ring_pole(a, b):
            parts = [e_ext[pole_row + a, b : b + 4].reshape(64, C)]
            parts += [l_late[a, s * 5 + b : s * 5 + b + 3].reshape(48, C) for s in range(2)]
            return jnp.concatenate(parts, axis=0)

        res = conv_dot(ring_pole, wf)
        pre[pole_row] = res[:64]
        fine_gelu(pole_row)
        for i in range(6):
            a, s = gelu_pair(res[64 + 16 * i : 80 + 16 * i])
            a = rounded(a)
            for k in range(2):
                put(act_e.ref, i * act_e.pitch + two + k, a[k : k + 1])
                put(slp_e.ref, i * slp_e.pitch + two + k, s[k : k + 1])
                if i in (2, 3):
                    put(act.ref, (two + k) * act.pitch + (63 if i == 3 else 0), a[k : k + 1])
        m = jnp.where(north, 1, 8)
        pool_row(m)
        pool_edges()
        pool_shift(m)
        put(tile, 0, row_get(sm0, m, 8, 16))
        put(tile, 16, row_get(sm1, m, 8, 16))
        put(tile, 32, row_get(sm1, m, 7, 1))
        put(tile, 33, row_get(sm0, m, 24, 1))
        for side in range(2):
            put(tile, 34 + side, get(slp_e.ref, (1 + 3 * side) * slp_e.pitch + pole_row, 1))
        p2_buf[...] = get(tile, 0, 48).astype(BF16)
        remote(5, 0, p2_buf, p2_slot, 0, far).start()

    cot_in.wait()

    @pl.loop(0, 16, unroll=4)
    def _(r):
        row_put(sx, r, 0, cot[r].astype(F32))
        for p in range(4):
            ctp[r + 1, pl.ds(p * 16, 16)] = row_get(sx, r, p, 16, 4).astype(BF16)

    @pl.loop(0, 8, unroll=4)
    def _(m):
        for p in range(2):
            total = 0.0
            for dr in range(2):
                for dp in range(2):
                    total = total + ctp[2 * m + dr + 1, pl.ds((2 * p + dp) * 16, 16)].astype(F32)
            row_put(gma, m + 2, p * 16, total)

    for q in range(4):
        total = 0.0
        for dr in range(2):
            for p in range(2):
                total = total + row_get(gma, 2 * q + dr + 2, p * 16, 16)
        row_put(gcax, q + 2, 8, total)

    for side, (mid, coarse) in enumerate(((0, 0), (6, 2))):
        for k in range(2):
            lr_buf[side, pl.ds(32 * k, 32)] = row_get(gma, mid + k + 2, 0, 32).astype(BF16)
            lr_buf[side, pl.ds(64 + 16 * k, 16)] = row_get(gcax, coarse + k + 2, 8, 16).astype(BF16)
    for side, (col, mids, coarse) in enumerate(((0, (0, 16), 0), (63, (15, 31), 14))):
        put(tile, 0, col_get(sx, col, 0, 16))
        for c in range(2):
            put(tile, 16 + 8 * c, col_get(gma, mids[c], 2, 8))
            put(tile, 32 + 4 * c, col_get(gcax, 8 + coarse + c, 2, 8)[:4])
        lc_buf[side] = get(tile, 0, 48).astype(BF16)
        for k, (row, mid, low) in enumerate(((0, 2, 2), (15, 8, 4))):
            for c in range(2):
                put(tile, 2 * c, col_get(gma, mids[c], mid, 8)[:2])
                put(tile, 4 + 2 * c, col_get(gcax, 8 + coarse + c, low, 8)[:2])
            put(tile, 8, get(sx.ref, row * 64 + col, 1))
            lk_buf[2 * k + side] = get(tile, 0, 16).astype(BF16)

    for d in (0, 1):
        send(1, d, lr_buf.at[d], lr_slot, 0)
    for d in (2, 3):
        send(1, d, lc_buf.at[d - 2], lc_slot, 2)
    for d in (4, 5, 6, 7):
        send(1, d, lk_buf.at[d - 4], lk_slot, 4)


    receive(side_e)
    place(
        side_e, jnp.where(north, 19, 2), jnp.where(north, 1, -1),
        lambda j: jnp.where(north, j, 2 - j), lambda j: jnp.where(north, j, 3 - j),
    )
    for i in range(3):
        phases(jnp.where(north, 19, 0) + i, range(6))

    @pl.loop(0, 10, unroll=5)
    def _(i):
        col = 8 - 3 + i + (i // 5) * 60
        for a in range(3):
            l_edge[a, i] = get(s_ext.ref, a * 80 + col, 32, 80).astype(BF16)

    def ring(a, b):
        parts = [e_ext[jnp.where(north, 20 - q, 1 + q) + a - 1, b : b + 4].reshape(64, C) for q in range(3)]
        parts += [l_edge[a, s * 5 + b : s * 5 + b + 3].reshape(96, C) for s in range(2)]
        return jnp.concatenate(parts, axis=0)

    res = conv_dot(ring, wf)
    for q in range(3):
        pre[jnp.where(north, 19 - q, q)] = res[q * 64 : (q + 1) * 64]
    pre_e[...] = res[192:].reshape(6, 32, C)

    @pl.loop(0, 6, unroll=2)
    def _(i):
        a, s = gelu_pair(pre_e[i])
        row_put(act_e, i, 0, rounded(a))
        row_put(slp_e, i, 0, s)

    for dst, src in ((act, act_e), (slp, slp_e)):
        col_put(dst, 0, 0, row_get(src, 2, 0, 24))
        col_put(dst, 63, 0, row_get(src, 3, 0, 24))

    @pl.loop(0, 3, unroll=3)
    def _(q):
        fine_gelu(jnp.where(north, 17, 0) + q)

    wm_in.wait()

    @pl.loop(0, 8, unroll=4)
    def _(i):
        pool_row(jnp.where(north, 2, 0) + i)

    pool_edges()

    @pl.loop(0, 8, unroll=8)
    def _(i):
        pool_shift(jnp.where(north, 2, 0) + i)

    early = jnp.where(north, 2, 0)
    pre_m[pl.ds(early, 6)] = conv_dot(
        lambda a, b: pf[pl.ds(early + a, 6), b : b + 2].reshape(192, C), wm
    ).reshape(6, 32, C)

    @pl.loop(0, 6, unroll=2)
    def _(i):
        mid_gelu(early + i)

    @pl.when(jnp.logical_not(pole))
    def _():
        receive(side_l)
        place(
            side_l, jnp.where(north, 2, 19), jnp.where(north, -1, 1),
            lambda j: jnp.where(south, 2 - j, j), lambda j: jnp.where(south, 3 - j, j),
        )
        for i in range(3):
            phases(jnp.where(north, 0, 19) + i, range(6))
        edge_first = jnp.where(north, 0, 17)
        edge_rows = lax.broadcasted_iota(jnp.int32, (16, 1), 0)
        flip = (north & (edge_rows < 2)) | (south & ((edge_rows == 1) | (edge_rows == 2)))

        @pl.loop(0, 10, unroll=5)
        def _(i):
            col = 8 - 3 + i + (i // 5) * 60
            low, mid, high = (get(s_ext.ref, (edge_first + a) * 80 + col, 16, 80) for a in range(3))
            l_late[0, i] = jnp.where(flip, high, low).astype(BF16)
            l_late[1, i] = mid.astype(BF16)
            l_late[2, i] = jnp.where(flip, low, high).astype(BF16)

        def ring_late(a, b):
            rows = [jnp.where(north, 1 + q, 20 - q) + (1 if q == 2 else sgn_l) * (a - 1) for q in range(3)]
            parts = [e_ext[r, b : b + 4].reshape(64, C) for r in rows]
            parts += [l_late[a, s * 5 + b : s * 5 + b + 3].reshape(48, C) for s in range(2)]
            return jnp.concatenate(parts, axis=0)

        res = conv_dot(ring_late, wf)
        for q in range(3):
            pre[jnp.where(north, q, 19 - q)] = res[q * 64 : (q + 1) * 64]
        for i in range(6):
            a, s = gelu_pair(res[192 + 16 * i : 208 + 16 * i])
            a = rounded(a)
            for k in range(3):
                put(act_e.ref, i * act_e.pitch + edge_first + k, a[k : k + 1])
                put(slp_e.ref, i * slp_e.pitch + edge_first + k, s[k : k + 1])

        @pl.loop(0, 3, unroll=3)
        def _(q):
            fine_gelu(jnp.where(north, 0, 17) + q)

        for i in range(2):
            pool_row(jnp.where(north, 0, 8) + i)
        pool_edges()
        for i in range(2):
            pool_shift(jnp.where(north, 0, 8) + i)

    @pl.when(pole)
    def _():
        recv(5, 0, p2_buf, p2_slot)
        m = jnp.where(north, 0, 9)
        put(tile, 0, p2_slot[...].astype(F32))
        for p, shifted in ((0, sm0), (1, sm1)):
            pf[m, 1 + p] = p2_slot[pl.ds(16 * p, 16)]
            row_put(shifted, m, 8, get(tile, 16 * p, 16))
        put(sm1.ref, m * sm1.pitch + 7, get(tile, 32, 1))
        put(sm0.ref, m * sm0.pitch + 24, get(tile, 33, 1))
        pool_shift(m)
        for side in range(2):
            put(slp_e.ref, (1 + 3 * side) * slp_e.pitch + beyond_row, get(tile, 34 + side, 1))

    late = jnp.where(north, 0, 6)
    pre_m[pl.ds(late, 2)] = conv_dot(
        lambda a, b: pf[pl.ds(late + a, 2), b : b + 2].reshape(64, C), wm
    ).reshape(2, 32, C)
    for i in range(2):
        mid_gelu(late + i)

    for q in range(4):
        total = 0.0
        for dr in range(2):
            for p in range(2):
                total = total + am[2 * q + dr, pl.ds(p * 16, 16)]
        total = 0.25 * total
        pml[q] = total.astype(BF16)
        row_put(sc, q + 3, 16, total)
    for side, (first, mids) in enumerate(((0, (0, 16)), (13, (15, 31)))):
        for c in range(3):
            put(tile, c * 4, col_get(sc, 16 + first + c, 3, 8)[:4])
        for c in range(2):
            put(tile, 16 + 8 * c, col_get(slm, mids[c], 2, 8))
        pc_buf[side] = get(tile, 0, 32).astype(BF16)
        for k, row in enumerate((2, 8)):
            for c in range(2):
                put(tile, 12 + 2 * c, col_get(slm, mids[c], row, 8)[:2])
            pk_buf[2 * k + side] = get(tile, 0, 16).astype(BF16)

    far_d, near_d = jnp.where(north, 0, 1), jnp.where(north, 1, 0)
    for d, first, to, target in ((0, far_d, far_slot, far), (1, near_d, near_slot, near)):
        copy = remote(2, d, pml.at[pl.ds(first, 3)], pr_slot.at[to], to, target)
        copy.start()
        sends.append(copy)
    for d in (4, 5, 6, 7):
        send(2, d, pk_buf.at[d - 4], pk_slot, 4)
    for d in (2, 3):
        send(2, d, pc_buf.at[d - 2], pc_slot, 2)
    for kind in (3, 4):
        for d, k, to, target in ((0, far_d, far_slot, far), (1, near_d, near_slot, near)):
            src, dst = (slb.at[pl.ds(6 * k, 2)], sr_slot) if kind == 3 else (ctp.at[1 + 15 * k], ct_slot)
            copy = remote(kind, d, src, dst.at[to], to, target)
            copy.start()
            sends.append(copy)
    @pl.when(pole)
    def _():
        sl_buf[...] = row_get(slp, pole_row, 0, 64).astype(BF16)
        remote(6, 0, sl_buf, sl_slot, 0, far).start()


    @pl.loop(0, 16, unroll=4)
    def _(r):
        for p in range(4):
            v = row_get(act, r + 2, p * 16, 16) + am[r // 2, pl.ds((p // 2) * 16, 16)]
            row_put(ns, r, p, v, 4)

    for k in range(2):
        recv(1, k, lr_buf.at[k], lr_slot.at[k])
    for k in range(2):
        recv(1, 2 + k, lc_buf.at[0], lc_slot.at[k])
        put(ts, k * 48, lc_slot[k].astype(F32))
    for k in range(4):
        recv(1, 4 + k, lk_buf.at[0], lk_slot.at[k])
        put(tk, k * 16, lk_slot[k].astype(F32))

    def pick(k, at):
        return get(ts, k * 48 + at, 1)

    def corner(k, at):
        return get(tk, k * 16 + at, 1)

    def edge_columns(dst, base, corner_base):
        for side in range(2):
            for c in range(2):
                to = side * 2 + c
                row_put(dst, to, 2, get(ts, side * 48 + base + 8 * c, 8))
                for j in range(2):
                    at = corner_base + 2 * c
                    row_put(dst, to, 1 - j, corner(side, at + jnp.where(north, j, 1 - j)))
                    row_put(dst, to, 10 + j, corner(2 + side, at + jnp.where(south, 1 - j, j)))

    for j in range(2):
        at_n, at_s = jnp.where(north, j, 1 - j), jnp.where(south, 1 - j, j)
        row_put(gma, 1 - j, 0, lr_slot[0, pl.ds(pl.multiple_of(32 * at_n, 32), 32)].astype(F32))
        row_put(gma, 10 + j, 0, lr_slot[1, pl.ds(pl.multiple_of(32 * at_s, 32), 32)].astype(F32))
        row_put(gcax, 1 - j, 8, lr_slot[0, pl.ds(pl.multiple_of(64 + 16 * at_n, 16), 16)].astype(F32))
        row_put(gcax, 6 + j, 8, lr_slot[1, pl.ds(pl.multiple_of(64 + 16 * at_s, 16), 16)].astype(F32))
    for side in range(2):
        row_put(cte, side, 2, get(ts, side * 48, 16))
        row_put(cte, side, 1, corner(side, 8))
        row_put(cte, side, 18, corner(2 + side, 8))
        for c in range(2):
            col = 8 + (16 if side else -2) + c
            for q in range(4):
                row_put(gcax, q + 2, col, pick(side, 32 + 4 * c + q))
            for j in range(2):
                row_put(gcax, 1 - j, col, corner(side, 4 + 2 * c + jnp.where(north, j, 1 - j)))
                row_put(gcax, 6 + j, col, corner(2 + side, 4 + 2 * c + jnp.where(south, 1 - j, j)))
    edge_columns(gmae, 16, 0)

    wc_in.wait()
    for k in range(2):
        recv(2, k, pml.at[pl.ds(0, 3)], pr_slot.at[k])
    for k in range(2):
        recv(2, 2 + k, pc_buf.at[0], pc_slot.at[k])
        put(ts, k * 48, pc_slot[k].astype(F32))
    for k in range(4):
        recv(2, 4 + k, pk_buf.at[0], pk_slot.at[k])
        put(tk, k * 16, pk_slot[k].astype(F32))
    for j in range(3):
        row_put(sc, 2 - j, 16, pr_slot[0, jnp.where(north, j, 2 - j)].astype(F32))
        row_put(sc, 7 + j, 16, pr_slot[1, jnp.where(south, 2 - j, j)].astype(F32))
    for side in range(2):
        for c in range(3):
            col = 16 + (16 if side else -3) + c
            for q in range(4):
                row_put(sc, q + 3, col, pick(side, 4 * c + q))
            for j in range(3):
                row_put(sc, 2 - j, col, corner(side, 4 * c + jnp.where(north, j, 3 - j)))
                row_put(sc, 7 + j, col, corner(2 + side, 4 * c + jnp.where(south, 3 - j, j)))

    @pl.loop(0, 10, unroll=True)
    def _(r):
        for b in range(3):
            cb[b, r] = row_get(sc, r, 7 + b, 32).astype(BF16)

    def coarse(a, b):
        rows = [1 + sgn_n * (a - 1), 2 + sgn_n * (a - 1)]
        tail = [7 + sgn_s * (a - 1), 8 + sgn_s * (a - 1)]
        parts = [cb[b, r] for r in rows] + [cb[b, 2 + a : 6 + a].reshape(128, C)]
        return jnp.concatenate(parts + [cb[b, r] for r in tail], axis=0)

    res = conv_dot(coarse, wc)
    for i in range(8):
        a, s = gelu_pair(res[i * 32 : (i + 1) * 32])
        if 2 <= i < 6:
            ac[i - 2] = rounded(a[8:24])
        row_put(gs, i, 8, row_get(gcax, i, 0, 32) * s)

    @pl.loop(0, 8, unroll=True)
    def _(r):
        for d in range(3):
            gb[d, r] = row_get(gs, r, 7 + d, 32).astype(BF16)

    for d in range(3):
        for k, (x, y) in enumerate(((0, 2), (1, 3), (4, 6), (5, 7))):
            gb[d, 8 + k] = (gb[d, x].astype(F32) + gb[d, y].astype(F32)).astype(BF16)
        gb[d, 12] = jnp.zeros((32, C), BF16)

    def coarse_t(a, b):
        d = 2 - b
        if a == 1:
            return gb[d, 1:7].reshape(192, C)
        if a == 0:
            rows = [jnp.where(north, 8, 2), jnp.where(north, 9, 3), 4, 5, jnp.where(south, 12, 6), jnp.where(south, 12, 7)]
        else:
            rows = [jnp.where(north, 12, 0), jnp.where(north, 12, 1), 2, 3, jnp.where(south, 10, 4), jnp.where(south, 11, 5)]
        return jnp.concatenate([gb[d, r] for r in rows], axis=0)

    res = conv_dot_t(coarse_t, wc)
    for i in range(6):
        row_put(bm, i, 0, 0.25 * res[i * 32 : (i + 1) * 32])

    for k in range(2):
        recv(3, k, slb.at[pl.ds(0, 2)], sr_slot.at[k])
    for j in range(2):
        row_put(slm, 1 - j, 0, sr_slot[0, jnp.where(north, j, 1 - j)].astype(F32))
        row_put(slm, 10 + j, 0, sr_slot[1, jnp.where(south, 1 - j, j)].astype(F32))
    edge_columns(sle, 16, 12)

    @pl.loop(0, 12, unroll=True)
    def _(k):
        below = row_get(bm, k // 2, 8, 16)
        for p, shifted in ((0, ms0), (1, ms1)):
            g = (row_get(gma, k, p * 16, 16) + below) * row_get(slm, k, p * 16, 16)
            mg[k, 1 + p] = g.astype(BF16)
            row_put(shifted, k, 8, g)

    for side in range(2):
        below = col_get(bm, 24 if side else 7, 0, 8)
        put(tile, 0, below, 2)
        put(tile, 1, below, 2)
        below = get(tile, 0, 16)
        for c in range(2):
            g = (row_get(gmae, side * 2 + c, 0, 16) + below) * row_get(sle, side * 2 + c, 0, 16)
            row_put(mc, side * 3 + (c + 1 if side else c), 0, g)
            if side == 0 and c == 1:
                col_put(ms1, 7, 0, g)
            if side == 1 and c == 0:
                col_put(ms0, 24, 0, g)
    row_put(mc, 2, 0, col_get(ms0, 8, 0, 16))
    row_put(mc, 3, 0, col_get(ms1, 23, 0, 16))

    @pl.loop(0, 12, unroll=True)
    def _(k):
        mg[k, 0] = row_get(ms1, k, 7, 16).astype(BF16)
        mg[k, 3] = row_get(ms0, k, 9, 16).astype(BF16)

    for k, (x, y) in enumerate(((0, 2), (1, 3), (8, 10), (9, 11))):
        mg[12 + k] = (mg[x].astype(F32) + mg[y].astype(F32)).astype(BF16)
    mg[16] = jnp.zeros((4, 16, C), BF16)

    half_rows = lax.broadcasted_iota(jnp.int32, (16, 1), 0)
    at_north = north & (half_rows < 2)
    at_south = south & ((half_rows == 8) | (half_rows == 9))
    for i in range(6):
        low, mid, high = (rounded(row_get(mc, i, e, 16)) for e in range(3))
        both = low + high
        ml[0, i] = jnp.where(at_north, both, jnp.where(at_south, 0.0, high)).astype(BF16)
        ml[1, i] = mid.astype(BF16)
        ml[2, i] = jnp.where(at_south, both, jnp.where(at_north, 0.0, low)).astype(BF16)

    def mid_t(a, b):
        ph = slice(2 - b, 4 - b)
        if a == 1:
            parts = [mg[1:11, ph].reshape(320, C)]
        else:
            if a == 0:
                top = [jnp.where(north, 12, 2), jnp.where(north, 13, 3)]
                body, tail = 4, [jnp.where(south, 16, 10), jnp.where(south, 16, 11)]
            else:
                top = [jnp.where(north, 16, 0), jnp.where(north, 16, 1)]
                body, tail = 2, [jnp.where(south, 14, 8), jnp.where(south, 15, 9)]
            parts = [mg[r, ph].reshape(32, C) for r in top]
            parts += [mg[body : body + 6, ph].reshape(192, C)]
            parts += [mg[r, ph].reshape(32, C) for r in tail]
        return jnp.concatenate(parts + [ml[a, 2 - b], ml[a, 5 - b]], axis=0)

    res = 0.25 * conv_dot_t(mid_t, wm)
    bfm[...] = res[:320].reshape(10, 32, C)
    for side in range(2):
        row_put(bfe, side, 0, res[320 + 16 * side : 336 + 16 * side])

    for k in range(2):
        recv(4, k, ctp.at[1], ct_slot.at[k])
        ctp[17 * k] = ct_slot[k]

    @pl.when(pole)
    def _():
        recv(6, 0, sl_buf, sl_slot)
        row_put(slp, beyond_row, 0, sl_slot[...].astype(F32))

    @pl.loop(0, 18, unroll=6)
    def _(k):
        for p in range(4):
            g = (
                ctp[k, pl.ds(p * 16, 16)].astype(F32) + bfm[(k + 1) // 2, pl.ds((p // 2) * 16, 16)]
            ) * row_get(slp, k + 1, p * 16, 16)
            g_ext[k, 1 + p] = g.astype(BF16)
            if p == 0:
                row_put(fs0, k, 8, g)
            if p == 3:
                row_put(fs3, k, 8, g)

    for side, (shifted, at) in enumerate(((fs3, 7), (fs0, 24))):
        below = row_get(bfe, side, 0, 16)
        put(tile, 0, below, 2)
        put(tile, 1, below, 2)
        g = (row_get(cte, side, 0, 32) + get(tile, 0, 32)) * row_get(slp_e, 1 + 3 * side, 0, 32)
        row_put(ge, side, 0, g)
        col_put(shifted, at, 0, row_get(ge, side, 1, 24))

    @pl.loop(0, 18, unroll=True)
    def _(k):
        g_ext[k, 0] = row_get(fs3, k, 7, 16).astype(BF16)
        g_ext[k, 5] = row_get(fs0, k, 9, 16).astype(BF16)

    for k, (x, y) in enumerate(((0, 2), (15, 17))):
        g_ext[18 + k] = (g_ext[x].astype(F32) + g_ext[y].astype(F32)).astype(BF16)
    g_ext[20] = jnp.zeros((6, 16, C), BF16)

    for copy in sends:
        copy.wait_send()

    @pl.when(pole)
    def _():
        far_rows(1).wait_send()
        for side in range(2):
            corner_copy(side, True, True).wait_send()
        remote(5, 0, p2_buf, p2_slot, 0, far).wait_send()
        remote(6, 0, sl_buf, sl_slot, 0, far).wait_send()

    @pl.when(jnp.logical_not(pole))
    def _():
        far_rows(3).wait_send()
        for side in range(2):
            corner_copy(side, True, False).wait_send()


def last_kernel(nlat, ns, ac, g_ext, wf, out_hbm, grad_hbm, out_v, grad_v, sx, acx, sem):
    lat = lax.axis_index("lat")
    north = lat == 0
    south = lat == nlat - 1
    sx, ns, acx = Rows(sx, 64), Rows(ns, 64), Rows(acx, 64)
    copies = []
    for h in range(2):

        def fine_t(a, b):
            ph = slice(2 - b, 6 - b)
            if a == 1:
                return g_ext[8 * h + 1 : 8 * h + 9, ph].reshape(512, C)
            first = 8 * h + 2 - a
            if h == 0:
                row = jnp.where(north, 20 if a else 18, first)
                parts = [g_ext[row, ph].reshape(64, C), g_ext[first + 1 : first + 8, ph].reshape(448, C)]
            else:
                row = jnp.where(south, 19 if a else 20, first + 7)
                parts = [g_ext[first : first + 7, ph].reshape(448, C), g_ext[row, ph].reshape(64, C)]
            return jnp.concatenate(parts, axis=0)

        res = conv_dot_t(fine_t, wf)
        if h == 0:
            for q in range(4):
                for p in range(4):
                    row_put(acx, q, p, ac[q], 4)
            for r in range(16):
                out_v[r] = (row_get(ns, r, 0, 64) + row_get(acx, r // 4, 0, 64)).astype(BF16)
            copies.append(pltpu.make_async_copy(out_v, out_hbm, sem.at[2]))
            copies[-1].start()
        for r in range(8):
            for p in range(4):
                row_put(sx, 8 * h + r, p, res[r * 64 + p * 16 : r * 64 + p * 16 + 16], 4)
            grad_v[8 * h + r] = row_get(sx, 8 * h + r, 0, 64).astype(BF16)
        half = pl.ds(8 * h, 8)
        copies.append(pltpu.make_async_copy(grad_v.at[half], grad_hbm.at[half], sem.at[h]))
        copies[-1].start()
    for copy in copies:
        copy.wait()


def body(nlat, nlon, hidden_in, cotangent, weight_fine, weight_mid, weight_coarse):
    hbm = pl.BlockSpec(memory_space=pltpu.HBM)
    field = (16, 64, C)
    weight = (3, 3, C, C)

    def v(*shape, dtype=BF16):
        return pltpu.VMEM(shape, dtype)

    def f(*shape):
        return pltpu.VMEM(shape, F32)

    scratch = dict(
        hid=v(*field), cot=v(*field), wm=v(*weight), wc=v(*weight),
        s_ext=f(3, 36 * 80, 128), e_ext=v(22, 6, 16, C), l_edge=v(3, 10, 32, C), l_late=v(3, 10, 16, C), pre=f(24, 64, C), pre_e=f(6, 32, C),
        act=f(3, 25 * 64, 128), slp=f(3, 25 * 64, 128), act_e=f(3, 6 * 40, 128), slp_e=f(3, 6 * 32, 128),
        sx=f(3, 17 * 64, 128), ctp=v(18, 64, C), cte=f(3, 2 * 32, 128), gma=f(3, 17 * 32, 128), gmae=f(3, 5 * 16, 128),
        gcax=f(3, 16 * 32, 128),
        pf=v(10, 4, 16, C), sm0=f(3, 17 * 32, 128), sm1=f(3, 17 * 32, 128), pre_m=f(8, 32, C), am=f(8, 32, C),
        slm=f(3, 17 * 32, 128), sle=f(3, 5 * 16, 128), slb=v(8, 32, C), pml=v(4, 16, C), sc=f(3, 12 * 48, 128),
        cb=v(3, 10, 32, C), gs=f(3, 8 * 48, 128), gb=v(3, 13, 32, C), bm=f(3, 9 * 32, 128),
        mg=v(17, 4, 16, C), ms0=f(3, 17 * 32, 128), ms1=f(3, 17 * 32, 128), mc=f(3, 6 * 24, 128), ml=v(3, 6, 16, C),
        bfm=f(10, 32, C), bfe=f(3, 2 * 16, 128), fs0=f(3, 25 * 32, 128), fs3=f(3, 25 * 32, 128),
        ge=f(3, 2 * 32, 128), tile=f(3, 48, 128), ts=f(3, 96, 128), tk=f(3, 80, 128),
        c_buf=v(2, 48, C), k_buf=v(4, 16, C), r_slot=v(2, 3, 64, C), c_slot=v(2, 48, C), k_slot=v(4, 16, C),
        kp_buf=v(2, 16, 128), kp_slot=v(4, 16, 128),
        lr_buf=v(2, 96, C), lc_buf=v(2, 48, C), lk_buf=v(4, 16, C),
        lr_slot=v(2, 96, C), lc_slot=v(2, 48, C), lk_slot=v(4, 16, C),
        pc_buf=v(2, 32, C), pk_buf=v(4, 16, C),
        p2_buf=v(48, C), p2_slot=v(48, C), sl_buf=v(64, C), sl_slot=v(64, C),
        pr_slot=v(2, 3, 16, C), sr_slot=v(2, 2, 32, C), ct_slot=v(2, 64, C), pc_slot=v(2, 32, C), pk_slot=v(4, 16, C),
        lsem=pltpu.SemaphoreType.DMA((8,)), ssem=pltpu.SemaphoreType.DMA((7, 8)), rsem=pltpu.SemaphoreType.DMA((7, 8)),
    )
    vmem = pl.BlockSpec(memory_space=pltpu.VMEM)
    results = pl.pallas_call(
        functools.partial(kernel, nlat, nlon),
        out_shape=(f(3, 17 * 64, 128), f(4, 16, C), v(21, 6, 16, C), v(*weight)),
        in_specs=[hbm] * 5,
        out_specs=(vmem,) * 4,
        scratch_shapes=list(scratch.values()),
        compiler_params=pltpu.CompilerParams(
            collective_id=0, has_side_effects=True, vmem_limit_bytes=52 * 2**20
        ),
    )(hidden_in, cotangent, weight_fine, weight_mid, weight_coarse)
    shape = jax.ShapeDtypeStruct(field, BF16)
    return pl.pallas_call(
        functools.partial(last_kernel, nlat),
        out_shape=(shape, shape),
        in_specs=[vmem] * 4,
        out_specs=(hbm, hbm),
        scratch_shapes=[v(*field), v(*field), f(3, 17 * 64, 128), f(3, 5 * 64, 128), pltpu.SemaphoreType.DMA((3,))],
        compiler_params=pltpu.CompilerParams(vmem_limit_bytes=36 * 2**20),
    )(*results)


def solution(mesh):
    field = P("lat", "lon", None)
    return jax.shard_map(
        functools.partial(body, mesh.shape["lat"], mesh.shape["lon"]),
        mesh=mesh,
        in_specs=(field, field, P(), P(), P()),
        out_specs=(field, field),
        check_vma=False,
    )
```
